32 devices in a mesh: seq: 2 (over x), batch: 4 (over y, core), tp: 4 (over z).
Axes of the slice: x: 2, y: 2, z: 4, core: 2. Of those that a mesh axis runs over, the one named last changes fastest.
Arguments:
- tokens: bfloat16 [16, 1024, 768], P('batch', ('seq', 'tp')), may hold values from -6 to 6
- first_values: bfloat16 [16, 1024, 384], P('batch', ('seq', 'tp')), may hold values from -6 to 6
- segment_ids: int32 [16, 1024], P('batch'), may hold values from 0 to 7, as said below
- cotangent: bfloat16 [16, 1024, 768], P('batch', ('seq', 'tp')), may hold values from -6 to 6
- norm1_gain: float32 [768], replicated, may hold values from 0.25 to 1.75
- norm1_bias: float32 [768], replicated, may hold values from -1.75 to 1.75
- w_query: bfloat16 [768, 768], P(None, 'tp'), may hold values from -0.21875 to 0.21875
- b_query: float32 [768], P('tp'), may hold values from -3 to 3
- w_key: bfloat16 [768, 768], P(None, 'tp'), may hold values from -0.21875 to 0.21875
- w_value: bfloat16 [768, 384], replicated, may hold values from -0.21875 to 0.21875
- b_value: float32 [384], replicated, may hold values from -3 to 3
- w_out: bfloat16 [768, 768], P('tp'), may hold values from -0.875 to 0.875
- b_out: float32 [768], replicated, may hold values from -1.75 to 1.75
- norm2_gain: float32 [768], replicated, may hold values from 0.25 to 1.75
- norm2_bias: float32 [768], replicated, may hold values from -1.75 to 1.75
- w_up: bfloat16 [768, 3072], P(None, 'tp'), may hold values from -0.21875 to 0.21875
- b_up: float32 [3072], P('tp'), may hold values from -3 to 3
- w_down: bfloat16 [3072, 768], P('tp'), may hold values from -0.109375 to 0.109375
- b_down: float32 [768], replicated, may hold values from -1.75 to 1.75
Outputs:
- output: bfloat16 [16, 1024, 768], P('batch', ('seq', 'tp'))
- grad_tokens: float32 [16, 1024, 768], P('batch', ('seq', 'tp'))
- grad_first_values: bfloat16 [16, 1024, 384], P('batch', ('seq', 'tp'))
- grad_norm1_gain: float32 [768], replicated
- grad_norm1_bias: float32 [768], replicated
- grad_w_query: float32 [768, 768], P(None, 'tp')
- grad_b_query: float32 [768], P('tp')
- grad_w_key: float32 [768, 768], P(None, 'tp')
- grad_w_value: float32 [768, 384], replicated
- grad_b_value: float32 [384], replicated
- grad_w_out: float32 [768, 768], P('tp')
- grad_b_out: float32 [768], replicated
- grad_norm2_gain: float32 [768], replicated
- grad_norm2_bias: float32 [768], replicated
- grad_w_up: float32 [768, 3072], P(None, 'tp')
- grad_b_up: float32 [3072], P('tp')
- grad_w_down: float32 [3072, 768], P('tp')
- grad_b_down: float32 [768], replicated
The draws below stay inside these ranges and needn't reach their ends.
Inputs may be any that keep to these rules, and one draw needn't show every extreme that they name: `segment_ids`: along each row the ids never fall. In each aligned block of 4 rows (the rows of one batch index) one row, drawn from the seed, is a single document of all 1024 tokens; the other rows are cut into documents at up to 7 positions, and end with id 7.
All inputs are finite; a program needn't handle non-finite values.
Results may differ from the reference program's by a relative error of at most 0.019.
Values may be sent and summed in bfloat16 or wider, within the bound.
A program may use at most 192 MiB of HBM per device.

```python
import math
import jax
import jax.numpy as jnp
from jax import lax

D = 768
HEADS = 12
HEAD_DIM = 64
FF = 3072
SEQ_LEN = 1024
ROW_DEV = 4
CUTS = 7
ROWS = 16
VALF = 384


def draw_segment_ids(key, part):
    key = jax.random.fold_in(key, 17)
    cut_key, pick_key = jax.random.split(key)
    cuts = jax.random.randint(cut_key, (ROWS, CUTS), 1, SEQ_LEN)
    places = jnp.arange(SEQ_LEN, dtype=jnp.int32)
    counts = jnp.sum((cuts[:, None, :] <= places[None, :, None]).astype(jnp.int32), axis=2)
    chosen = jax.random.randint(pick_key, (ROWS // ROW_DEV,), 0, ROW_DEV)
    row_ids = jnp.arange(ROWS, dtype=jnp.int32)
    whole = row_ids % ROW_DEV == chosen[row_ids // ROW_DEV]
    return jnp.where(whole[:, None], 0, counts).astype(jnp.int32)


def level_of(own_key, extent, cuts, low, top_value):
    gain = 1.0
    for position, shards_of in cuts:
        draws = jax.random.uniform(jax.random.fold_in(jax.random.fold_in(own_key, 6), position), (shards_of,), jnp.float32, low / len(cuts), top_value / len(cuts))
        gain = gain * jnp.repeat(jnp.exp(draws), extent[position] // shards_of).reshape((-1,) + (1,) * (len(extent) - 1 - position))
    return gain


def noise(rng, shape, scale, most, cuts=(), held_as=jnp.bfloat16):
    entries = scale * jax.random.normal(rng, shape, jnp.float32)
    if cuts:
        entries = entries * level_of(rng, shape, cuts, -0.22, 0.18)
    return jnp.clip(entries, -most, most).astype(held_as)


def setup_inputs(seed: int = 0) -> dict:
    seeds = jax.random.split(jax.random.key(seed), 20)
    return {
        "tokens": noise(seeds[0], (ROWS, SEQ_LEN, D), 1.0, 6.0, ((0, 4), (1, 8))),
        "first_values": noise(seeds[1], (ROWS, SEQ_LEN, VALF), 1.0, 6.0, ((0, 4), (1, 8))),
        "segment_ids": draw_segment_ids(jax.random.fold_in(seeds[19], 71), 0),
        "cotangent": noise(seeds[3], (ROWS, SEQ_LEN, D), 1.0, 6.0, ((0, 4), (1, 8))),
        "norm1_gain": jnp.clip(1.0 + 0.15 * jax.random.normal(seeds[4], (D,), jnp.float32), 0.25, 1.75),
        "norm1_bias": noise(seeds[5], (D,), 0.3, 1.75, (), jnp.float32),
        "w_query": noise(seeds[6], (D, HEADS * HEAD_DIM), D ** -0.5, 0.21875, ((1, 4),)),
        "b_query": noise(seeds[7], (HEADS * HEAD_DIM,), 0.5, 3.0, ((0, 4),), jnp.float32),
        "w_key": noise(seeds[8], (D, HEADS * HEAD_DIM), D ** -0.5, 0.21875, ((1, 4),)),
        "w_value": noise(seeds[9], (D, VALF), D ** -0.5, 0.21875),
        "b_value": noise(seeds[10], (VALF,), 0.5, 3.0, (), jnp.float32),
        "w_out": noise(seeds[11], (HEADS * HEAD_DIM, D), (D // 16) ** -0.5, 0.875, ((0, 4),)),
        "b_out": noise(seeds[12], (D,), 0.3, 1.75, (), jnp.float32),
        "norm2_gain": jnp.clip(1.0 + 0.15 * jax.random.normal(seeds[13], (D,), jnp.float32), 0.25, 1.75),
        "norm2_bias": noise(seeds[14], (D,), 0.3, 1.75, (), jnp.float32),
        "w_up": noise(seeds[15], (D, FF), D ** -0.5, 0.21875, ((1, 4),)),
        "b_up": noise(seeds[16], (FF,), 0.5, 3.0, ((0, 4),), jnp.float32),
        "w_down": noise(seeds[17], (FF, D), FF ** -0.5, 0.109375, ((0, 4),)),
        "b_down": noise(seeds[18], (D,), 0.3, 1.75, (), jnp.float32),
    }


eps = 1e-05
highest = lax.Precision.HIGHEST

@jax.custom_vjp
def low(v):
    return lax.optimization_barrier(v.astype(jnp.bfloat16)).astype(jnp.float32)

@jax.custom_vjp
def low_back(v):
    return v

def low_keep(v):
    return (low(v), None)

def low_pass(kept, grad):
    return (grad,)

def back_keep(v):
    return (v, None)

def back_low(kept, grad):
    return (low(grad),)
low.defvjp(low_keep, low_pass)
low_back.defvjp(back_keep, back_low)

def both_ways(value):
    return low(low_back(value))

def layer_norm(values, norm_gain, norm_bias):
    average = lax.optimization_barrier(jnp.mean(values, axis=-1, keepdims=True))
    centered = values - average
    inverse = lax.rsqrt(lax.optimization_barrier(jnp.mean(centered * centered, axis=-1, keepdims=True)) + eps)
    return centered * inverse * norm_gain + norm_bias

def project(values, weight):
    return jnp.einsum('gtd,de->gte', values, weight, precision=highest)

def attention(query, keys, values, segments):
    length = query.shape[1]
    width = min(512, length)
    positions = jnp.arange(length, dtype=jnp.int32)
    factor = HEAD_DIM ** (-0.5)

    @jax.checkpoint
    def block(index):
        first = (index * width).astype(jnp.int32)
        query_part = lax.dynamic_slice_in_dim(query, first, width, 1)
        query_seg = lax.dynamic_slice_in_dim(segments, first, width, 1)
        query_pos = first + jnp.arange(width, dtype=jnp.int32)
        scores = low_back(jnp.einsum('gqhc,gkhc->ghqk', query_part, keys, precision=highest) * factor)
        allowed = (query_seg[:, :, None] == segments[:, None, :]) & (positions[None, None, :] <= query_pos[None, :, None])
        scores = jnp.where(allowed[:, None], scores, -1e+30)
        top = lax.optimization_barrier(jnp.max(scores, axis=-1, keepdims=True))
        weights = jnp.exp(scores - top)
        probs = weights / lax.optimization_barrier(jnp.sum(weights, axis=-1, keepdims=True))
        return jnp.einsum('ghqk,gkhc->gqhc', low(probs), values, precision=highest)
    blocks = lax.map(block, jnp.arange(length // width, dtype=jnp.int32))
    return jnp.moveaxis(blocks, 0, 1).reshape(query.shape)

def forward(params, tokens, first_values, segments):
    norm1_gain, norm1_bias, w_query, b_query, w_key, w_value, b_value, w_out, b_out, norm2_gain, norm2_bias, w_up, b_up, w_down, b_down = params
    groups = tokens.shape[0]
    length = tokens.shape[1]
    half_heads = HEADS // 2
    normed = low(layer_norm(tokens, norm1_gain, norm1_bias))
    query = both_ways(project(normed, w_query) + b_query)
    keys = both_ways(project(normed, w_key))
    fresh = project(normed, w_value) + b_value
    values = both_ways(jnp.concatenate([fresh.reshape(groups, length, half_heads, HEAD_DIM), first_values.reshape(groups, length, half_heads, HEAD_DIM)], axis=2))
    attended = attention(query.reshape(groups, length, HEADS, HEAD_DIM), keys.reshape(groups, length, HEADS, HEAD_DIM), values, segments)
    attended = both_ways(attended.reshape(groups, length, HEADS * HEAD_DIM))
    middle = tokens + low_back(project(attended, w_out) + b_out)
    normed_two = low(layer_norm(middle, norm2_gain, norm2_bias))
    hidden = low_back(project(normed_two, w_up) + b_up)
    activated = low(jax.nn.gelu(hidden, approximate=True))
    return middle + low_back(project(activated, w_down) + b_down)

def reference(tokens, first_values, segment_ids, cotangent, norm1_gain, norm1_bias, w_query, b_query, w_key, w_value, b_value, w_out, b_out, norm2_gain, norm2_bias, w_up, b_up, w_down, b_down):
    params = tuple((item.astype(jnp.float32) for item in (norm1_gain, norm1_bias, w_query, b_query, w_key, w_value, b_value, w_out, b_out, norm2_gain, norm2_bias, w_up, b_up, w_down, b_down)))
    rows = tokens.shape[0]
    group = math.gcd(rows, 4)
    count = rows // group

    def shaped(array):
        return array.reshape((count, group) + array.shape[1:])
    zeros = tuple((jnp.zeros_like(item) for item in params))

    def one_group(totals, inputs):
        token_rows, first_rows, segment_rows, cotangent_rows = inputs

        def local(param_list, token_part, first_part):
            return forward(param_list, token_part, first_part, segment_rows)
        result, pullback = jax.vjp(local, params, token_rows.astype(jnp.float32), first_rows.astype(jnp.float32))
        grads, grad_token_rows, grad_first_rows = pullback(cotangent_rows.astype(jnp.float32))
        totals = tuple((left + right for left, right in zip(totals, grads)))
        return (totals, (result.astype(jnp.bfloat16), grad_token_rows, grad_first_rows.astype(jnp.bfloat16)))
    totals, stacked = lax.scan(one_group, zeros, (shaped(tokens), shaped(first_values), shaped(segment_ids), shaped(cotangent)))
    output = stacked[0].reshape(tokens.shape)
    grad_tokens = stacked[1].reshape(tokens.shape)
    grad_first_values = stacked[2].reshape(first_values.shape)
    return (output, grad_tokens, grad_first_values, totals[0], totals[1], totals[2], totals[3], totals[4], totals[5], totals[6], totals[7], totals[8], totals[9], totals[10], totals[11], totals[12], totals[13], totals[14])
```

```python
import math

import jax
import jax.numpy as jnp
from jax import lax
from jax.experimental import pallas as pl
from jax.experimental.pallas import tpu as pltpu
from jax.sharding import PartitionSpec as P

HEADS = 12
HEAD_DIM = 64


eps = 1e-05
block_cap = 256
far_below = -1e30


def from_behind(block, axis, distance):
    devices = range(lax.axis_size(axis))
    route = [((i - distance) % len(devices), i) for i in devices]
    return lax.ppermute(block, axis, route)


def layer_norm(values, norm_gain, norm_bias):
    average = jnp.mean(values, axis=-1, keepdims=True)
    centered = values - average
    inverse = lax.rsqrt(jnp.mean(centered * centered, axis=-1, keepdims=True) + eps)
    unit = centered * inverse
    return (unit * norm_gain + norm_bias, unit, inverse)


def norm_back(grad_result, unit, inverse, norm_gain):
    scaled = grad_result * norm_gain
    return inverse * (
        scaled
        - jnp.mean(scaled, axis=-1, keepdims=True)
        - unit * jnp.mean(scaled * unit, axis=-1, keepdims=True)
    )


def project(values, weight):
    return jnp.einsum("rtd,de->rte", values, weight, preferred_element_type=jnp.float32)


def project_back(grads, weight):
    return jnp.einsum("rte,de->rtd", grads, weight, preferred_element_type=jnp.float32)


def weight_grad(values, grads):
    return jnp.einsum("rtd,rte->de", values, grads, preferred_element_type=jnp.float32)


def column_sum(values):
    return jnp.sum(values, axis=(0, 1), dtype=jnp.float32)


def gelu_tanh(values):
    return jax.nn.gelu(values, approximate=True)


def over_key_blocks(arrays, key_first, state, step, limit):
    count = arrays[0].shape[1]
    width = math.gcd(count, block_cap)

    def one(index, carry):
        offset = index * width
        parts = tuple((lax.dynamic_slice_in_dim(item, offset, width, 1) for item in arrays))
        first_key = key_first + offset

        def taken(inner):
            return step(inner, parts, first_key, offset)

        def skipped(inner):
            return inner

        return lax.cond(first_key <= limit, taken, skipped, carry)

    return lax.fori_loop(0, count // width, one, state)


def on_device(
    tokens,
    first_values,
    segment_ids,
    cotangent,
    norm1_gain,
    norm1_bias,
    w_query,
    b_query,
    w_key,
    w_value,
    b_value,
    w_out,
    b_out,
    norm2_gain,
    norm2_bias,
    w_up,
    b_up,
    w_down,
    b_down,
):
    rows = tokens.shape[0]
    model_width = tokens.shape[2]
    tp_count = lax.axis_size("tp")
    seq_count = lax.axis_size("seq")
    local_len = tokens.shape[1] * tp_count
    heads = w_query.shape[1] // HEAD_DIM
    width_tp = heads * HEAD_DIM
    valf_all = w_value.shape[1]
    factor = HEAD_DIM ** (-0.5)
    seq_index = lax.axis_index("seq")
    head_first = lax.axis_index("tp") * heads
    is_fresh = head_first < HEADS // 2
    fresh_col = jnp.minimum(head_first * HEAD_DIM, valf_all - width_tp)
    reuse_col = jnp.maximum(head_first * HEAD_DIM - valf_all, 0)
    own_first = seq_index * local_len
    own_last = own_first + local_len - 1
    own_pos = own_first + jnp.arange(local_len, dtype=jnp.int32)
    own_seg = lax.dynamic_slice_in_dim(segment_ids, own_first, local_len, 1)

    def masked_scores(query4, key_part, query_pos, query_seg, key_first):
        width = key_part.shape[1]
        scores = (
            jnp.einsum("rqhc,rkhc->rhqk", query4, key_part, preferred_element_type=jnp.float32)
            * factor
        )
        key_seg = lax.dynamic_slice_in_dim(segment_ids, key_first, width, 1)
        key_pos = key_first + jnp.arange(width, dtype=jnp.int32)
        allowed = (query_seg[:, :, None] == key_seg[:, None, :]) & (
            key_pos[None, None, :] <= query_pos[None, :, None]
        )
        return (scores, allowed[:, None])

    resid = tokens.astype(jnp.float32)
    normed_one, unit_one, inverse_one = layer_norm(resid, norm1_gain, norm1_bias)
    rows_one, grad_rows, first_rows = (
        lax.all_gather(normed_one.astype(jnp.bfloat16), "tp", axis=1, tiled=True),
        lax.all_gather(cotangent, "tp", axis=1, tiled=True),
        lax.all_gather(first_values, "tp", axis=1, tiled=True),
    )
    query4 = (
        (project(rows_one, w_query) + b_query)
        .astype(jnp.bfloat16)
        .reshape(rows, local_len, heads, HEAD_DIM)
    )
    keys4 = project(rows_one, w_key).astype(jnp.bfloat16).reshape(rows, local_len, heads, HEAD_DIM)
    w_part = lax.dynamic_slice_in_dim(w_value, fresh_col, width_tp, 1)
    b_part = lax.dynamic_slice_in_dim(b_value, fresh_col, width_tp, 0)

    def fresh_side(normed_rows):
        return (project(normed_rows, w_part) + b_part).astype(jnp.bfloat16)

    def reuse_side(normed_rows):
        return lax.dynamic_slice_in_dim(first_rows, reuse_col, width_tp, 2)

    vals4 = lax.cond(is_fresh, fresh_side, reuse_side, rows_one).reshape(
        rows, local_len, heads, HEAD_DIM
    )

    def stats_step(carry, parts, key_first, offset):
        top, total = carry
        scores, allowed = masked_scores(query4, parts[0], own_pos, own_seg, key_first)
        masked = jnp.where(allowed, scores, far_below)
        new_top = jnp.maximum(top, jnp.max(masked, axis=3))
        weights = jnp.where(allowed, jnp.exp(masked - new_top[..., None]), 0.0)
        return (new_top, total * jnp.exp(top - new_top) + jnp.sum(weights, axis=3))

    start_top = jnp.full((rows, heads, local_len), far_below, jnp.float32)
    start_total = jnp.zeros((rows, heads, local_len), jnp.float32)
    top, total = over_key_blocks(
        (lax.all_gather(keys4, "seq", axis=1, tiled=True),),
        jnp.int32(0),
        (start_top, start_total),
        stats_step,
        own_last,
    )
    lse = top + jnp.log(total)

    def value_step(acc, parts, key_first, offset):
        scores, allowed = masked_scores(query4, parts[0], own_pos, own_seg, key_first)
        weights = jnp.where(allowed, jnp.exp(scores - lse[..., None]), 0.0).astype(jnp.bfloat16)
        return acc + jnp.einsum(
            "rhqk,rkhc->rqhc", weights, parts[1], preferred_element_type=jnp.float32
        )

    zeros_q = jnp.zeros((rows, local_len, heads, HEAD_DIM), jnp.float32)
    attended = over_key_blocks(
        (
            lax.all_gather(keys4, "seq", axis=1, tiled=True),
            lax.all_gather(vals4, "seq", axis=1, tiled=True),
        ),
        jnp.int32(0),
        zeros_q,
        value_step,
        own_last,
    )
    attended_low = attended.astype(jnp.bfloat16).reshape(rows, local_len, width_tp)
    attn_share = lax.psum_scatter(
        project(attended_low, w_out).astype(jnp.bfloat16), "tp", scatter_dimension=1, tiled=True
    ).astype(jnp.float32)
    middle = resid + attn_share + b_out
    normed_two, unit_two, inverse_two = layer_norm(middle, norm2_gain, norm2_bias)
    rows_two = lax.all_gather(normed_two.astype(jnp.bfloat16), "tp", axis=1, tiled=True)
    hidden_pre = project(rows_two, w_up) + b_up
    activated_full, gelu_pull = jax.vjp(gelu_tanh, hidden_pre)
    activated = activated_full.astype(jnp.bfloat16)
    mlp_share = lax.psum_scatter(
        project(activated, w_down).astype(jnp.bfloat16), "tp", scatter_dimension=1, tiled=True
    ).astype(jnp.float32)
    output = (middle + mlp_share + b_down).astype(jnp.bfloat16)
    grad_b_down = column_sum(grad_rows)
    grad_w_down = weight_grad(activated, grad_rows)
    grad_hidden = gelu_pull(project_back(grad_rows, w_down))[0].astype(jnp.bfloat16)
    grad_b_up = column_sum(grad_hidden)
    grad_w_up = weight_grad(rows_two, grad_hidden)
    back_two = lax.psum_scatter(
        project_back(grad_hidden, w_up).astype(jnp.bfloat16), "tp", scatter_dimension=1, tiled=True
    ).astype(jnp.float32)
    grad_gain_two = jnp.sum(back_two * unit_two, axis=(0, 1))
    grad_bias_two = jnp.sum(back_two, axis=(0, 1))
    grad_middle = cotangent.astype(jnp.float32) + norm_back(
        back_two, unit_two, inverse_two, norm2_gain
    )
    grad_mid_rows = lax.all_gather(grad_middle.astype(jnp.bfloat16), "tp", axis=1, tiled=True)
    grad_b_out = column_sum(grad_mid_rows)
    grad_w_out = weight_grad(attended_low, grad_mid_rows)
    grad_out4 = (
        project_back(grad_mid_rows, w_out)
        .astype(jnp.bfloat16)
        .reshape(rows, local_len, heads, HEAD_DIM)
    )
    delta = jnp.einsum("rqhc,rqhc->rhq", grad_out4.astype(jnp.float32), attended)

    def pair_terms(key_side, val_side, key_first, grad_query, grad_keys, grad_vals):

        def pair_step(carry, parts, first, offset):
            acc_query, acc_keys, acc_vals = carry
            key_part, val_part = parts
            width = key_part.shape[1]
            scores, allowed = masked_scores(query4, key_part, own_pos, own_seg, first)
            probs = jnp.where(allowed, jnp.exp(scores - lse[..., None]), 0.0)
            grad_val = jnp.einsum(
                "rhqk,rqhc->rkhc",
                probs.astype(jnp.bfloat16),
                grad_out4,
                preferred_element_type=jnp.float32,
            )
            grad_prob = jnp.einsum(
                "rqhc,rkhc->rhqk", grad_out4, val_part, preferred_element_type=jnp.float32
            )
            grad_score = (probs * (grad_prob - delta[..., None])).astype(jnp.bfloat16)
            acc_query = (
                acc_query
                + jnp.einsum(
                    "rhqk,rkhc->rqhc", grad_score, key_part, preferred_element_type=jnp.float32
                )
                * factor
            )
            grad_key = (
                jnp.einsum(
                    "rhqk,rqhc->rkhc", grad_score, query4, preferred_element_type=jnp.float32
                )
                * factor
            )
            acc_keys = lax.dynamic_update_slice_in_dim(
                acc_keys, lax.dynamic_slice_in_dim(acc_keys, offset, width, 1) + grad_key, offset, 1
            )
            acc_vals = lax.dynamic_update_slice_in_dim(
                acc_vals, lax.dynamic_slice_in_dim(acc_vals, offset, width, 1) + grad_val, offset, 1
            )
            return (acc_query, acc_keys, acc_vals)

        return over_key_blocks(
            (key_side, val_side), key_first, (grad_query, grad_keys, grad_vals), pair_step, own_last
        )

    def turn_keys(turn, carry):
        moving_keys, moving_vals, moving_gk, moving_gv, grad_query = carry
        anchor = (seq_index - turn) % seq_count
        grad_query, moving_gk, moving_gv = pair_terms(
            moving_keys, moving_vals, anchor * local_len, grad_query, moving_gk, moving_gv
        )
        moving_keys, moving_vals, moving_gk, moving_gv = (
            from_behind(moving_keys, "seq", 1),
            from_behind(moving_vals, "seq", 1),
            from_behind(moving_gk.astype(jnp.bfloat16), "seq", 1).astype(moving_gk.dtype),
            from_behind(moving_gv.astype(jnp.bfloat16), "seq", 1).astype(moving_gv.dtype),
        )
        return (moving_keys, moving_vals, moving_gk, moving_gv, grad_query)

    start_state = (keys4, vals4, zeros_q, zeros_q, zeros_q)
    final_state = lax.fori_loop(0, seq_count, turn_keys, start_state)
    grad_keys4, grad_vals4, grad_query4 = (final_state[2], final_state[3], final_state[4])
    grad_query = grad_query4.astype(jnp.bfloat16).reshape(rows, local_len, width_tp)
    grad_keys = grad_keys4.astype(jnp.bfloat16).reshape(rows, local_len, width_tp)
    grad_vals = grad_vals4.astype(jnp.bfloat16).reshape(rows, local_len, width_tp)

    def fresh_back(grad_flat):
        gw_full = lax.dynamic_update_slice_in_dim(
            jnp.zeros((model_width, valf_all), jnp.float32),
            weight_grad(rows_one, grad_flat),
            fresh_col,
            1,
        )
        gb_full = lax.dynamic_update_slice_in_dim(
            jnp.zeros((valf_all,), jnp.float32), column_sum(grad_flat), fresh_col, 0
        )
        back_value = project_back(grad_flat, w_part)
        reuse_full = jnp.zeros((rows, local_len, valf_all), jnp.float32)
        return (gw_full, gb_full, back_value, reuse_full)

    def reuse_back(grad_flat):
        gw_full = jnp.zeros((model_width, valf_all), jnp.float32)
        gb_full = jnp.zeros((valf_all,), jnp.float32)
        back_value = jnp.zeros((rows, local_len, model_width), jnp.float32)
        reuse_full = lax.dynamic_update_slice_in_dim(
            jnp.zeros((rows, local_len, valf_all), jnp.float32),
            grad_flat.astype(jnp.float32),
            reuse_col,
            2,
        )
        return (gw_full, gb_full, back_value, reuse_full)

    grad_w_value, grad_b_value, back_value, reuse_full = lax.cond(
        is_fresh, fresh_back, reuse_back, grad_vals
    )
    grad_b_query = column_sum(grad_query)
    grad_w_query = weight_grad(rows_one, grad_query)
    grad_w_key = weight_grad(rows_one, grad_keys)
    back_terms = project_back(grad_query, w_query) + project_back(grad_keys, w_key) + back_value
    back_one, reuse_sum = (
        lax.psum_scatter(
            back_terms.astype(jnp.bfloat16), "tp", scatter_dimension=1, tiled=True
        ).astype(jnp.float32),
        lax.psum_scatter(
            reuse_full.astype(jnp.bfloat16), "tp", scatter_dimension=1, tiled=True
        ).astype(jnp.float32),
    )
    grad_first_values = reuse_sum.astype(jnp.bfloat16)
    grad_gain_one = jnp.sum(back_one * unit_one, axis=(0, 1))
    grad_bias_one = jnp.sum(back_one, axis=(0, 1))
    grad_tokens = grad_middle + norm_back(back_one, unit_one, inverse_one, norm1_gain)
    summed = lax.psum(
        (
            grad_w_query,
            grad_w_key,
            grad_w_out,
            grad_w_up,
            grad_w_down,
            grad_b_query,
            grad_b_out,
            grad_b_up,
            grad_b_down,
        ),
        ("seq", "batch"),
    )
    norm_sums = lax.psum(
        (grad_gain_one, grad_bias_one, grad_gain_two, grad_bias_two, grad_w_value, grad_b_value),
        ("seq", "batch", "tp"),
    )
    return (
        output,
        grad_tokens,
        grad_first_values,
        norm_sums[0],
        norm_sums[1],
        summed[0],
        summed[5],
        summed[1],
        norm_sums[4],
        norm_sums[5],
        summed[2],
        summed[6],
        norm_sums[2],
        norm_sums[3],
        summed[3],
        summed[7],
        summed[4],
        summed[8],
    )


BF = jnp.bfloat16
F4 = jnp.float32
MESH = pl.DeviceIdType.MESH
QB = 256


def dot(a, b):
    return lax.dot_general(a, b, (((1,), (0,)), ((), ())), preferred_element_type=F4)


def dot_nt(a, b):
    return lax.dot_general(a, b, (((1,), (1,)), ((), ())), preferred_element_type=F4)


def dot_tn(a, b):
    return lax.dot_general(a, b, (((0,), (0,)), ((), ())), preferred_element_type=F4)


def maybe(cond, act):
    if cond is None:
        act()
    else:
        pl.when(cond)(act)


class Wire:
    def __init__(self, copy, send_if=None, recv_if=None):
        self.copy, self.send_if, self.recv_if = copy, send_if, recv_if

    def start(self):
        maybe(self.send_if, self.copy.start)

    def arrived(self):
        maybe(self.recv_if, self.copy.wait_recv)

    def sent(self):
        maybe(self.send_if, self.copy.wait_send)


class Own:
    def __init__(self, copy, when=None):
        self.copy, self.when = copy, when

    def start(self):
        maybe(self.when, self.copy.start)

    def arrived(self):
        maybe(self.when, self.copy.wait)

    def sent(self):
        pass


class Net:
    def __init__(self, send_sems, recv_sems, own_sems):
        self.send_sems, self.recv_sems, self.own_sems = send_sems, recv_sems, own_sems
        self.n_send = self.n_recv = self.n_own = 0
        self.all = []

    def recv_slots(self, count):
        self.n_recv += count
        return self.n_recv - count

    def wire(self, src, dst, device, send_if=None, recv_if=None, slot=None):
        if slot is None:
            slot = self.recv_slots(1)
        copy = pltpu.make_async_remote_copy(
            src_ref=src,
            dst_ref=dst,
            send_sem=self.send_sems.at[self.n_send],
            recv_sem=self.recv_sems.at[slot],
            device_id=device,
            device_id_type=MESH,
        )
        self.n_send += 1
        made = Wire(copy, send_if, recv_if)
        self.all.append(made)
        return made

    def done(self, wire):
        wire.sent()
        self.all = [item for item in self.all if item is not wire]

    def own(self, src, dst, when=None):
        copy = pltpu.make_async_copy(src, dst, self.own_sems.at[self.n_own])
        self.n_own += 1
        return Own(copy, when)


def norm_stats(values):
    average = jnp.mean(values, axis=-1, keepdims=True)
    centered = values - average
    inverse = lax.rsqrt(jnp.mean(centered * centered, axis=-1, keepdims=True) + eps)
    return centered * inverse, inverse


def layer_kernel(
    tokens, first, cot_in, seg, wa_in, wup_in, wdown_in, wval_in, bvec_in, vecs,
    out, gtok, gfirst, f_up, f_down, f_wa, f_wv, f_small,
    x_own, n1, segint, segrow, segcol, bvec, wa, wval, wup, wdown,
    q, k, v, att, lse, mid, n2, cot,
    mine, xs, xr, out_s, gm, gatt, gv_s,
    gup, gdown, up_r1, up_r2, up_r3, down_r1, down_r2, down_r3,
    gwa, wa_r1, wa_r2, wa_r3, gwv, wv_r1, wv_r2, wv_r3,
    small, small_r, small_z, f_s, f_t, f_w, f_v,
    send_sems, recv_sems, own_sems,
):
    s, b, t = lax.axis_index("seq"), lax.axis_index("batch"), lax.axis_index("tp")
    y, c = lax.div(b, 2), lax.rem(b, 2)
    sn, yn, cn = 1 - s, 1 - y, 1 - c
    rows, blk, width = tokens.shape
    half = rows * blk
    length = 2 * half
    net = Net(send_sems, recv_sems, own_sems)

    def dev(ds, dy, dc, dt):
        return (ds, 2 * dy + dc, dt)

    def ring(step):
        return lax.rem(t + step + rows, rows)

    x_nbr, y_nbr, diag, mate = dev(sn, y, c, t), dev(s, yn, c, t), dev(sn, yn, c, t), dev(s, y, cn, t)
    home = lax.div(t, 2) == c
    away = lax.div(t, 2) != c
    same, other = s == c, s != c

    gate = pltpu.get_barrier_semaphore()
    peers = [(s, 2 * yn + c, t), (sn, 2 * yn + c, t)]
    for ds in range(2):
        for dc in range(2):
            for dt in range(rows):
                if ds or dc or dt:
                    peers.append((lax.rem(s + ds, 2), 2 * y + lax.rem(c + dc, 2), lax.rem(t + dt, rows)))
    for peer in peers:
        pl.semaphore_signal(gate, inc=1, device_id=peer, device_id_type=MESH)
    pl.semaphore_wait(gate, len(peers))

    def swap(src, dst):
        wires = []
        for step in range(rows):
            r = ring(step)
            if step == 0:
                wires.append((
                    net.wire(src.at[r], dst.at[t], dev(c, y, s, r), other, other),
                    net.own(src.at[r], dst.at[t], same),
                ))
            else:
                wires.append((net.wire(src.at[r], dst.at[t], dev(c, y, s, r)),))
        return wires

    def start_all(wires):
        for group in wires:
            for wire in group:
                wire.start()

    def arrived_all(wires):
        for group in wires:
            for wire in group:
                wire.arrived()

    seg_wire = net.wire(segint.at[0], segint.at[1], mate)
    bvec_wires = []
    for step in range(1, rows):
        bvec_wires.append(net.wire(bvec.at[0], bvec.at[step], dev(s, y, c, ring(-step))))
    wa_z = []
    for step in range(1, rows):
        wa_z.append(net.wire(
            wa_in.at[:, s, y], wa.at[:, lax.rem(t, 2), s, y], dev(s, y, c, ring(step)),
            home, lax.div(ring(-step), 2) == c,
        ))
    wa_own = net.own(wa_in, wa.at[:, lax.rem(t, 2)], home)
    token_wires = swap(tokens, x_own)
    wval_own = net.own(wval_in, wval, c == 0)
    lanes_c = pl.ds(pl.multiple_of(c * (wup.shape[-1]), 128), wup.shape[-1])
    up_own = net.own(wup_in.at[:, :, :, lanes_c], wup.at[0])
    down_own = net.own(wdown_in.at[c], wdown.at[0])

    bvec[0] = bvec_in[...]
    row_ids = lax.broadcasted_iota(jnp.int32, seg.shape, 0)
    seg_row = jnp.sum(jnp.where(row_ids == t, seg[...], 0), axis=0, keepdims=True)
    segint[0] = jnp.broadcast_to(seg_row, segint.shape[1:])
    for wire in wa_z:
        wire.start()
    seg_wire.start()
    for wire in bvec_wires:
        wire.start()
    start_all(token_wires)
    for own in (wa_own, wval_own, up_own, down_own):
        own.start()

    first_slot = net.recv_slots(2 * rows)
    first_wires = []
    for step in range(rows):
        r = ring(step)
        to = net.wire(
            first.at[r], v.at[s * rows + t], dev(c, y, 1, r),
            (c == 0) | (s == 0) if step == 0 else None, None, first_slot + s * rows + step,
        )
        first_wires.append(to)
    first_own = net.own(first.at[t], v.at[s * rows + t], (c == 1) & (s == 1))

    def first_arrived():
        for source in range(2):
            for step in range(rows):
                def take(source=source, step=step):
                    pltpu.make_async_remote_copy(
                        src_ref=first.at[0], dst_ref=v.at[0], send_sem=send_sems.at[0],
                        recv_sem=recv_sems.at[first_slot + source * rows + step],
                        device_id=mate, device_id_type=MESH,
                    ).wait_recv()
                if source == 1 and step == 0:
                    pl.when(s == 0)(take)
                else:
                    take()
        first_own.arrived()

    up_z, down_z = [], []
    for step in range(1, rows):
        up_z.append(net.wire(wup_in.at[s, y, :, lanes_c], wup.at[step, s, y], dev(s, y, c, ring(-step))))
        down_z.append(net.wire(wdown_in.at[c, s, y], wdown.at[step, s, y], dev(s, y, c, ring(-step))))
    rest = pl.ds(1, rows - 1)
    up_one = net.wire(wup.at[rest, s, y], wup.at[rest, s, y], x_nbr)
    up_two = net.wire(wup.at[rest, :, y], wup.at[rest, :, y], y_nbr)
    down_one = net.wire(wdown.at[rest, s, y], wdown.at[rest, s, y], y_nbr)
    down_two = net.wire(wdown.at[rest, s], wdown.at[rest, s], x_nbr)
    cot_wires = swap(cot_in, cot.at[s])
    cot_mate = net.wire(cot.at[c], cot.at[c], mate)

    wa_plane = []
    for step in range(1, rows):
        ours = lax.div(ring(-step), 2) == c
        piece = wa.at[:, lax.rem(ring(-step), 2), s, y]
        wa_plane.append([net.wire(piece, piece, to, ours, ours) for to in (x_nbr, y_nbr, diag)])
    for step in range(1, rows):
        wa_z[step - 1].arrived()
        for wire in wa_plane[step - 1]:
            wire.start()

    seg_wire.arrived()
    chosen = jnp.where(same, segint[0], segint[1]).astype(F4)
    segrow[...] = chosen
    for part in range(length // 128):
        piece = jnp.broadcast_to(chosen[0:1, part * 128:(part + 1) * 128], (128, 128))
        segcol[part * 128:(part + 1) * 128, :] = piece.T

    n1_wires = []
    for step in range(rows):
        place = ring(-step)
        for wire in token_wires[step]:
            wire.arrived()
        unit, _ = norm_stats(x_own[place].astype(F4))
        n1[c, place] = (unit * vecs[0:1, :] + vecs[1:2, :]).astype(BF)
        wire = net.wire(n1.at[c, place], n1.at[c, place], mate)
        wire.start()
        n1_wires.append(wire)
    for wire in first_wires:
        wire.start()
    first_own.start()
    for wire in up_z + down_z:
        wire.start()
    for group in wa_plane:
        for wire in group:
            wire.arrived()
    wa_own.arrived()
    wval_own.arrived()
    for wire in bvec_wires:
        wire.arrived()
    for wire in n1_wires:
        wire.arrived()

    heads_width = q.shape[1]
    factor = HEAD_DIM ** (-0.5)
    b_q = (bvec[lax.rem(2 * c + rows - t, rows), 1:2, :heads_width]
           + bvec[lax.rem(2 * c + 1 + rows - t, rows), 1:2, :heads_width])
    wq, wk, wo = (wa.at[i] for i in range(3))

    def flat(ref_value):
        return ref_value.reshape(-1, ref_value.shape[-1])

    per_half = half // QB
    per_blk = QB // blk

    def n1_rows(i):
        return flat(n1[lax.div(i, per_half), pl.ds(lax.rem(i, per_half) * per_blk, per_blk)])

    def project_in(i, carry):
        at = pl.ds(pl.multiple_of(i * QB, QB), QB)
        block = n1_rows(i)
        q[at, :] = ((dot_nt(block, flat(wq[...])) + b_q) * factor).astype(BF)
        k_block = dot_nt(block, flat(wk[...]))
        k[at, :] = k_block.astype(BF)
        return carry

    lax.fori_loop(0, length // QB, project_in, 0)

    @pl.when(c == 0)
    def _():
        def fresh(i, carry):
            got = (dot(n1_rows(i), wval[...]) + vecs[6:7, :heads_width]).astype(BF)
            v[pl.ds(i * per_blk, per_blk)] = got.reshape(per_blk, blk, heads_width)
            return carry

        lax.fori_loop(0, length // QB, fresh, 0)

    @pl.when(c == 1)
    def _():
        first_arrived()

    pairs = heads_width // 128
    n_q = length // QB
    lane = lax.broadcasted_iota(jnp.int32, (1, 128), 1)
    keeps = (lane < HEAD_DIM, lane >= HEAD_DIM)

    def attend(j, bias, lsecol):
        count = (j + 1) * QB
        at = slice(j * QB, count)
        key_pos = lax.broadcasted_iota(jnp.int32, (QB, count), 1)
        query_pos = j * QB + lax.broadcasted_iota(jnp.int32, (QB, count), 0)
        allowed = (segcol[at, 0:1] == segrow[0:1, :count]) & (key_pos <= query_pos)
        bias[:, :count] = jnp.where(allowed, 0.0, far_below)
        lsecol[...] = jnp.zeros_like(lsecol)

        def pair(hp, carry):
            lanes = pl.ds(pl.multiple_of(hp * 128, 128), 128)
            q_pair = q[at, lanes]
            k_pair = k[:count, lanes]
            v_pair = flat(v[:count // blk, :, lanes])
            total = None
            for i in range(2):
                scores = dot_nt(q_pair, jnp.where(keeps[i], k_pair, 0.0)) + bias[:, :count]
                top = jnp.max(scores, axis=1, keepdims=True)
                weights = jnp.exp(scores - top)
                norm = jnp.sum(weights, axis=1, keepdims=True)
                part = dot(weights.astype(BF), jnp.where(keeps[i], v_pair, 0.0)) * (1.0 / norm)
                total = part if total is None else total + part
                lsecol[...] = jnp.where(lane == 2 * hp + i, top + jnp.log(norm), lsecol[...])
            att[at, lanes] = total.astype(BF)
            return carry

        lax.fori_loop(0, pairs, pair, 0)
        lse[:, at] = lsecol[...].T[:lse.shape[0], :]

    def relay_weights(stage):
        if stage == 0:
            for wire in up_z:
                wire.arrived()
            up_one.start()
            for wire in down_z:
                wire.arrived()
            down_one.start()
            start_all(cot_wires)
        if stage == 1:
            up_one.arrived()
            up_two.start()
            down_one.arrived()
            down_two.start()

    def attention(bias, lsecol):
        for j in range(n_q):
            if j == n_q - 1:
                relay_weights(0)
            attend(j, bias, lsecol)

    pl.run_scoped(attention, pltpu.VMEM((QB, length), F4), pltpu.VMEM((QB, 128), F4))

    att_wire = net.wire(xs.at[0], xr.at[0], mate)

    def half_rows(h, i):
        return pl.ds(pl.multiple_of(h * half + i * QB, QB), QB)

    def out_proj(i, carry):
        part = dot(att[half_rows(cn, i), :], flat(wo[...]))
        xs[0, pl.ds(i * QB, QB), :] = part.astype(BF)
        return carry

    lax.fori_loop(0, per_half, out_proj, 0)
    att_wire.start()

    def out_proj_mine(i, carry):
        mine[pl.ds(i * QB, QB), :] = dot(att[half_rows(c, i), :], flat(wo[...]))
        return carry

    lax.fori_loop(0, per_half, out_proj_mine, 0)
    att_wire.arrived()

    n2_wires = []
    for i in range(rows):
        at = slice(i * blk, (i + 1) * blk)
        middle = x_own[i].astype(F4) + mine[at, :] + xr[0, at, :].astype(F4) + vecs[4:5, :]
        mid[at, :] = middle
        unit, _ = norm_stats(middle)
        n2[c, i] = (unit * vecs[2:3, :] + vecs[3:4, :]).astype(BF)
        wire = net.wire(n2.at[c, i], n2.at[c, i], mate)
        wire.start()
        n2_wires.append(wire)
    relay_weights(1)
    arrived_all(cot_wires)
    cot_mate.start()
    up_own.arrived()
    down_own.arrived()
    up_two.arrived()
    down_two.arrived()

    hid = wup.shape[-1]
    back_wire = net.wire(xs.at[1], xr.at[1], mate)
    mlp_wire = net.wire(xs.at[2], xr.at[2], mate)
    out_wires = swap(out_s, out)
    gm_wires = [net.wire(gm.at[c, i], gm.at[c, i], mate) for i in range(rows)]
    up_rs = (net.wire(gup.at[:, sn], up_r1, x_nbr), net.wire(gup.at[:, s, yn], up_r2, y_nbr))
    down_rs = (net.wire(gdown.at[:, :, yn], down_r1, y_nbr), net.wire(gdown.at[:, sn, y], down_r2, x_nbr))
    up_rz = [net.wire(gup.at[i, s, y], up_r3.at[i], dev(s, y, c, ring(i))) for i in range(1, rows)]
    down_rz = [net.wire(gdown.at[i, s, y], down_r3.at[i], dev(s, y, c, ring(i))) for i in range(1, rows)]
    gelu_scale = math.sqrt(2.0 / math.pi)

    def feed_forward(act, ghid, bup_sum, back_own):
        bup_sum[...] = jnp.zeros_like(bup_sum)

        def block(h, i, keep):
            at = half_rows(h, i)
            n2_block = flat(n2[h, pl.ds(i * per_blk, per_blk)])
            cot_block = flat(cot[h, pl.ds(i * per_blk, per_blk)])
            mlp = back = None
            for p in range(rows):
                cols = slice(p * hid, (p + 1) * hid)
                w_u = flat(wup[p])
                w_d = flat(wdown[p])
                z = dot(n2_block, w_u) + bvec[p, 0:1, lanes_c]
                z2 = z * z
                th = jnp.tanh(gelu_scale * z * (1.0 + 0.044715 * z2))
                cdf = 0.5 * (1.0 + th)
                a = (z * cdf).astype(BF)
                slope = cdf + 0.5 * z * (1.0 - th * th) * (gelu_scale * (1.0 + 3 * 0.044715 * z2))
                act[at, cols] = a
                part = dot(a, w_d)
                mlp = part if mlp is None else mlp + part
                g = (dot_nt(cot_block, w_d) * slope).astype(BF)
                ghid[at, cols] = g
                bup_sum[0:1, cols] += jnp.sum(g.astype(F4), axis=0, keepdims=True)
                part = dot_nt(g, w_u)
                back = part if back is None else back + part
            to = pl.ds(pl.multiple_of(i * QB, QB), QB)
            if keep:
                mine[to, :] = mlp
                back_own[to, :] = back
            else:
                xs[2, to, :] = mlp.astype(BF)
                xs[1, to, :] = back.astype(BF)

        def mine_block(i, carry):
            block(c, i, True)
            return carry

        def mate_block(i, carry):
            block(cn, i, False)
            return carry

        lax.fori_loop(0, per_half, mine_block, 0)
        for wire in n2_wires:
            wire.arrived()
        cot_mate.arrived()
        lax.fori_loop(0, per_half, mate_block, 0)
        back_wire.start()
        mlp_wire.start()

        def down_grad(p, carry):
            cols = pl.ds(pl.multiple_of(p * hid, 128), hid)
            got = dot_tn(act[:, cols], flat(cot[...]))
            gdown[p] = got.astype(BF).reshape(gdown.shape[1:])
            return carry

        lax.fori_loop(0, rows, down_grad, 0)
        down_rs[0].start()

        def up_grad(p, carry):
            cols = pl.ds(pl.multiple_of(p * hid, 128), hid)
            for m in range(2):
                n2_part = flat(n2[:, :, :, m * (width // 2):(m + 1) * (width // 2)])
                got = dot_tn(n2_part, ghid[:, cols])
                gup[p, m] = got.astype(BF).reshape(gup.shape[2:])
            return carry

        lax.fori_loop(0, rows, up_grad, 0)
        up_rs[0].start()
        small[0] = jnp.zeros(small.shape[1:], F4)
        for p in range(rows):
            small[0, pl.ds(8 + ring(p), 1), lanes_c] = bup_sum[0:1, p * hid:(p + 1) * hid]

        back_wire.arrived()
        mlp_wire.arrived()
        sums = [jnp.zeros((1, width), F4) for _ in range(4)]
        for i in range(rows):
            at = slice(i * blk, (i + 1) * blk)
            middle = mid[at, :]
            out_s[i] = (middle + mine[at, :] + xr[2, at, :].astype(F4) + vecs[5:6, :]).astype(BF)
            unit, inverse = norm_stats(middle)
            back = back_own[at, :] + xr[1, at, :].astype(F4)
            cot_block = cot[c, i].astype(F4)
            g_middle = cot_block + norm_back(back, unit, inverse, vecs[2:3, :])
            mid[at, :] = g_middle
            g_low = g_middle.astype(BF)
            gm[c, i] = g_low
            gm_wires[i].start()
            for n, item in enumerate((back * unit, back, g_low.astype(F4), cot_block)):
                sums[n] += jnp.sum(item, axis=0, keepdims=True)
        for n in range(4):
            small[0, 2 + n:3 + n, :] = sums[n]
        start_all(out_wires)

    pl.run_scoped(
        feed_forward,
        pltpu.VMEM((length, rows * hid), BF),
        pltpu.VMEM((length, rows * hid), BF),
        pltpu.VMEM((8, rows * hid), F4),
        pltpu.VMEM((half, width), F4),
    )

    up_own_f = net.own(f_s.at[0], f_up.at[s, y, :, lanes_c])
    up_ag = (
        net.wire(f_s.at[0], f_up.at[s, y, :, lanes_c], x_nbr),
        net.wire(f_up.at[:, y, :, lanes_c], f_up.at[:, y, :, lanes_c], y_nbr),
        net.wire(f_up.at[:, :, :, lanes_c], f_up.at[:, :, :, lanes_c], mate),
    )
    down_own_f = net.own(f_t, f_down.at[c, s, y])
    down_ag = (
        net.wire(f_t, f_down.at[c, s, y], y_nbr),
        net.wire(f_down.at[c, s], f_down.at[c, s], x_nbr),
        net.wire(f_down.at[c], f_down.at[c], mate),
    )

    def add(one, two):
        return (one.astype(F4) + two.astype(F4)).astype(BF)

    def ffn_reduce(stage):
        if stage == 0:
            down_rs[0].arrived()
            up_rs[0].arrived()

            def one(p, carry):
                gdown[p, :, y] = add(gdown[p, :, y], down_r1[p])
                gup[p, s] = add(gup[p, s], up_r1[p])
                return carry

            lax.fori_loop(0, rows, one, 0)
            down_rs[1].start()
            up_rs[1].start()
        if stage == 1:
            down_rs[1].arrived()
            up_rs[1].arrived()

            def two(p, carry):
                gdown[p, s, y] = add(gdown[p, s, y], down_r2[p])
                gup[p, s, y] = add(gup[p, s, y], up_r2[p])
                return carry

            lax.fori_loop(0, rows, two, 0)
            for wire in down_rz + up_rz:
                wire.start()
        if stage == 2:
            for wire in down_rz + up_rz:
                wire.arrived()
            for to, kept, got in ((f_s.at[0], gup[0, s, y], up_r3), (f_t, gdown[0, s, y], down_r3)):
                total = kept.astype(F4)
                for i in range(1, rows):
                    total += got[i].astype(F4)
                to[...] = total.astype(BF)
            for wire in (up_own_f, down_own_f, up_ag[0], down_ag[0]):
                wire.start()
        if stage == 3:
            for wire in (up_own_f, down_own_f, up_ag[0], down_ag[0]):
                wire.arrived()
            up_ag[1].start()
            down_ag[1].start()
        if stage == 4:
            up_ag[1].arrived()
            down_ag[1].arrived()
            up_ag[2].start()
            down_ag[2].start()
        if stage == 5:
            up_ag[2].arrived()
            down_ag[2].arrived()

    back1_wire = net.wire(xs.at[0], xr.at[0], mate)
    gtok_wires = swap(out_s, gtok)
    gfirst_slot = net.recv_slots(rows)
    gfirst_wires = []
    for h in range(2):
        for step in range(rows):
            j = ring(step)
            to_me = (c == 1) & (s == h) & (s == 1) if step == 0 else None
            fine = (c == 1) & jnp.logical_not(to_me) if step == 0 else c == 1
            gfirst_wires.append(net.wire(
                gv_s.at[h * rows + j], gfirst.at[t], dev(h, y, s, j), fine, None, gfirst_slot + step,
            ))
    gfirst_own = net.own(gv_s.at[rows + t], gfirst.at[t], (c == 1) & (s == 1))
    wa_rs = (net.wire(gwa.at[:, :, sn], wa_r1, x_nbr), net.wire(gwa.at[:, :, s, yn], wa_r2, y_nbr))
    wa_rz = []
    for step in range(1, rows):
        to = ring(step)
        wa_rz.append(net.wire(
            gwa.at[:, lax.rem(to, 2), s, y], wa_r3.at[step], dev(s, y, c, to), lax.div(to, 2) == c, home,
        ))
    wa_own_f = net.own(f_w, f_wa.at[:, s, y], home)
    wa_ag = (
        net.wire(f_w, f_wa.at[:, s, y], x_nbr, home, home),
        net.wire(f_wa.at[:, :, y], f_wa.at[:, :, y], y_nbr, home, home),
        net.wire(f_wa, f_wa, mate, home, away),
    )
    lead, follow = c == 0, c == 1
    wv_rs = (
        net.wire(gwv.at[sn], wv_r1, x_nbr, lead, lead),
        net.wire(gwv.at[s, yn], wv_r2, y_nbr, lead, lead),
    )
    wv_rz = [
        net.wire(wv_r3.at[t], wv_r3.at[t], dev(s, y, c, ring(step)), lead, lead) for step in range(1, rows)
    ]
    wv_own_f = net.own(f_v, f_wv.at[s, y], lead)
    wv_ag = (
        net.wire(f_v, f_wv.at[s, y], x_nbr, lead, lead),
        net.wire(f_wv.at[:, y], f_wv.at[:, y], y_nbr, lead, lead),
        net.wire(f_wv, f_wv, mate, lead, follow),
    )
    small_ar = [net.wire(small.at[i], small_r.at[i], to) for i, to in enumerate((mate, x_nbr, y_nbr))]
    small_rz = [net.wire(small_z.at[t], small_z.at[t], dev(s, y, c, ring(step))) for step in range(1, rows)]

    def small_reduce(stage):
        if stage == 0:
            small_ar[0].start()
        elif stage < 3:
            small_ar[stage - 1].arrived()
            small[stage] = small[stage - 1] + small_r[stage - 1]
            small_ar[stage].start()
        elif stage == 3:
            small_ar[2].arrived()
            small_z[t] = small[2] + small_r[2]
            for wire in small_rz:
                wire.start()
        else:
            for wire in small_rz:
                wire.arrived()
            f_small[...] = (small_z[0] + small_z[1]) + (small_z[2] + small_z[3])

    heads_here = heads_width // HEAD_DIM
    pick_head = lax.broadcasted_iota(jnp.int32, (lse.shape[0], heads_width), 1) // HEAD_DIM
    pick = (pick_head == lax.broadcasted_iota(jnp.int32, pick_head.shape, 0)).astype(BF)

    def attention_back(gk, gv, delta, tmp, gq, kt, gqt, bias_t):
        kt[...] = k[...].T
        gk[...] = jnp.zeros_like(gk)
        gv[...] = jnp.zeros_like(gv)

        def grad_att(h, i):
            at = half_rows(h, i)
            block = flat(gm[h, pl.ds(i * per_blk, per_blk)])
            low = dot_nt(block, flat(wo[...])).astype(BF)
            gatt[at, :] = low
            product = low.astype(F4) * att[at, :].astype(F4)
            high = product.astype(BF)
            rest_of = (product - high.astype(F4)).astype(BF)
            delta[:, at] = dot_nt(pick, high) + dot_nt(pick, rest_of)

        def grad_att_mine(i, carry):
            grad_att(c, i)
            return carry

        def grad_att_mate(i, carry):
            grad_att(cn, i)
            return carry

        lax.fori_loop(0, per_half, grad_att_mine, 0)
        for wire in gm_wires:
            wire.arrived()
        lax.fori_loop(0, per_half, grad_att_mate, 0)
        gwa[2] = dot_tn(att[...], flat(gm[...])).astype(BF).reshape(gwa.shape[1:])

        def back_block(j):
            count = (j + 1) * QB
            at = slice(j * QB, count)
            key_pos = lax.broadcasted_iota(jnp.int32, (count, QB), 0)
            query_pos = j * QB + lax.broadcasted_iota(jnp.int32, (count, QB), 1)
            allowed = (segcol[:count, 0:1] == segrow[0:1, at]) & (key_pos <= query_pos)
            bias_t[:count, :] = jnp.where(allowed, 0.0, far_below)

            def pair(hp, carry):
                lanes = pl.ds(pl.multiple_of(hp * 128, 128), 128)
                q_pair = q[at, lanes]
                k_pair = k[:count, lanes]
                v_pair = flat(v[:count // blk, :, lanes])
                ga_pair = gatt[at, lanes]
                sum_k = sum_v = None
                for i in range(2):
                    head = 2 * hp + i
                    scores = dot_nt(jnp.where(keeps[i], k_pair, 0.0), q_pair) + bias_t[:count, :]
                    probs = jnp.exp(scores - lse[pl.ds(head, 1), at])
                    grad_prob = dot_nt(jnp.where(keeps[i], v_pair, 0.0), ga_pair)
                    grad_score = (probs * (grad_prob - delta[pl.ds(head, 1), at])).astype(BF)
                    part_v = dot(probs.astype(BF), jnp.where(keeps[i], ga_pair, 0.0))
                    part_k = dot(grad_score, jnp.where(keeps[i], q_pair, 0.0))
                    sum_v = part_v if sum_v is None else sum_v + part_v
                    sum_k = part_k if sum_k is None else sum_k + part_k
                    channels = pl.ds(pl.multiple_of(hp * 128 + i * HEAD_DIM, HEAD_DIM), HEAD_DIM)
                    gqt[channels, at] = (dot(kt[channels, :count], grad_score) * factor).astype(BF)
                gk[:count, lanes] += sum_k
                gv[:count, lanes] += sum_v
                return carry

            lax.fori_loop(0, pairs, pair, 0)

        for j in range(n_q):
            back_block(j)
            if j >= 1:
                ffn_reduce(j - 1)

        gq[...] = gqt[...].T
        gk_low = gk[...].astype(BF)
        k[...] = gk_low
        gv_s[...] = gv[...].astype(BF).reshape(gv_s.shape)

        def back_rows(h, i):
            at = half_rows(h, i)
            tmp[...] = dot(gq[at, :], flat(wq[...])) + dot(k[at, :], flat(wk[...]))

            @pl.when(lead)
            def _():
                block = flat(gv_s[pl.ds(h * rows + i * per_blk, per_blk)])
                tmp[...] += dot_nt(block, wval[...])

        def back_mate(i, carry):
            back_rows(cn, i)
            xs[0, pl.ds(pl.multiple_of(i * QB, QB), QB), :] = tmp[...].astype(BF)
            return carry

        def back_mine(i, carry):
            back_rows(c, i)
            mine[pl.ds(pl.multiple_of(i * QB, QB), QB), :] = tmp[...]
            return carry

        net.done(att_wire)
        lax.fori_loop(0, per_half, back_mate, 0)
        back1_wire.start()
        for wire in gfirst_wires:
            wire.start()
        gfirst_own.start()
        lax.fori_loop(0, per_half, back_mine, 0)
        n1_all = flat(n1[...])
        gwa[0] = dot(gqt[...], n1_all).astype(BF).reshape(gwa.shape[1:])
        gwa[1] = dot_tn(k[...], n1_all).astype(BF).reshape(gwa.shape[1:])
        wa_rs[0].start()
        small[0, 7:8, lanes_h] = jnp.sum(gq[...].astype(F4), axis=0, keepdims=True)

        @pl.when(lead)
        def _():
            gv_low = flat(gv_s[...])
            gwv[...] = dot_tn(gv_low, n1_all).astype(BF).reshape(gwv.shape)
            small[0, 6:7, :heads_width] = jnp.sum(gv_low.astype(F4), axis=0, keepdims=True)

        wv_rs[0].start()

    lanes_h = pl.ds(pl.multiple_of(c * heads_width, 128), heads_width)
    pl.run_scoped(
        attention_back,
        pltpu.VMEM((length, heads_width), F4),
        pltpu.VMEM((length, heads_width), F4),
        pltpu.VMEM((lse.shape[0], length), F4),
        pltpu.VMEM((QB, width), F4),
        pltpu.VMEM((length, heads_width), BF),
        pltpu.VMEM((heads_width, length), BF),
        pltpu.VMEM((heads_width, length), BF),
        pltpu.VMEM((length, QB), F4),
    )

    back1_wire.arrived()
    for group in out_wires:
        net.done(group[0])
    out_wires[0][1].arrived()
    gain_sum = jnp.zeros((1, width), F4)
    bias_sum = jnp.zeros((1, width), F4)
    for i in range(rows):
        at = slice(i * blk, (i + 1) * blk)
        unit, inverse = norm_stats(x_own[i].astype(F4))
        back = mine[at, :] + xr[0, at, :].astype(F4)
        gain_sum += jnp.sum(back * unit, axis=0, keepdims=True)
        bias_sum += jnp.sum(back, axis=0, keepdims=True)
        out_s[i] = (mid[at, :] + norm_back(back, unit, inverse, vecs[0:1, :])).astype(BF)
    small[0, 0:1, :] = gain_sum
    small[0, 1:2, :] = bias_sum
    start_all(gtok_wires)
    small_reduce(0)

    wa_rs[0].arrived()
    gwa[:, :, s] = add(gwa[:, :, s], wa_r1[...])
    wa_rs[1].start()

    @pl.when(lead)
    def _():
        wv_rs[0].copy.wait_recv()
        gwv[s] = add(gwv[s], wv_r1[...])
        wv_rs[1].copy.start()

    small_reduce(1)
    ffn_reduce(3)
    small_reduce(2)
    wa_rs[1].arrived()
    gwa[:, :, s, y] = add(gwa[:, :, s, y], wa_r2[...])
    for wire in wa_rz:
        wire.start()

    @pl.when(lead)
    def _():
        wv_rs[1].copy.wait_recv()
        wv_r3[t] = add(gwv[s, y], wv_r2[...])
        for wire in wv_rz:
            wire.copy.start()

    small_reduce(3)
    ffn_reduce(4)

    @pl.when(home)
    def _():
        for wire in wa_rz:
            wire.copy.wait_recv()
        total = gwa[:, lax.rem(t, 2), s, y].astype(F4)
        for i in range(1, rows):
            total += wa_r3[i].astype(F4)
        f_w[...] = total.astype(BF)

    wa_own_f.start()
    wa_ag[0].start()

    @pl.when(lead)
    def _():
        for wire in wv_rz:
            wire.copy.wait_recv()
        parts = [wv_r3[i].astype(F4) for i in range(rows)]
        f_v[...] = ((parts[0] + parts[1]) + (parts[2] + parts[3])).astype(BF)

    wv_own_f.start()
    wv_ag[0].start()
    small_reduce(4)
    for stage in range(2):
        for wire in ((wa_own_f, wv_own_f) if stage == 0 else ()) + (wa_ag[stage], wv_ag[stage]):
            wire.arrived()
        wa_ag[stage + 1].start()
        wv_ag[stage + 1].start()
    ffn_reduce(5)
    wa_ag[2].arrived()
    wv_ag[2].arrived()
    for group in out_wires:
        group[0].arrived()
    arrived_all(gtok_wires)
    for step in range(rows):
        def take(step=step):
            pltpu.make_async_remote_copy(
                src_ref=gv_s.at[0], dst_ref=gfirst.at[0], send_sem=send_sems.at[0],
                recv_sem=recv_sems.at[gfirst_slot + step], device_id=mate, device_id_type=MESH,
            ).wait_recv()
        if step == 0:
            pl.when((c == 0) | (s == 0))(take)
        else:
            take()
    gfirst_own.arrived()
    for wire in net.all:
        wire.sent()


def whole_layer(
    tokens, first_values, segment_ids, cotangent, norm1_gain, norm1_bias, w_query, b_query, w_key,
    w_value, b_value, w_out, b_out, norm2_gain, norm2_bias, w_up, b_up, w_down, b_down,
):
    rows, blk, width = tokens.shape
    half = rows * blk
    length = 2 * half
    valf = w_value.shape[1]
    tp_width = w_query.shape[1]
    hid = w_up.shape[1] // 2
    t = lax.axis_index("tp")
    wa_in = jnp.stack([w_query.T, w_key.T, w_out]).reshape(3, 2, 2, tp_width // 4, width)
    odd = lax.rem(t, 2) == 1
    b_q = jnp.where(odd, jnp.pad(b_query, (tp_width, width - 2 * tp_width)), jnp.pad(b_query, (0, width - tp_width)))
    bvec = jnp.concatenate([b_up[None], b_q[None], jnp.zeros((6, width), F4)])
    vecs = jnp.stack([
        norm1_gain, norm1_bias, norm2_gain, norm2_bias, b_out, b_down,
        jnp.pad(b_value, (0, width - valf)), jnp.zeros((width,), F4),
    ])
    hbm = pl.BlockSpec(memory_space=pl.ANY)
    vmem = pl.BlockSpec(memory_space=pltpu.VMEM)
    piece = tp_width // 4
    up_rows, down_rows = width // 4, hid // 4

    def of(*shape, dtype=BF):
        return jax.ShapeDtypeStruct(shape, dtype)

    def room(*shape, dtype=BF):
        return pltpu.VMEM(shape, dtype)

    outs = (
        of(rows, blk, width), of(rows, blk, width), of(rows, blk, valf),
        of(2, 2, up_rows, 2 * hid), of(2, 2, 2, down_rows, width),
        of(3, 2, 2, piece, width), of(2, 2, valf // 4, width), of(16, width, dtype=F4),
    )
    scratch = [
        room(rows, blk, width), room(2, rows, blk, width), room(2, 8, length, dtype=jnp.int32),
        room(8, length, dtype=F4), room(length, 128, dtype=F4), room(rows, 8, width, dtype=F4),
        room(3, 2, 2, 2, piece, width), room(width, valf),
        room(rows, 2, 2, up_rows, hid), room(rows, 2, 2, down_rows, width),
        room(length, 2 * tp_width), room(length, 2 * tp_width), room(2 * rows, blk, valf),
        room(length, 2 * tp_width), room(16, length, dtype=F4),
        room(half, width, dtype=F4), room(2, rows, blk, width), room(2, rows, blk, width),
        room(half, width, dtype=F4), room(3, half, width), room(3, half, width),
        room(rows, blk, width), room(2, rows, blk, width),
        room(length, 2 * tp_width), room(2 * rows, blk, valf),
        room(rows, 2, 2, up_rows, hid), room(rows, 2, 2, down_rows, width),
        room(rows, 2, up_rows, hid), room(rows, up_rows, hid), room(rows, up_rows, hid),
        room(rows, 2, down_rows, width), room(rows, down_rows, width), room(rows, down_rows, width),
        room(3, 2, 2, 2, piece, width), room(3, 2, 2, piece, width), room(3, 2, piece, width), room(rows, 3, piece, width),
        room(2, 2, valf // 4, width), room(2, valf // 4, width), room(valf // 4, width), room(rows, valf // 4, width),
        room(3, 16, width, dtype=F4), room(3, 16, width, dtype=F4), room(rows, 16, width, dtype=F4),
        room(1, up_rows, hid), room(down_rows, width), room(3, piece, width), room(valf // 4, width),
        pltpu.SemaphoreType.DMA((SENDS,)), pltpu.SemaphoreType.DMA((RECVS,)), pltpu.SemaphoreType.DMA((OWNS,)),
    ]
    out, gtok, gfirst, f_up, f_down, f_wa, f_wv, f_small = pl.pallas_call(
        layer_kernel,
        out_shape=outs,
        in_specs=[hbm, hbm, hbm, vmem, hbm, hbm, hbm, hbm, vmem, vmem],
        out_specs=(hbm,) * 7 + (vmem,),
        scratch_shapes=scratch,
        compiler_params=pltpu.CompilerParams(
            collective_id=0, has_side_effects=True, vmem_limit_bytes=VMEM_BYTES
        ),
    )(
        tokens, first_values, cotangent, segment_ids, wa_in,
        w_up.reshape(2, 2, up_rows, 2 * hid), w_down.reshape(2, 2, 2, down_rows, width), w_value, bvec, vecs,
    )
    wa_flat = f_wa.reshape(3, tp_width, width).astype(F4)
    grad_b_query = lax.dynamic_slice(f_small, (7, t * tp_width), (1, tp_width))[0]
    grad_b_up = lax.dynamic_slice(f_small, (8 + t, 0), (1, width))[0]
    return (
        out,
        gtok.astype(F4),
        gfirst,
        f_small[0],
        f_small[1],
        wa_flat[0].T,
        grad_b_query,
        wa_flat[1].T,
        f_wv.reshape(valf, width).astype(F4).T,
        f_small[6, :valf],
        wa_flat[2],
        f_small[4],
        f_small[2],
        f_small[3],
        f_up.reshape(width, 2 * hid).astype(F4),
        grad_b_up,
        f_down.reshape(2 * hid, width).astype(F4),
        f_small[5],
    )


SENDS = 120
RECVS = 120
OWNS = 16
VMEM_BYTES = 63 * 1024 * 1024


def fits(mesh):
    return mesh.shape["seq"] == 2 and mesh.shape["batch"] == 4 and mesh.shape["tp"] == 4


def solution(mesh):
    placed = (
        P("batch", ("seq", "tp"), None),
        P("batch", ("seq", "tp"), None),
        P("batch", None),
        P("batch", ("seq", "tp"), None),
        P(),
        P(),
        P(None, "tp"),
        P("tp"),
        P(None, "tp"),
        P(),
        P(),
        P("tp", None),
        P(),
        P(),
        P(),
        P(None, "tp"),
        P("tp"),
        P("tp", None),
        P(),
    )
    return jax.shard_map(
        whole_layer if fits(mesh) else on_device,
        mesh=mesh,
        in_specs=placed,
        out_specs=(
            P("batch", ("seq", "tp"), None),
            P("batch", ("seq", "tp"), None),
            P("batch", ("seq", "tp"), None),
            P(),
            P(),
            P(None, "tp"),
            P("tp"),
            P(None, "tp"),
            P(),
            P(),
            P("tp", None),
            P(),
            P(),
            P(),
            P(None, "tp"),
            P("tp"),
            P("tp", None),
            P(),
        ),
        check_vma=False,
    )
```

```python
import math

import jax
import jax.numpy as jnp
from jax import lax
from jax.experimental import pallas as pl
from jax.experimental.pallas import tpu as pltpu
from jax.sharding import PartitionSpec as P

HEADS = 12
HEAD_DIM = 64


eps = 1e-05
block_cap = 256
far_below = -1e30


def from_behind(block, axis, distance):
    devices = range(lax.axis_size(axis))
    route = [((i - distance) % len(devices), i) for i in devices]
    return lax.ppermute(block, axis, route)


def layer_norm(values, norm_gain, norm_bias):
    average = jnp.mean(values, axis=-1, keepdims=True)
    centered = values - average
    inverse = lax.rsqrt(jnp.mean(centered * centered, axis=-1, keepdims=True) + eps)
    unit = centered * inverse
    return (unit * norm_gain + norm_bias, unit, inverse)


def norm_back(grad_result, unit, inverse, norm_gain):
    scaled = grad_result * norm_gain
    return inverse * (
        scaled
        - jnp.mean(scaled, axis=-1, keepdims=True)
        - unit * jnp.mean(scaled * unit, axis=-1, keepdims=True)
    )


def project(values, weight):
    return jnp.einsum("rtd,de->rte", values, weight, preferred_element_type=jnp.float32)


def project_back(grads, weight):
    return jnp.einsum("rte,de->rtd", grads, weight, preferred_element_type=jnp.float32)


def weight_grad(values, grads):
    return jnp.einsum("rtd,rte->de", values, grads, preferred_element_type=jnp.float32)


def column_sum(values):
    return jnp.sum(values, axis=(0, 1), dtype=jnp.float32)


def gelu_tanh(values):
    return jax.nn.gelu(values, approximate=True)


def over_key_blocks(arrays, key_first, state, step, limit):
    count = arrays[0].shape[1]
    width = math.gcd(count, block_cap)

    def one(index, carry):
        offset = index * width
        parts = tuple((lax.dynamic_slice_in_dim(item, offset, width, 1) for item in arrays))
        first_key = key_first + offset

        def taken(inner):
            return step(inner, parts, first_key, offset)

        def skipped(inner):
            return inner

        return lax.cond(first_key <= limit, taken, skipped, carry)

    return lax.fori_loop(0, count // width, one, state)


def on_device(
    tokens,
    first_values,
    segment_ids,
    cotangent,
    norm1_gain,
    norm1_bias,
    w_query,
    b_query,
    w_key,
    w_value,
    b_value,
    w_out,
    b_out,
    norm2_gain,
    norm2_bias,
    w_up,
    b_up,
    w_down,
    b_down,
):
    rows = tokens.shape[0]
    model_width = tokens.shape[2]
    tp_count = lax.axis_size("tp")
    seq_count = lax.axis_size("seq")
    local_len = tokens.shape[1] * tp_count
    heads = w_query.shape[1] // HEAD_DIM
    width_tp = heads * HEAD_DIM
    valf_all = w_value.shape[1]
    factor = HEAD_DIM ** (-0.5)
    seq_index = lax.axis_index("seq")
    head_first = lax.axis_index("tp") * heads
    is_fresh = head_first < HEADS // 2
    fresh_col = jnp.minimum(head_first * HEAD_DIM, valf_all - width_tp)
    reuse_col = jnp.maximum(head_first * HEAD_DIM - valf_all, 0)
    own_first = seq_index * local_len
    own_last = own_first + local_len - 1
    own_pos = own_first + jnp.arange(local_len, dtype=jnp.int32)
    own_seg = lax.dynamic_slice_in_dim(segment_ids, own_first, local_len, 1)

    def masked_scores(query4, key_part, query_pos, query_seg, key_first):
        width = key_part.shape[1]
        scores = (
            jnp.einsum("rqhc,rkhc->rhqk", query4, key_part, preferred_element_type=jnp.float32)
            * factor
        )
        key_seg = lax.dynamic_slice_in_dim(segment_ids, key_first, width, 1)
        key_pos = key_first + jnp.arange(width, dtype=jnp.int32)
        allowed = (query_seg[:, :, None] == key_seg[:, None, :]) & (
            key_pos[None, None, :] <= query_pos[None, :, None]
        )
        return (scores, allowed[:, None])

    resid = tokens.astype(jnp.float32)
    normed_one, unit_one, inverse_one = layer_norm(resid, norm1_gain, norm1_bias)
    rows_one, grad_rows, first_rows = (
        lax.all_gather(normed_one.astype(jnp.bfloat16), "tp", axis=1, tiled=True),
        lax.all_gather(cotangent, "tp", axis=1, tiled=True),
        lax.all_gather(first_values, "tp", axis=1, tiled=True),
    )
    query4 = (
        (project(rows_one, w_query) + b_query)
        .astype(jnp.bfloat16)
        .reshape(rows, local_len, heads, HEAD_DIM)
    )
    keys4 = project(rows_one, w_key).astype(jnp.bfloat16).reshape(rows, local_len, heads, HEAD_DIM)
    w_part = lax.dynamic_slice_in_dim(w_value, fresh_col, width_tp, 1)
    b_part = lax.dynamic_slice_in_dim(b_value, fresh_col, width_tp, 0)

    def fresh_side(normed_rows):
        return (project(normed_rows, w_part) + b_part).astype(jnp.bfloat16)

    def reuse_side(normed_rows):
        return lax.dynamic_slice_in_dim(first_rows, reuse_col, width_tp, 2)

    vals4 = lax.cond(is_fresh, fresh_side, reuse_side, rows_one).reshape(
        rows, local_len, heads, HEAD_DIM
    )

    def stats_step(carry, parts, key_first, offset):
        top, total = carry
        scores, allowed = masked_scores(query4, parts[0], own_pos, own_seg, key_first)
        masked = jnp.where(allowed, scores, far_below)
        new_top = jnp.maximum(top, jnp.max(masked, axis=3))
        weights = jnp.where(allowed, jnp.exp(masked - new_top[..., None]), 0.0)
        return (new_top, total * jnp.exp(top - new_top) + jnp.sum(weights, axis=3))

    start_top = jnp.full((rows, heads, local_len), far_below, jnp.float32)
    start_total = jnp.zeros((rows, heads, local_len), jnp.float32)
    top, total = over_key_blocks(
        (lax.all_gather(keys4, "seq", axis=1, tiled=True),),
        jnp.int32(0),
        (start_top, start_total),
        stats_step,
        own_last,
    )
    lse = top + jnp.log(total)

    def value_step(acc, parts, key_first, offset):
        scores, allowed = masked_scores(query4, parts[0], own_pos, own_seg, key_first)
        weights = jnp.where(allowed, jnp.exp(scores - lse[..., None]), 0.0).astype(jnp.bfloat16)
        return acc + jnp.einsum(
            "rhqk,rkhc->rqhc", weights, parts[1], preferred_element_type=jnp.float32
        )

    zeros_q = jnp.zeros((rows, local_len, heads, HEAD_DIM), jnp.float32)
    attended = over_key_blocks(
        (
            lax.all_gather(keys4, "seq", axis=1, tiled=True),
            lax.all_gather(vals4, "seq", axis=1, tiled=True),
        ),
        jnp.int32(0),
        zeros_q,
        value_step,
        own_last,
    )
    attended_low = attended.astype(jnp.bfloat16).reshape(rows, local_len, width_tp)
    attn_share = lax.psum_scatter(
        project(attended_low, w_out).astype(jnp.bfloat16), "tp", scatter_dimension=1, tiled=True
    ).astype(jnp.float32)
    middle = resid + attn_share + b_out
    normed_two, unit_two, inverse_two = layer_norm(middle, norm2_gain, norm2_bias)
    rows_two = lax.all_gather(normed_two.astype(jnp.bfloat16), "tp", axis=1, tiled=True)
    hidden_pre = project(rows_two, w_up) + b_up
    activated_full, gelu_pull = jax.vjp(gelu_tanh, hidden_pre)
    activated = activated_full.astype(jnp.bfloat16)
    mlp_share = lax.psum_scatter(
        project(activated, w_down).astype(jnp.bfloat16), "tp", scatter_dimension=1, tiled=True
    ).astype(jnp.float32)
    output = (middle + mlp_share + b_down).astype(jnp.bfloat16)
    grad_b_down = column_sum(grad_rows)
    grad_w_down = weight_grad(activated, grad_rows)
    grad_hidden = gelu_pull(project_back(grad_rows, w_down))[0].astype(jnp.bfloat16)
    grad_b_up = column_sum(grad_hidden)
    grad_w_up = weight_grad(rows_two, grad_hidden)
    back_two = lax.psum_scatter(
        project_back(grad_hidden, w_up).astype(jnp.bfloat16), "tp", scatter_dimension=1, tiled=True
    ).astype(jnp.float32)
    grad_gain_two = jnp.sum(back_two * unit_two, axis=(0, 1))
    grad_bias_two = jnp.sum(back_two, axis=(0, 1))
    grad_middle = cotangent.astype(jnp.float32) + norm_back(
        back_two, unit_two, inverse_two, norm2_gain
    )
    grad_mid_rows = lax.all_gather(grad_middle.astype(jnp.bfloat16), "tp", axis=1, tiled=True)
    grad_b_out = column_sum(grad_mid_rows)
    grad_w_out = weight_grad(attended_low, grad_mid_rows)
    grad_out4 = (
        project_back(grad_mid_rows, w_out)
        .astype(jnp.bfloat16)
        .reshape(rows, local_len, heads, HEAD_DIM)
    )
    delta = jnp.einsum("rqhc,rqhc->rhq", grad_out4.astype(jnp.float32), attended)

    def pair_terms(key_side, val_side, key_first, grad_query, grad_keys, grad_vals):

        def pair_step(carry, parts, first, offset):
            acc_query, acc_keys, acc_vals = carry
            key_part, val_part = parts
            width = key_part.shape[1]
            scores, allowed = masked_scores(query4, key_part, own_pos, own_seg, first)
            probs = jnp.where(allowed, jnp.exp(scores - lse[..., None]), 0.0)
            grad_val = jnp.einsum(
                "rhqk,rqhc->rkhc",
                probs.astype(jnp.bfloat16),
                grad_out4,
                preferred_element_type=jnp.float32,
            )
            grad_prob = jnp.einsum(
                "rqhc,rkhc->rhqk", grad_out4, val_part, preferred_element_type=jnp.float32
            )
            grad_score = (probs * (grad_prob - delta[..., None])).astype(jnp.bfloat16)
            acc_query = (
                acc_query
                + jnp.einsum(
                    "rhqk,rkhc->rqhc", grad_score, key_part, preferred_element_type=jnp.float32
                )
                * factor
            )
            grad_key = (
                jnp.einsum(
                    "rhqk,rqhc->rkhc", grad_score, query4, preferred_element_type=jnp.float32
                )
                * factor
            )
            acc_keys = lax.dynamic_update_slice_in_dim(
                acc_keys, lax.dynamic_slice_in_dim(acc_keys, offset, width, 1) + grad_key, offset, 1
            )
            acc_vals = lax.dynamic_update_slice_in_dim(
                acc_vals, lax.dynamic_slice_in_dim(acc_vals, offset, width, 1) + grad_val, offset, 1
            )
            return (acc_query, acc_keys, acc_vals)

        return over_key_blocks(
            (key_side, val_side), key_first, (grad_query, grad_keys, grad_vals), pair_step, own_last
        )

    def turn_keys(turn, carry):
        moving_keys, moving_vals, moving_gk, moving_gv, grad_query = carry
        anchor = (seq_index - turn) % seq_count
        grad_query, moving_gk, moving_gv = pair_terms(
            moving_keys, moving_vals, anchor * local_len, grad_query, moving_gk, moving_gv
        )
        moving_keys, moving_vals, moving_gk, moving_gv = (
            from_behind(moving_keys, "seq", 1),
            from_behind(moving_vals, "seq", 1),
            from_behind(moving_gk.astype(jnp.bfloat16), "seq", 1).astype(moving_gk.dtype),
            from_behind(moving_gv.astype(jnp.bfloat16), "seq", 1).astype(moving_gv.dtype),
        )
        return (moving_keys, moving_vals, moving_gk, moving_gv, grad_query)

    start_state = (keys4, vals4, zeros_q, zeros_q, zeros_q)
    final_state = lax.fori_loop(0, seq_count, turn_keys, start_state)
    grad_keys4, grad_vals4, grad_query4 = (final_state[2], final_state[3], final_state[4])
    grad_query = grad_query4.astype(jnp.bfloat16).reshape(rows, local_len, width_tp)
    grad_keys = grad_keys4.astype(jnp.bfloat16).reshape(rows, local_len, width_tp)
    grad_vals = grad_vals4.astype(jnp.bfloat16).reshape(rows, local_len, width_tp)

    def fresh_back(grad_flat):
        gw_full = lax.dynamic_update_slice_in_dim(
            jnp.zeros((model_width, valf_all), jnp.float32),
            weight_grad(rows_one, grad_flat),
            fresh_col,
            1,
        )
        gb_full = lax.dynamic_update_slice_in_dim(
            jnp.zeros((valf_all,), jnp.float32), column_sum(grad_flat), fresh_col, 0
        )
        back_value = project_back(grad_flat, w_part)
        reuse_full = jnp.zeros((rows, local_len, valf_all), jnp.float32)
        return (gw_full, gb_full, back_value, reuse_full)

    def reuse_back(grad_flat):
        gw_full = jnp.zeros((model_width, valf_all), jnp.float32)
        gb_full = jnp.zeros((valf_all,), jnp.float32)
        back_value = jnp.zeros((rows, local_len, model_width), jnp.float32)
        reuse_full = lax.dynamic_update_slice_in_dim(
            jnp.zeros((rows, local_len, valf_all), jnp.float32),
            grad_flat.astype(jnp.float32),
            reuse_col,
            2,
        )
        return (gw_full, gb_full, back_value, reuse_full)

    grad_w_value, grad_b_value, back_value, reuse_full = lax.cond(
        is_fresh, fresh_back, reuse_back, grad_vals
    )
    grad_b_query = column_sum(grad_query)
    grad_w_query = weight_grad(rows_one, grad_query)
    grad_w_key = weight_grad(rows_one, grad_keys)
    back_terms = project_back(grad_query, w_query) + project_back(grad_keys, w_key) + back_value
    back_one, reuse_sum = (
        lax.psum_scatter(
            back_terms.astype(jnp.bfloat16), "tp", scatter_dimension=1, tiled=True
        ).astype(jnp.float32),
        lax.psum_scatter(
            reuse_full.astype(jnp.bfloat16), "tp", scatter_dimension=1, tiled=True
        ).astype(jnp.float32),
    )
    grad_first_values = reuse_sum.astype(jnp.bfloat16)
    grad_gain_one = jnp.sum(back_one * unit_one, axis=(0, 1))
    grad_bias_one = jnp.sum(back_one, axis=(0, 1))
    grad_tokens = grad_middle + norm_back(back_one, unit_one, inverse_one, norm1_gain)
    summed = lax.psum(
        (
            grad_w_query,
            grad_w_key,
            grad_w_out,
            grad_w_up,
            grad_w_down,
            grad_b_query,
            grad_b_out,
            grad_b_up,
            grad_b_down,
        ),
        ("seq", "batch"),
    )
    norm_sums = lax.psum(
        (grad_gain_one, grad_bias_one, grad_gain_two, grad_bias_two, grad_w_value, grad_b_value),
        ("seq", "batch", "tp"),
    )
    return (
        output,
        grad_tokens,
        grad_first_values,
        norm_sums[0],
        norm_sums[1],
        summed[0],
        summed[5],
        summed[1],
        norm_sums[4],
        norm_sums[5],
        summed[2],
        summed[6],
        norm_sums[2],
        norm_sums[3],
        summed[3],
        summed[7],
        summed[4],
        summed[8],
    )


BF = jnp.bfloat16
F4 = jnp.float32
MESH = pl.DeviceIdType.MESH
QB = 256


def dot(a, b):
    return lax.dot_general(a, b, (((1,), (0,)), ((), ())), preferred_element_type=F4)


def dot_nt(a, b):
    return lax.dot_general(a, b, (((1,), (1,)), ((), ())), preferred_element_type=F4)


def dot_tn(a, b):
    return lax.dot_general(a, b, (((0,), (0,)), ((), ())), preferred_element_type=F4)


def maybe(cond, act):
    if cond is None:
        act()
    else:
        pl.when(cond)(act)


class Wire:
    def __init__(self, copy, send_if=None, recv_if=None):
        self.copy, self.send_if, self.recv_if = copy, send_if, recv_if

    def start(self):
        maybe(self.send_if, self.copy.start)

    def arrived(self):
        maybe(self.recv_if, self.copy.wait_recv)

    def sent(self):
        maybe(self.send_if, self.copy.wait_send)


class Own:
    def __init__(self, copy, when=None):
        self.copy, self.when = copy, when

    def start(self):
        maybe(self.when, self.copy.start)

    def arrived(self):
        maybe(self.when, self.copy.wait)

    def sent(self):
        pass


class Net:
    def __init__(self, send_sems, recv_sems, own_sems):
        self.send_sems, self.recv_sems, self.own_sems = send_sems, recv_sems, own_sems
        self.n_send = self.n_recv = self.n_own = 0
        self.all = []

    def recv_slots(self, count):
        self.n_recv += count
        return self.n_recv - count

    def wire(self, src, dst, device, send_if=None, recv_if=None, slot=None):
        if slot is None:
            slot = self.recv_slots(1)
        copy = pltpu.make_async_remote_copy(
            src_ref=src,
            dst_ref=dst,
            send_sem=self.send_sems.at[self.n_send],
            recv_sem=self.recv_sems.at[slot],
            device_id=device,
            device_id_type=MESH,
        )
        self.n_send += 1
        made = Wire(copy, send_if, recv_if)
        self.all.append(made)
        return made

    def done(self, wire):
        wire.sent()
        self.all = [item for item in self.all if item is not wire]

    def own(self, src, dst, when=None):
        copy = pltpu.make_async_copy(src, dst, self.own_sems.at[self.n_own])
        self.n_own += 1
        return Own(copy, when)


def norm_stats(values):
    average = jnp.mean(values, axis=-1, keepdims=True)
    centered = values - average
    inverse = lax.rsqrt(jnp.mean(centered * centered, axis=-1, keepdims=True) + eps)
    return centered * inverse, inverse


def layer_kernel(
    tokens, first, cot_in, seg, wa_in, wup_in, wdown_in, wval_in, bvec_in, vecs,
    out, gtok, gfirst, f_up, f_down, f_wa, f_wv, f_small,
    x_own, n1, segint, segrow, segcol, bvec, wa, wval, wup, wdown,
    q, k, v, att, lse, mid, n2, cot,
    mine, xs, xr, out_s, gm, gatt, gv_s,
    gup, gdown, up_r1, up_r2, up_r3, down_r1, down_r2, down_r3,
    gwa, wa_r1, wa_r2, wa_r3, gwv, wv_r1, wv_r3,
    small, small_p, small_z, f_s, f_t, f_w, f_v,
    send_sems, recv_sems, own_sems,
):
    s, b, t = lax.axis_index("seq"), lax.axis_index("batch"), lax.axis_index("tp")
    y, c = lax.div(b, 2), lax.rem(b, 2)
    sn, yn, cn = 1 - s, 1 - y, 1 - c
    rows, blk, width = tokens.shape
    half = rows * blk
    length = 2 * half
    net = Net(send_sems, recv_sems, own_sems)

    def dev(ds, dy, dc, dt):
        return (ds, 2 * dy + dc, dt)

    def ring(step):
        return lax.rem(t + step + rows, rows)

    x_nbr, y_nbr, diag, mate = dev(sn, y, c, t), dev(s, yn, c, t), dev(sn, yn, c, t), dev(s, y, cn, t)
    home = lax.div(t, 2) == c
    away = lax.div(t, 2) != c
    same, other = s == c, s != c

    gate = pltpu.get_barrier_semaphore()
    peers = [(ds, 2 * yn + dc, t) for ds in range(2) for dc in range(2)]
    for ds in range(2):
        for dc in range(2):
            for dt in range(rows):
                if ds or dc or dt:
                    peers.append((lax.rem(s + ds, 2), 2 * y + lax.rem(c + dc, 2), lax.rem(t + dt, rows)))
    for peer in peers:
        pl.semaphore_signal(gate, inc=1, device_id=peer, device_id_type=MESH)
    pl.semaphore_wait(gate, len(peers))

    def swap(src, dst):
        wires = []
        for step in range(rows):
            r = ring(step)
            if step == 0:
                wires.append((
                    net.wire(src.at[r], dst.at[t], dev(c, y, s, r), other, other),
                    net.own(src.at[r], dst.at[t], same),
                ))
            else:
                wires.append((net.wire(src.at[r], dst.at[t], dev(c, y, s, r)),))
        return wires

    def start_all(wires):
        for group in wires:
            for wire in group:
                wire.start()

    def sent_all(wires):
        for wire in wires:
            net.done(wire)

    def arrived_all(wires):
        for group in wires:
            for wire in group:
                wire.arrived()

    seg_wire = net.wire(segint.at[0], segint.at[1], mate)
    bvec_wires = []
    for step in range(1, rows):
        bvec_wires.append(net.wire(bvec.at[0], bvec.at[step], dev(s, y, c, ring(-step))))
    wa_own = net.own(wa_in, wa.at[:, lax.rem(t, 2)], home)
    token_wires = swap(tokens, x_own)
    wval_own = net.own(wval_in, wval, c == 0)
    lanes_c = pl.ds(pl.multiple_of(c * (wup.shape[-1]), 128), wup.shape[-1])
    up_own = net.own(wup_in.at[:, :, :, lanes_c], wup.at[0])
    down_own = net.own(wdown_in.at[c], wdown.at[0])

    first_slot = net.recv_slots(2 * rows)
    first_wires = []
    for step in range(rows):
        r = ring(step)
        to = net.wire(
            first.at[r], v.at[s * rows + t], dev(c, y, 1, r),
            (c == 0) | (s == 0) if step == 0 else None, None, first_slot + s * rows + step,
        )
        first_wires.append(to)
    first_own = net.own(first.at[t], v.at[s * rows + t], (c == 1) & (s == 1))

    def first_arrived():
        for source in range(2):
            for step in range(rows):
                def take(source=source, step=step):
                    pltpu.make_async_remote_copy(
                        src_ref=first.at[0], dst_ref=v.at[0], send_sem=send_sems.at[0],
                        recv_sem=recv_sems.at[first_slot + source * rows + step],
                        device_id=mate, device_id_type=MESH,
                    ).wait_recv()
                if source == 1 and step == 0:
                    pl.when(s == 0)(take)
                else:
                    take()
        first_own.arrived()

    def along(own_piece, at_slot, only=None):
        rounds = []
        for r in range(1, rows):
            pair = []
            for right in (True, False):
                source = t - (r - 1) if right else t + (r - 1)
                came = t - r if right else t + r
                inside = (source >= 0) & (t < rows - 1) if right else (source < rows) & (t > 0)
                comes = came >= 0 if right else came < rows
                if only is not None:
                    inside, comes = inside & only(source), comes & only(came)
                held = (rows - r + 1 if right else r - 1) % rows
                lands = rows - r if right else r
                src = own_piece if r == 1 else at_slot(source, held)
                to = dev(s, y, c, jnp.minimum(t + 1, rows - 1) if right else jnp.maximum(t - 1, 0))
                pair.append(net.wire(src, at_slot(source, lands), to, inside, comes))
            rounds.append(pair)
        return rounds

    def heads_slot(source, step):
        return wa.at[:, lax.rem(source + rows, 2), s, y]

    wa_z = along(wa_in.at[:, s, y], heads_slot, lambda source: lax.div(source, 2) == c)
    up_z = along(wup_in.at[s, y, :, lanes_c], lambda source, step: wup.at[step, s, y])
    down_z = along(wdown_in.at[c, s, y], lambda source, step: wdown.at[step, s, y])

    class Relay:
        def __init__(self, k_, at_one, at_two, x_first, when=None):
            self.k, self.when = k_, when
            self.one = net.wire(at_one, at_one, x_nbr if x_first else y_nbr, when, when)
            self.two = net.wire(at_two, at_two, y_nbr if x_first else x_nbr, when, when)

        def at_round(self, r, act):
            if r == self.k:
                pl.when(t + self.k < rows)(act)
            if r == rows - self.k:
                pl.when(t + self.k >= rows)(act)

        def first_hop(self, r):
            self.at_round(r, self.one.start)

        def second_hop(self, r):
            def act():
                self.one.arrived()
                self.two.start()

            self.at_round(r, act)

    wa_relay, up_relay, down_relay = [], [], []
    for k_ in range(1, rows):
        source = ring(k_)
        slot_of = lax.rem(source, 2)
        wa_relay.append(Relay(
            k_, wa.at[:, slot_of, s, y], wa.at[:, slot_of, :, y], True, lax.div(source, 2) == c,
        ))
        up_relay.append(Relay(k_, wup.at[k_, s, y], wup.at[k_, :, y], True))
        down_relay.append(Relay(k_, wdown.at[k_, s, y], wdown.at[k_, s], False))
    cot_wires = swap(cot_in, cot.at[s])
    cot_mate = net.wire(cot.at[c], cot.at[c], mate)

    bvec[0] = bvec_in[...]
    row_ids = lax.broadcasted_iota(jnp.int32, seg.shape, 0)
    seg_row = jnp.sum(jnp.where(row_ids == t, seg[...], 0), axis=0, keepdims=True)
    segint[0] = jnp.broadcast_to(seg_row, segint.shape[1:])
    for group in (wa_z[0], up_z[0], down_z[0]):
        for wire in group:
            wire.start()
    seg_wire.start()
    for wire in bvec_wires:
        wire.start()
    for own in (wa_own, wval_own, up_own, down_own):
        own.start()

    paths = ((wa_z, wa_relay), (up_z, up_relay), (down_z, down_relay))

    def hop(r):
        for wires, relays in paths:
            for wire in wires[r - 1]:
                wire.arrived()
            if r < rows - 1:
                for wire in wires[r]:
                    wire.start()
            for relay in relays:
                relay.first_hop(r)

    def second_hop(r):
        for _, relays in paths:
            for relay in relays:
                relay.second_hop(r)

    hop(1)
    hop(2)
    start_all(token_wires)
    second_hop(1)
    seg_wire.arrived()
    chosen = jnp.where(same, segint[0], segint[1]).astype(F4)
    segrow[...] = chosen
    for part in range(length // 128):
        piece = jnp.broadcast_to(chosen[0:1, part * 128:(part + 1) * 128], (128, 128))
        segcol[part * 128:(part + 1) * 128, :] = piece.T
    hop(3)
    second_hop(2)
    sent_all([group[0] for group in token_wires[1:]])
    for wire in first_wires:
        wire.start()
    first_own.start()

    n1_wires = []
    for step in range(rows):
        place = ring(-step)
        for wire in token_wires[step]:
            wire.arrived()
        unit, _ = norm_stats(x_own[place].astype(F4))
        n1[c, place] = (unit * vecs[0:1, :] + vecs[1:2, :]).astype(BF)
        wire = net.wire(n1.at[c, place], n1.at[c, place], mate)
        wire.start()
        n1_wires.append(wire)
    second_hop(3)
    for relay in wa_relay:
        relay.two.arrived()
    wa_own.arrived()
    wval_own.arrived()
    for wire in bvec_wires:
        wire.arrived()
    for wire in n1_wires:
        wire.arrived()

    heads_width = q.shape[1]
    factor = HEAD_DIM ** (-0.5)
    b_q = (bvec[lax.rem(2 * c + rows - t, rows), 1:2, :heads_width]
           + bvec[lax.rem(2 * c + 1 + rows - t, rows), 1:2, :heads_width])
    wq, wk, wo = (wa.at[i] for i in range(3))

    def flat(ref_value):
        return ref_value.reshape(-1, ref_value.shape[-1])

    per_half = half // QB
    per_blk = QB // blk

    def n1_rows(i):
        return flat(n1[lax.div(i, per_half), pl.ds(lax.rem(i, per_half) * per_blk, per_blk)])

    def project_in(i, carry):
        at = pl.ds(pl.multiple_of(i * QB, QB), QB)
        block = n1_rows(i)
        q[at, :] = ((dot_nt(block, flat(wq[...])) + b_q) * factor).astype(BF)
        k_block = dot_nt(block, flat(wk[...]))
        k[at, :] = k_block.astype(BF)
        return carry

    lax.fori_loop(0, length // QB, project_in, 0)
    sent_all(first_wires)
    start_all(cot_wires)


    @pl.when(c == 0)
    def _():
        def fresh(i, carry):
            got = (dot(n1_rows(i), wval[...]) + vecs[6:7, :heads_width]).astype(BF)
            v[pl.ds(i * per_blk, per_blk)] = got.reshape(per_blk, blk, heads_width)
            return carry

        lax.fori_loop(0, length // QB, fresh, 0)

    @pl.when(c == 1)
    def _():
        first_arrived()

    pairs = heads_width // 128
    n_q = length // QB
    lane = lax.broadcasted_iota(jnp.int32, (1, 128), 1)
    keeps = (lane < HEAD_DIM, lane >= HEAD_DIM)

    def attend(j, bias, lsecol):
        count = (j + 1) * QB
        at = slice(j * QB, count)
        key_pos = lax.broadcasted_iota(jnp.int32, (QB, count), 1)
        query_pos = j * QB + lax.broadcasted_iota(jnp.int32, (QB, count), 0)
        allowed = (segcol[at, 0:1] == segrow[0:1, :count]) & (key_pos <= query_pos)
        bias[:, :count] = jnp.where(allowed, 0.0, far_below)
        lsecol[...] = jnp.zeros_like(lsecol)

        def pair(hp, carry):
            lanes = pl.ds(pl.multiple_of(hp * 128, 128), 128)
            q_pair = q[at, lanes]
            k_pair = k[:count, lanes]
            v_pair = flat(v[:count // blk, :, lanes])
            total = None
            for i in range(2):
                scores = dot_nt(q_pair, jnp.where(keeps[i], k_pair, 0.0)) + bias[:, :count]
                top = jnp.max(scores, axis=1, keepdims=True)
                weights = jnp.exp(scores - top)
                norm = jnp.sum(weights, axis=1, keepdims=True)
                part = dot(weights.astype(BF), jnp.where(keeps[i], v_pair, 0.0)) * (1.0 / norm)
                total = part if total is None else total + part
                lsecol[...] = jnp.where(lane == 2 * hp + i, top + jnp.log(norm), lsecol[...])
            att[at, lanes] = total.astype(BF)
            return carry

        lax.fori_loop(0, pairs, pair, 0)
        lse[:, at] = lsecol[...].T[:lse.shape[0], :]

    def attention(bias, lsecol):
        for j in range(n_q):
            attend(j, bias, lsecol)

    pl.run_scoped(attention, pltpu.VMEM((QB, length), F4), pltpu.VMEM((QB, 128), F4))

    att_wire = net.wire(xs.at[0], xr.at[0], mate)

    def half_rows(h, i):
        return pl.ds(pl.multiple_of(h * half + i * QB, QB), QB)

    def out_proj(i, carry):
        part = dot(att[half_rows(cn, i), :], flat(wo[...]))
        xs[0, pl.ds(i * QB, QB), :] = part.astype(BF)
        return carry

    lax.fori_loop(0, per_half, out_proj, 0)
    att_wire.start()

    def out_proj_mine(i, carry):
        mine[pl.ds(i * QB, QB), :] = dot(att[half_rows(c, i), :], flat(wo[...]))
        return carry

    lax.fori_loop(0, per_half, out_proj_mine, 0)
    att_wire.arrived()

    n2_wires = []
    for i in range(rows):
        at = slice(i * blk, (i + 1) * blk)
        middle = x_own[i].astype(F4) + mine[at, :] + xr[0, at, :].astype(F4) + vecs[4:5, :]
        mid[at, :] = middle
        unit, _ = norm_stats(middle)
        n2[c, i] = (unit * vecs[2:3, :] + vecs[3:4, :]).astype(BF)
        wire = net.wire(n2.at[c, i], n2.at[c, i], mate)
        wire.start()
        n2_wires.append(wire)
    up_own.arrived()
    down_own.arrived()
    for relay in up_relay + down_relay:
        relay.two.arrived()

    hid = wup.shape[-1]
    back_wire = net.wire(xs.at[1], xr.at[1], mate)
    mlp_wire = net.wire(xs.at[2], xr.at[2], mate)
    out_wires = swap(out_s, out)
    gm_wires = [net.wire(gm.at[c, i], gm.at[c, i], mate) for i in range(rows)]
    order = tuple(range(1, rows)) + (0,)

    class Reduce:
        def __init__(self, grad, one, two, z, p, y_first):
            self.grad, self.p, self.y_first = grad, p, y_first
            self.got_one, self.got_two, self.z = one, two, None
            if y_first:
                self.one = net.wire(grad.at[p, :, yn], one.at[p], y_nbr)
                self.two = net.wire(grad.at[p, sn, y], two.at[p], x_nbr)
            else:
                self.one = net.wire(grad.at[p, sn], one.at[p], x_nbr)
                self.two = net.wire(grad.at[p, s, yn], two.at[p], y_nbr)
            if p:
                self.z = net.wire(grad.at[p, s, y], z.at[p], dev(s, y, c, ring(p)))

        def run(self, stage):
            grad, p = self.grad, self.p
            if stage == 1:
                self.one.arrived()
                if self.y_first:
                    grad[p, :, y] = add(grad[p, :, y], self.got_one[p])
                else:
                    grad[p, s] = add(grad[p, s], self.got_one[p])
                self.two.start()
            else:
                self.two.arrived()
                grad[p, s, y] = add(grad[p, s, y], self.got_two[p])
                if p:
                    self.z.start()

    def add(one, two):
        return (one.astype(F4) + two.astype(F4)).astype(BF)

    down_rs = [Reduce(gdown, down_r1, down_r2, down_r3, p, True) for p in range(rows)]
    up_rs = [Reduce(gup, up_r1, up_r2, up_r3, p, p < rows // 2) for p in range(rows)]

    class Small:
        def __init__(self, group):
            self.group = group
            self.here = 4 * s + 2 * y + c
            mine_at = small_p.at[group, self.here]
            self.plane = []
            for ds in range(2):
                for dy in range(2):
                    for dc in range(2):
                        if ds or dy or dc:
                            to = dev(lax.rem(s + ds, 2), lax.rem(y + dy, 2), lax.rem(c + dc, 2), t)
                            self.plane.append(net.wire(mine_at, mine_at, to))
            at_z = small_z.at[group, t]
            self.z = [net.wire(at_z, at_z, dev(s, y, c, ring(step))) for step in range(1, rows)]

        def run(self, stage):
            group = self.group
            if stage == 0:
                small_p[group, self.here] = small[group]
                for wire in self.plane:
                    wire.start()
            elif stage == 1:
                for wire in self.plane:
                    wire.arrived()
                total = small_p[group, 0]
                for i in range(1, 8):
                    total = total + small_p[group, i]
                small_z[group, t] = total
                for wire in self.z:
                    wire.start()
            else:
                for wire in self.z:
                    wire.arrived()
                f_small[8 * group:8 * group + 8, :] = (
                    (small_z[group, 0] + small_z[group, 1]) + (small_z[group, 2] + small_z[group, 3])
                )

    small_sums = [Small(0), Small(1)]
    gelu_scale = math.sqrt(2.0 / math.pi)

    def feed_forward(act, ghid, bup_sum, back_own):
        bup_sum[...] = jnp.zeros_like(bup_sum)

        def forward(h, i, keep):
            at = half_rows(h, i)
            n2_block = flat(n2[h, pl.ds(i * per_blk, per_blk)])
            mlp = None
            for p in range(rows):
                cols = slice(p * hid, (p + 1) * hid)
                z = dot(n2_block, flat(wup[p])) + bvec[p, 0:1, lanes_c]
                z2 = z * z
                th = jnp.tanh(gelu_scale * z * (1.0 + 0.044715 * z2))
                cdf = 0.5 * (1.0 + th)
                a = (z * cdf).astype(BF)
                slope = cdf + 0.5 * z * (1.0 - th * th) * (gelu_scale * (1.0 + 3 * 0.044715 * z2))
                act[at, cols] = a
                ghid[at, cols] = slope.astype(BF)
                part = dot(a, flat(wdown[p]))
                mlp = part if mlp is None else mlp + part
            to = pl.ds(pl.multiple_of(i * QB, QB), QB)
            if keep:
                mine[to, :] = mlp
            else:
                xs[2, to, :] = mlp.astype(BF)

        def backward(h, i, keep):
            at = half_rows(h, i)
            cot_block = flat(cot[h, pl.ds(i * per_blk, per_blk)])
            back = None
            for p in range(rows):
                cols = slice(p * hid, (p + 1) * hid)
                g = (dot_nt(cot_block, flat(wdown[p])) * ghid[at, cols].astype(F4)).astype(BF)
                ghid[at, cols] = g
                bup_sum[0:1, cols] += jnp.sum(g.astype(F4), axis=0, keepdims=True)
                part = dot_nt(g, flat(wup[p]))
                back = part if back is None else back + part
            to = pl.ds(pl.multiple_of(i * QB, QB), QB)
            if keep:
                back_own[to, :] = back
            else:
                xs[1, to, :] = back.astype(BF)

        def each(step, h, keep):
            def body(i, carry):
                step(h, i, keep)
                return carry

            lax.fori_loop(0, per_half, body, 0)

        each(forward, c, True)
        for wire in n2_wires:
            wire.arrived()
        each(forward, cn, False)
        mlp_wire.start()
        arrived_all(cot_wires)
        cot_mate.start()
        each(backward, c, True)
        mlp_wire.arrived()
        for i in range(rows):
            at = slice(i * blk, (i + 1) * blk)
            out_s[i] = (mid[at, :] + mine[at, :] + xr[2, at, :].astype(F4) + vecs[5:6, :]).astype(BF)
        start_all(out_wires)
        cot_mate.arrived()

        for p in order:
            got = dot_tn(act[:, p * hid:(p + 1) * hid], flat(cot[...]))
            gdown[p] = got.astype(BF).reshape(gdown.shape[1:])
            down_rs[p].one.start()
        each(backward, cn, False)
        back_wire.start()
        for p in order:
            for m in range(2):
                n2_part = flat(n2[:, :, :, m * (width // 2):(m + 1) * (width // 2)])
                got = dot_tn(n2_part, ghid[:, p * hid:(p + 1) * hid])
                gup[p, m] = got.astype(BF).reshape(gup.shape[2:])
            up_rs[p].one.start()
        small[...] = jnp.zeros_like(small)
        for p in range(rows):
            small[1, pl.ds(ring(p), 1), lanes_c] = bup_sum[0:1, p * hid:(p + 1) * hid]

        back_wire.arrived()
        sums = [jnp.zeros((1, width), F4) for _ in range(4)]
        for i in range(rows):
            at = slice(i * blk, (i + 1) * blk)
            middle = mid[at, :]
            unit, inverse = norm_stats(middle)
            back = back_own[at, :] + xr[1, at, :].astype(F4)
            cot_block = cot[c, i].astype(F4)
            g_middle = cot_block + norm_back(back, unit, inverse, vecs[2:3, :])
            mid[at, :] = g_middle
            g_low = g_middle.astype(BF)
            gm[c, i] = g_low
            gm_wires[i].start()
            for n, item in enumerate((back * unit, back, g_low.astype(F4), cot_block)):
                sums[n] += jnp.sum(item, axis=0, keepdims=True)
        for n in range(4):
            small[1, 4 + n:5 + n, :] = sums[n]
        small_sums[1].run(0)

    pl.run_scoped(
        feed_forward,
        pltpu.VMEM((length, rows * hid), BF),
        pltpu.VMEM((length, rows * hid), BF),
        pltpu.VMEM((8, rows * hid), F4),
        pltpu.VMEM((half, width), F4),
    )

    plane = ((x_nbr, sn, y), (y_nbr, s, yn), (diag, sn, yn))

    class Gather:
        def __init__(self, parts, grad, got, total, at_own, at_core):
            self.parts, self.grad, self.got, self.total = parts, grad, got, total
            self.keep = net.own(total, at_own)
            self.ag = [net.wire(total, at_own, to) for to, _, _ in plane]
            self.over = net.wire(at_core, at_core, mate)

        def run(self, stage):
            if stage == 0:
                for p in range(1, rows):
                    self.parts[p].z.arrived()
                total = self.grad[0, s, y].astype(F4)
                for p in range(1, rows):
                    total += self.got[p].astype(F4)
                self.total[...] = total.astype(BF)
                self.keep.start()
                for wire in self.ag:
                    wire.start()
            elif stage == 1:
                self.keep.arrived()
                for wire in self.ag:
                    wire.arrived()
                self.over.start()
            else:
                self.over.arrived()

    up_end = Gather(up_rs, gup, up_r3, f_s.at[0], f_up.at[s, y, :, lanes_c], f_up.at[:, :, :, lanes_c])
    down_end = Gather(down_rs, gdown, down_r3, f_t, f_down.at[c, s, y], f_down.at[c])

    back1_wire = net.wire(xs.at[0], xr.at[0], mate)
    gtok_wires = swap(out_s, gtok)
    gfirst_slot = net.recv_slots(rows)
    gfirst_wires = []
    for h in range(2):
        for step in range(rows):
            j = ring(step)
            to_me = (c == 1) & (s == h) & (s == 1) if step == 0 else None
            fine = (c == 1) & jnp.logical_not(to_me) if step == 0 else c == 1
            gfirst_wires.append(net.wire(
                gv_s.at[h * rows + j], gfirst.at[t], dev(h, y, s, j), fine, None, gfirst_slot + step,
            ))
    gfirst_own = net.own(gv_s.at[rows + t], gfirst.at[t], (c == 1) & (s == 1))
    class Heads:
        def __init__(self, first_one, count, x_first):
            self.part = part = pl.ds(first_one, count)
            self.x_first = x_first
            if x_first:
                self.one = net.wire(gwa.at[part, :, sn], wa_r1.at[part], x_nbr)
                self.two = net.wire(gwa.at[part, :, s, yn], wa_r2.at[part], y_nbr)
            else:
                self.one = net.wire(gwa.at[part, :, :, yn], wa_r1.at[part], y_nbr)
                self.two = net.wire(gwa.at[part, :, sn, y], wa_r2.at[part], x_nbr)
            self.rz = []
            for step in range(1, rows):
                to = ring(step)
                self.rz.append(net.wire(
                    gwa.at[part, lax.rem(to, 2), s, y], wa_r3.at[step, part], dev(s, y, c, to),
                    lax.div(to, 2) == c, home,
                ))
            self.keep = net.own(f_w.at[part], f_wa.at[part, s, y], home)
            self.ag = [net.wire(f_w.at[part], f_wa.at[part, s, y], to, home, home) for to, _, _ in plane]
            self.over = net.wire(f_wa.at[part], f_wa.at[part], mate, home, away)

        def run(self, stage):
            part = self.part
            if stage == 0:
                self.one.start()
            elif stage == 0.5:
                self.one.arrived()
                if self.x_first:
                    gwa[part, :, s] = add(gwa[part, :, s], wa_r1[part])
                else:
                    gwa[part, :, :, y] = add(gwa[part, :, :, y], wa_r1[part])
                self.two.start()
            elif stage == 1:
                self.two.arrived()
                gwa[part, :, s, y] = add(gwa[part, :, s, y], wa_r2[part])
                for wire in self.rz:
                    wire.start()
            elif stage == 2:
                @pl.when(home)
                def _():
                    for wire in self.rz:
                        wire.copy.wait_recv()
                    total = gwa[part, lax.rem(t, 2), s, y].astype(F4)
                    for i in range(1, rows):
                        total += wa_r3[i, part].astype(F4)
                    f_w[part] = total.astype(BF)

                self.keep.start()
                for wire in self.ag:
                    wire.start()
            elif stage == 3:
                self.keep.arrived()
                for wire in self.ag:
                    wire.arrived()
                self.over.start()
            else:
                self.over.arrived()

    heads_out, heads_q, heads_k = Heads(2, 1, False), Heads(0, 1, True), Heads(1, 1, False)
    lead, follow = c == 0, c == 1
    wv_rs = [net.wire(gwv.at[ds, dy], wv_r1.at[i], to, lead, lead) for i, (to, ds, dy) in enumerate(plane)]
    wv_rz = [
        net.wire(wv_r3.at[t], wv_r3.at[t], dev(s, y, c, ring(step)), lead, lead) for step in range(1, rows)
    ]
    wv_own_f = net.own(f_v, f_wv.at[s, y], lead)
    wv_ag = [net.wire(f_v, f_wv.at[s, y], to, lead, lead) for to, _, _ in plane]
    wv_over = net.wire(f_wv, f_wv, mate, lead, follow)

    def fresh_reduce(stage):
        if stage == 0:
            for wire in wv_rs:
                wire.start()
        elif stage == 1:
            @pl.when(lead)
            def _():
                for wire in wv_rs:
                    wire.copy.wait_recv()
                total = gwv[s, y].astype(F4)
                for i in range(3):
                    total += wv_r1[i].astype(F4)
                wv_r3[t] = total.astype(BF)

            for wire in wv_rz:
                wire.start()
        elif stage == 2:
            @pl.when(lead)
            def _():
                for wire in wv_rz:
                    wire.copy.wait_recv()
                parts = [wv_r3[i].astype(F4) for i in range(rows)]
                f_v[...] = ((parts[0] + parts[1]) + (parts[2] + parts[3])).astype(BF)

            wv_own_f.start()
            for wire in wv_ag:
                wire.start()
        elif stage == 3:
            wv_own_f.arrived()
            for wire in wv_ag:
                wire.arrived()
            wv_over.start()
        else:
            wv_over.arrived()

    heads_here = heads_width // HEAD_DIM
    pick_head = lax.broadcasted_iota(jnp.int32, (lse.shape[0], heads_width), 1) // HEAD_DIM
    pick = (pick_head == lax.broadcasted_iota(jnp.int32, pick_head.shape, 0)).astype(BF)

    def attention_back(gk, gv, delta, tmp, gq, kt, gqt, bias_t):
        kt[...] = k[...].T
        gk[...] = jnp.zeros_like(gk)
        gv[...] = jnp.zeros_like(gv)

        def grad_att(h, i):
            at = half_rows(h, i)
            block = flat(gm[h, pl.ds(i * per_blk, per_blk)])
            low = dot_nt(block, flat(wo[...])).astype(BF)
            gatt[at, :] = low
            product = low.astype(F4) * att[at, :].astype(F4)
            high = product.astype(BF)
            rest_of = (product - high.astype(F4)).astype(BF)
            delta[:, at] = dot_nt(pick, high) + dot_nt(pick, rest_of)

        def grad_att_mine(i, carry):
            grad_att(c, i)
            return carry

        def grad_att_mate(i, carry):
            grad_att(cn, i)
            return carry

        lax.fori_loop(0, per_half, grad_att_mine, 0)
        for wire in gm_wires:
            wire.arrived()
        lax.fori_loop(0, per_half, grad_att_mate, 0)
        gwa[2] = dot_tn(att[...], flat(gm[...])).astype(BF).reshape(gwa.shape[1:])
        heads_out.run(0)
        down_rs[1].run(1)
        down_rs[2].run(1)

        def back_block(j):
            count = (j + 1) * QB
            at = slice(j * QB, count)
            key_pos = lax.broadcasted_iota(jnp.int32, (count, QB), 0)
            query_pos = j * QB + lax.broadcasted_iota(jnp.int32, (count, QB), 1)
            allowed = (segcol[:count, 0:1] == segrow[0:1, at]) & (key_pos <= query_pos)
            bias_t[:count, :] = jnp.where(allowed, 0.0, far_below)

            def pair(hp, carry):
                lanes = pl.ds(pl.multiple_of(hp * 128, 128), 128)
                q_pair = q[at, lanes]
                k_pair = k[:count, lanes]
                v_pair = flat(v[:count // blk, :, lanes])
                ga_pair = gatt[at, lanes]
                sum_k = sum_v = None
                for i in range(2):
                    head = 2 * hp + i
                    scores = dot_nt(jnp.where(keeps[i], k_pair, 0.0), q_pair) + bias_t[:count, :]
                    probs = jnp.exp(scores - lse[pl.ds(head, 1), at])
                    grad_prob = dot_nt(jnp.where(keeps[i], v_pair, 0.0), ga_pair)
                    grad_score = (probs * (grad_prob - delta[pl.ds(head, 1), at])).astype(BF)
                    part_v = dot(probs.astype(BF), jnp.where(keeps[i], ga_pair, 0.0))
                    part_k = dot(grad_score, jnp.where(keeps[i], q_pair, 0.0))
                    sum_v = part_v if sum_v is None else sum_v + part_v
                    sum_k = part_k if sum_k is None else sum_k + part_k
                    channels = pl.ds(pl.multiple_of(hp * 128 + i * HEAD_DIM, HEAD_DIM), HEAD_DIM)
                    gqt[channels, at] = (dot(kt[channels, :count], grad_score) * factor).astype(BF)
                gk[:count, lanes] += sum_k
                gv[:count, lanes] += sum_v
                return carry

            lax.fori_loop(0, pairs, pair, 0)

        for j in range(n_q):
            back_block(j)
            if j == 1:
                down_rs[3].run(1)
                up_rs[2].run(1)
            if j == 2:
                down_rs[0].run(1)
                up_rs[3].run(1)
                down_rs[1].run(2)
                down_rs[2].run(2)
            if j == 3:
                up_rs[1].run(1)
                down_rs[3].run(2)
                up_rs[2].run(2)
                up_rs[3].run(2)

        gq[...] = gqt[...].T
        gk_low = gk[...].astype(BF)
        k[...] = gk_low
        gv_s[...] = gv[...].astype(BF).reshape(gv_s.shape)

        n1_all = flat(n1[...])
        gwa[0] = dot(gqt[...], n1_all).astype(BF).reshape(gwa.shape[1:])
        heads_q.run(0)
        gwa[1] = dot_tn(k[...], n1_all).astype(BF).reshape(gwa.shape[1:])
        heads_k.run(0)
        for wire in gfirst_wires:
            wire.start()
        gfirst_own.start()
        up_rs[0].run(1)
        down_rs[0].run(2)
        small[0, 7:8, lanes_h] = jnp.sum(gq[...].astype(F4), axis=0, keepdims=True)

        @pl.when(lead)
        def _():
            gv_low = flat(gv_s[...])
            gwv[...] = dot_tn(gv_low, n1_all).astype(BF).reshape(gwv.shape)
            small[0, 6:7, :heads_width] = jnp.sum(gv_low.astype(F4), axis=0, keepdims=True)

        fresh_reduce(0)
        heads_out.run(0.5)
        small_sums[1].run(1)

        def back_rows(h, i):
            at = half_rows(h, i)
            tmp[...] = dot(gq[at, :], flat(wq[...])) + dot(k[at, :], flat(wk[...]))

            @pl.when(lead)
            def _():
                block = flat(gv_s[pl.ds(h * rows + i * per_blk, per_blk)])
                tmp[...] += dot_nt(block, wval[...])

        def back_mate(i, carry):
            back_rows(cn, i)
            xs[0, pl.ds(pl.multiple_of(i * QB, QB), QB), :] = tmp[...].astype(BF)
            return carry

        def back_mine(i, carry):
            back_rows(c, i)
            mine[pl.ds(pl.multiple_of(i * QB, QB), QB), :] = tmp[...]
            return carry

        net.done(att_wire)
        lax.fori_loop(0, per_half, back_mate, 0)
        back1_wire.start()
        lax.fori_loop(0, per_half, back_mine, 0)
        up_rs[1].run(2)

    lanes_h = pl.ds(pl.multiple_of(c * heads_width, 128), heads_width)
    pl.run_scoped(
        attention_back,
        pltpu.VMEM((length, heads_width), F4),
        pltpu.VMEM((length, heads_width), F4),
        pltpu.VMEM((lse.shape[0], length), F4),
        pltpu.VMEM((QB, width), F4),
        pltpu.VMEM((length, heads_width), BF),
        pltpu.VMEM((heads_width, length), BF),
        pltpu.VMEM((heads_width, length), BF),
        pltpu.VMEM((length, QB), F4),
    )

    back1_wire.arrived()
    for group in out_wires:
        net.done(group[0])
    out_wires[0][1].arrived()
    gain_sum = jnp.zeros((1, width), F4)
    bias_sum = jnp.zeros((1, width), F4)
    for i in range(rows):
        at = slice(i * blk, (i + 1) * blk)
        unit, inverse = norm_stats(x_own[i].astype(F4))
        back = mine[at, :] + xr[0, at, :].astype(F4)
        gain_sum += jnp.sum(back * unit, axis=0, keepdims=True)
        bias_sum += jnp.sum(back, axis=0, keepdims=True)
        out_s[i] = (mid[at, :] + norm_back(back, unit, inverse, vecs[0:1, :])).astype(BF)
    small[0, 0:1, :] = gain_sum
    small[0, 1:2, :] = bias_sum
    start_all(gtok_wires)
    small_sums[0].run(0)

    heads_out.run(1)
    up_rs[0].run(2)
    down_end.run(0)
    heads_q.run(0.5)
    heads_k.run(0.5)
    fresh_reduce(1)
    small_sums[0].run(1)
    heads_q.run(1)
    heads_k.run(1)
    heads_out.run(2)
    up_end.run(0)
    down_end.run(1)
    fresh_reduce(2)
    heads_q.run(2)
    heads_k.run(2)
    heads_out.run(3)
    up_end.run(1)
    fresh_reduce(3)
    heads_q.run(3)
    heads_k.run(3)
    small_sums[1].run(2)
    small_sums[0].run(2)
    down_end.run(2)
    up_end.run(2)
    heads_out.run(4)
    heads_q.run(4)
    heads_k.run(4)
    fresh_reduce(4)
    for group in out_wires:
        group[0].arrived()
    arrived_all(gtok_wires)
    for step in range(rows):
        def take(step=step):
            pltpu.make_async_remote_copy(
                src_ref=gv_s.at[0], dst_ref=gfirst.at[0], send_sem=send_sems.at[0],
                recv_sem=recv_sems.at[gfirst_slot + step], device_id=mate, device_id_type=MESH,
            ).wait_recv()
        if step == 0:
            pl.when((c == 0) | (s == 0))(take)
        else:
            take()
    gfirst_own.arrived()
    for wire in net.all:
        wire.sent()


def whole_layer(
    tokens, first_values, segment_ids, cotangent, norm1_gain, norm1_bias, w_query, b_query, w_key,
    w_value, b_value, w_out, b_out, norm2_gain, norm2_bias, w_up, b_up, w_down, b_down,
):
    rows, blk, width = tokens.shape
    half = rows * blk
    length = 2 * half
    valf = w_value.shape[1]
    tp_width = w_query.shape[1]
    hid = w_up.shape[1] // 2
    t = lax.axis_index("tp")
    wa_in = jnp.stack([w_query.T, w_key.T, w_out]).reshape(3, 2, 2, tp_width // 4, width)
    odd = lax.rem(t, 2) == 1
    b_q = jnp.where(odd, jnp.pad(b_query, (tp_width, width - 2 * tp_width)), jnp.pad(b_query, (0, width - tp_width)))
    bvec = jnp.concatenate([b_up[None], b_q[None], jnp.zeros((6, width), F4)])
    vecs = jnp.stack([
        norm1_gain, norm1_bias, norm2_gain, norm2_bias, b_out, b_down,
        jnp.pad(b_value, (0, width - valf)), jnp.zeros((width,), F4),
    ])
    hbm = pl.BlockSpec(memory_space=pl.ANY)
    vmem = pl.BlockSpec(memory_space=pltpu.VMEM)
    piece = tp_width // 4
    up_rows, down_rows = width // 4, hid // 4

    def of(*shape, dtype=BF):
        return jax.ShapeDtypeStruct(shape, dtype)

    def room(*shape, dtype=BF):
        return pltpu.VMEM(shape, dtype)

    outs = (
        of(rows, blk, width), of(rows, blk, width), of(rows, blk, valf),
        of(2, 2, up_rows, 2 * hid), of(2, 2, 2, down_rows, width),
        of(3, 2, 2, piece, width), of(2, 2, valf // 4, width), of(16, width, dtype=F4),
    )
    scratch = [
        room(rows, blk, width), room(2, rows, blk, width), room(2, 8, length, dtype=jnp.int32),
        room(8, length, dtype=F4), room(length, 128, dtype=F4), room(rows, 8, width, dtype=F4),
        room(3, 2, 2, 2, piece, width), room(width, valf),
        room(rows, 2, 2, up_rows, hid), room(rows, 2, 2, down_rows, width),
        room(length, 2 * tp_width), room(length, 2 * tp_width), room(2 * rows, blk, valf),
        room(length, 2 * tp_width), room(16, length, dtype=F4),
        room(half, width, dtype=F4), room(2, rows, blk, width), room(2, rows, blk, width),
        room(half, width, dtype=F4), room(3, half, width), room(3, half, width),
        room(rows, blk, width), room(2, rows, blk, width),
        room(length, 2 * tp_width), room(2 * rows, blk, valf),
        room(rows, 2, 2, up_rows, hid), room(rows, 2, 2, down_rows, width),
        room(rows, 2, up_rows, hid), room(rows, up_rows, hid), room(rows, up_rows, hid),
        room(rows, 2, down_rows, width), room(rows, down_rows, width), room(rows, down_rows, width),
        room(3, 2, 2, 2, piece, width), room(3, 2, 2, piece, width), room(3, 2, piece, width), room(rows, 3, piece, width),
        room(2, 2, valf // 4, width), room(3, valf // 4, width), room(rows, valf // 4, width),
        room(2, 8, width, dtype=F4), room(2, 8, 8, width, dtype=F4), room(2, rows, 8, width, dtype=F4),
        room(1, up_rows, hid), room(down_rows, width), room(3, piece, width), room(valf // 4, width),
        pltpu.SemaphoreType.DMA((SENDS,)), pltpu.SemaphoreType.DMA((RECVS,)), pltpu.SemaphoreType.DMA((OWNS,)),
    ]
    out, gtok, gfirst, f_up, f_down, f_wa, f_wv, f_small = pl.pallas_call(
        layer_kernel,
        out_shape=outs,
        in_specs=[hbm, hbm, hbm, vmem, hbm, hbm, hbm, hbm, vmem, vmem],
        out_specs=(hbm,) * 7 + (vmem,),
        scratch_shapes=scratch,
        compiler_params=pltpu.CompilerParams(
            collective_id=0, has_side_effects=True, vmem_limit_bytes=VMEM_BYTES
        ),
    )(
        tokens, first_values, cotangent, segment_ids, wa_in,
        w_up.reshape(2, 2, up_rows, 2 * hid), w_down.reshape(2, 2, 2, down_rows, width), w_value, bvec, vecs,
    )
    wa_flat = f_wa.reshape(3, tp_width, width).astype(F4)
    grad_b_query = lax.dynamic_slice(f_small, (7, t * tp_width), (1, tp_width))[0]
    grad_b_up = lax.dynamic_slice(f_small, (8 + t, 0), (1, width))[0]
    return (
        out,
        gtok.astype(F4),
        gfirst,
        f_small[0],
        f_small[1],
        wa_flat[0].T,
        grad_b_query,
        wa_flat[1].T,
        f_wv.reshape(valf, width).astype(F4).T,
        f_small[6, :valf],
        wa_flat[2],
        f_small[14],
        f_small[12],
        f_small[13],
        f_up.reshape(width, 2 * hid).astype(F4),
        grad_b_up,
        f_down.reshape(2 * hid, width).astype(F4),
        f_small[15],
    )


SENDS = 176
RECVS = 176
OWNS = 16
VMEM_BYTES = 63 * 1024 * 1024


def fits(mesh):
    return mesh.shape["seq"] == 2 and mesh.shape["batch"] == 4 and mesh.shape["tp"] == 4


def solution(mesh):
    placed = (
        P("batch", ("seq", "tp"), None),
        P("batch", ("seq", "tp"), None),
        P("batch", None),
        P("batch", ("seq", "tp"), None),
        P(),
        P(),
        P(None, "tp"),
        P("tp"),
        P(None, "tp"),
        P(),
        P(),
        P("tp", None),
        P(),
        P(),
        P(),
        P(None, "tp"),
        P("tp"),
        P("tp", None),
        P(),
    )
    return jax.shard_map(
        whole_layer if fits(mesh) else on_device,
        mesh=mesh,
        in_specs=placed,
        out_specs=(
            P("batch", ("seq", "tp"), None),
            P("batch", ("seq", "tp"), None),
            P("batch", ("seq", "tp"), None),
            P(),
            P(),
            P(None, "tp"),
            P("tp"),
            P(None, "tp"),
            P(),
            P(),
            P("tp", None),
            P(),
            P(),
            P(),
            P(None, "tp"),
            P("tp"),
            P("tp", None),
            P(),
        ),
        check_vma=False,
    )
```

```python
import math

import jax
import jax.numpy as jnp
from jax import lax
from jax.experimental import pallas as pl
from jax.experimental.pallas import tpu as pltpu
from jax.sharding import PartitionSpec as P

HEADS = 12
HEAD_DIM = 64


eps = 1e-05
block_cap = 256
far_below = -1e30


def from_behind(block, axis, distance):
    devices = range(lax.axis_size(axis))
    route = [((i - distance) % len(devices), i) for i in devices]
    return lax.ppermute(block, axis, route)


def layer_norm(values, norm_gain, norm_bias):
    average = jnp.mean(values, axis=-1, keepdims=True)
    centered = values - average
    inverse = lax.rsqrt(jnp.mean(centered * centered, axis=-1, keepdims=True) + eps)
    unit = centered * inverse
    return (unit * norm_gain + norm_bias, unit, inverse)


def norm_back(grad_result, unit, inverse, norm_gain):
    scaled = grad_result * norm_gain
    return inverse * (
        scaled
        - jnp.mean(scaled, axis=-1, keepdims=True)
        - unit * jnp.mean(scaled * unit, axis=-1, keepdims=True)
    )


def project(values, weight):
    return jnp.einsum("rtd,de->rte", values, weight, preferred_element_type=jnp.float32)


def project_back(grads, weight):
    return jnp.einsum("rte,de->rtd", grads, weight, preferred_element_type=jnp.float32)


def weight_grad(values, grads):
    return jnp.einsum("rtd,rte->de", values, grads, preferred_element_type=jnp.float32)


def column_sum(values):
    return jnp.sum(values, axis=(0, 1), dtype=jnp.float32)


def gelu_tanh(values):
    return jax.nn.gelu(values, approximate=True)


def over_key_blocks(arrays, key_first, state, step, limit):
    count = arrays[0].shape[1]
    width = math.gcd(count, block_cap)

    def one(index, carry):
        offset = index * width
        parts = tuple((lax.dynamic_slice_in_dim(item, offset, width, 1) for item in arrays))
        first_key = key_first + offset

        def taken(inner):
            return step(inner, parts, first_key, offset)

        def skipped(inner):
            return inner

        return lax.cond(first_key <= limit, taken, skipped, carry)

    return lax.fori_loop(0, count // width, one, state)


def on_device(
    tokens,
    first_values,
    segment_ids,
    cotangent,
    norm1_gain,
    norm1_bias,
    w_query,
    b_query,
    w_key,
    w_value,
    b_value,
    w_out,
    b_out,
    norm2_gain,
    norm2_bias,
    w_up,
    b_up,
    w_down,
    b_down,
):
    rows = tokens.shape[0]
    model_width = tokens.shape[2]
    tp_count = lax.axis_size("tp")
    seq_count = lax.axis_size("seq")
    local_len = tokens.shape[1] * tp_count
    heads = w_query.shape[1] // HEAD_DIM
    width_tp = heads * HEAD_DIM
    valf_all = w_value.shape[1]
    factor = HEAD_DIM ** (-0.5)
    seq_index = lax.axis_index("seq")
    head_first = lax.axis_index("tp") * heads
    is_fresh = head_first < HEADS // 2
    fresh_col = jnp.minimum(head_first * HEAD_DIM, valf_all - width_tp)
    reuse_col = jnp.maximum(head_first * HEAD_DIM - valf_all, 0)
    own_first = seq_index * local_len
    own_last = own_first + local_len - 1
    own_pos = own_first + jnp.arange(local_len, dtype=jnp.int32)
    own_seg = lax.dynamic_slice_in_dim(segment_ids, own_first, local_len, 1)

    def masked_scores(query4, key_part, query_pos, query_seg, key_first):
        width = key_part.shape[1]
        scores = (
            jnp.einsum("rqhc,rkhc->rhqk", query4, key_part, preferred_element_type=jnp.float32)
            * factor
        )
        key_seg = lax.dynamic_slice_in_dim(segment_ids, key_first, width, 1)
        key_pos = key_first + jnp.arange(width, dtype=jnp.int32)
        allowed = (query_seg[:, :, None] == key_seg[:, None, :]) & (
            key_pos[None, None, :] <= query_pos[None, :, None]
        )
        return (scores, allowed[:, None])

    resid = tokens.astype(jnp.float32)
    normed_one, unit_one, inverse_one = layer_norm(resid, norm1_gain, norm1_bias)
    rows_one, grad_rows, first_rows = (
        lax.all_gather(normed_one.astype(jnp.bfloat16), "tp", axis=1, tiled=True),
        lax.all_gather(cotangent, "tp", axis=1, tiled=True),
        lax.all_gather(first_values, "tp", axis=1, tiled=True),
    )
    query4 = (
        (project(rows_one, w_query) + b_query)
        .astype(jnp.bfloat16)
        .reshape(rows, local_len, heads, HEAD_DIM)
    )
    keys4 = project(rows_one, w_key).astype(jnp.bfloat16).reshape(rows, local_len, heads, HEAD_DIM)
    w_part = lax.dynamic_slice_in_dim(w_value, fresh_col, width_tp, 1)
    b_part = lax.dynamic_slice_in_dim(b_value, fresh_col, width_tp, 0)

    def fresh_side(normed_rows):
        return (project(normed_rows, w_part) + b_part).astype(jnp.bfloat16)

    def reuse_side(normed_rows):
        return lax.dynamic_slice_in_dim(first_rows, reuse_col, width_tp, 2)

    vals4 = lax.cond(is_fresh, fresh_side, reuse_side, rows_one).reshape(
        rows, local_len, heads, HEAD_DIM
    )

    def stats_step(carry, parts, key_first, offset):
        top, total = carry
        scores, allowed = masked_scores(query4, parts[0], own_pos, own_seg, key_first)
        masked = jnp.where(allowed, scores, far_below)
        new_top = jnp.maximum(top, jnp.max(masked, axis=3))
        weights = jnp.where(allowed, jnp.exp(masked - new_top[..., None]), 0.0)
        return (new_top, total * jnp.exp(top - new_top) + jnp.sum(weights, axis=3))

    start_top = jnp.full((rows, heads, local_len), far_below, jnp.float32)
    start_total = jnp.zeros((rows, heads, local_len), jnp.float32)
    top, total = over_key_blocks(
        (lax.all_gather(keys4, "seq", axis=1, tiled=True),),
        jnp.int32(0),
        (start_top, start_total),
        stats_step,
        own_last,
    )
    lse = top + jnp.log(total)

    def value_step(acc, parts, key_first, offset):
        scores, allowed = masked_scores(query4, parts[0], own_pos, own_seg, key_first)
        weights = jnp.where(allowed, jnp.exp(scores - lse[..., None]), 0.0).astype(jnp.bfloat16)
        return acc + jnp.einsum(
            "rhqk,rkhc->rqhc", weights, parts[1], preferred_element_type=jnp.float32
        )

    zeros_q = jnp.zeros((rows, local_len, heads, HEAD_DIM), jnp.float32)
    attended = over_key_blocks(
        (
            lax.all_gather(keys4, "seq", axis=1, tiled=True),
            lax.all_gather(vals4, "seq", axis=1, tiled=True),
        ),
        jnp.int32(0),
        zeros_q,
        value_step,
        own_last,
    )
    attended_low = attended.astype(jnp.bfloat16).reshape(rows, local_len, width_tp)
    attn_share = lax.psum_scatter(
        project(attended_low, w_out).astype(jnp.bfloat16), "tp", scatter_dimension=1, tiled=True
    ).astype(jnp.float32)
    middle = resid + attn_share + b_out
    normed_two, unit_two, inverse_two = layer_norm(middle, norm2_gain, norm2_bias)
    rows_two = lax.all_gather(normed_two.astype(jnp.bfloat16), "tp", axis=1, tiled=True)
    hidden_pre = project(rows_two, w_up) + b_up
    activated_full, gelu_pull = jax.vjp(gelu_tanh, hidden_pre)
    activated = activated_full.astype(jnp.bfloat16)
    mlp_share = lax.psum_scatter(
        project(activated, w_down).astype(jnp.bfloat16), "tp", scatter_dimension=1, tiled=True
    ).astype(jnp.float32)
    output = (middle + mlp_share + b_down).astype(jnp.bfloat16)
    grad_b_down = column_sum(grad_rows)
    grad_w_down = weight_grad(activated, grad_rows)
    grad_hidden = gelu_pull(project_back(grad_rows, w_down))[0].astype(jnp.bfloat16)
    grad_b_up = column_sum(grad_hidden)
    grad_w_up = weight_grad(rows_two, grad_hidden)
    back_two = lax.psum_scatter(
        project_back(grad_hidden, w_up).astype(jnp.bfloat16), "tp", scatter_dimension=1, tiled=True
    ).astype(jnp.float32)
    grad_gain_two = jnp.sum(back_two * unit_two, axis=(0, 1))
    grad_bias_two = jnp.sum(back_two, axis=(0, 1))
    grad_middle = cotangent.astype(jnp.float32) + norm_back(
        back_two, unit_two, inverse_two, norm2_gain
    )
    grad_mid_rows = lax.all_gather(grad_middle.astype(jnp.bfloat16), "tp", axis=1, tiled=True)
    grad_b_out = column_sum(grad_mid_rows)
    grad_w_out = weight_grad(attended_low, grad_mid_rows)
    grad_out4 = (
        project_back(grad_mid_rows, w_out)
        .astype(jnp.bfloat16)
        .reshape(rows, local_len, heads, HEAD_DIM)
    )
    delta = jnp.einsum("rqhc,rqhc->rhq", grad_out4.astype(jnp.float32), attended)

    def pair_terms(key_side, val_side, key_first, grad_query, grad_keys, grad_vals):

        def pair_step(carry, parts, first, offset):
            acc_query, acc_keys, acc_vals = carry
            key_part, val_part = parts
            width = key_part.shape[1]
            scores, allowed = masked_scores(query4, key_part, own_pos, own_seg, first)
            probs = jnp.where(allowed, jnp.exp(scores - lse[..., None]), 0.0)
            grad_val = jnp.einsum(
                "rhqk,rqhc->rkhc",
                probs.astype(jnp.bfloat16),
                grad_out4,
                preferred_element_type=jnp.float32,
            )
            grad_prob = jnp.einsum(
                "rqhc,rkhc->rhqk", grad_out4, val_part, preferred_element_type=jnp.float32
            )
            grad_score = (probs * (grad_prob - delta[..., None])).astype(jnp.bfloat16)
            acc_query = (
                acc_query
                + jnp.einsum(
                    "rhqk,rkhc->rqhc", grad_score, key_part, preferred_element_type=jnp.float32
                )
                * factor
            )
            grad_key = (
                jnp.einsum(
                    "rhqk,rqhc->rkhc", grad_score, query4, preferred_element_type=jnp.float32
                )
                * factor
            )
            acc_keys = lax.dynamic_update_slice_in_dim(
                acc_keys, lax.dynamic_slice_in_dim(acc_keys, offset, width, 1) + grad_key, offset, 1
            )
            acc_vals = lax.dynamic_update_slice_in_dim(
                acc_vals, lax.dynamic_slice_in_dim(acc_vals, offset, width, 1) + grad_val, offset, 1
            )
            return (acc_query, acc_keys, acc_vals)

        return over_key_blocks(
            (key_side, val_side), key_first, (grad_query, grad_keys, grad_vals), pair_step, own_last
        )

    def turn_keys(turn, carry):
        moving_keys, moving_vals, moving_gk, moving_gv, grad_query = carry
        anchor = (seq_index - turn) % seq_count
        grad_query, moving_gk, moving_gv = pair_terms(
            moving_keys, moving_vals, anchor * local_len, grad_query, moving_gk, moving_gv
        )
        moving_keys, moving_vals, moving_gk, moving_gv = (
            from_behind(moving_keys, "seq", 1),
            from_behind(moving_vals, "seq", 1),
            from_behind(moving_gk.astype(jnp.bfloat16), "seq", 1).astype(moving_gk.dtype),
            from_behind(moving_gv.astype(jnp.bfloat16), "seq", 1).astype(moving_gv.dtype),
        )
        return (moving_keys, moving_vals, moving_gk, moving_gv, grad_query)

    start_state = (keys4, vals4, zeros_q, zeros_q, zeros_q)
    final_state = lax.fori_loop(0, seq_count, turn_keys, start_state)
    grad_keys4, grad_vals4, grad_query4 = (final_state[2], final_state[3], final_state[4])
    grad_query = grad_query4.astype(jnp.bfloat16).reshape(rows, local_len, width_tp)
    grad_keys = grad_keys4.astype(jnp.bfloat16).reshape(rows, local_len, width_tp)
    grad_vals = grad_vals4.astype(jnp.bfloat16).reshape(rows, local_len, width_tp)

    def fresh_back(grad_flat):
        gw_full = lax.dynamic_update_slice_in_dim(
            jnp.zeros((model_width, valf_all), jnp.float32),
            weight_grad(rows_one, grad_flat),
            fresh_col,
            1,
        )
        gb_full = lax.dynamic_update_slice_in_dim(
            jnp.zeros((valf_all,), jnp.float32), column_sum(grad_flat), fresh_col, 0
        )
        back_value = project_back(grad_flat, w_part)
        reuse_full = jnp.zeros((rows, local_len, valf_all), jnp.float32)
        return (gw_full, gb_full, back_value, reuse_full)

    def reuse_back(grad_flat):
        gw_full = jnp.zeros((model_width, valf_all), jnp.float32)
        gb_full = jnp.zeros((valf_all,), jnp.float32)
        back_value = jnp.zeros((rows, local_len, model_width), jnp.float32)
        reuse_full = lax.dynamic_update_slice_in_dim(
            jnp.zeros((rows, local_len, valf_all), jnp.float32),
            grad_flat.astype(jnp.float32),
            reuse_col,
            2,
        )
        return (gw_full, gb_full, back_value, reuse_full)

    grad_w_value, grad_b_value, back_value, reuse_full = lax.cond(
        is_fresh, fresh_back, reuse_back, grad_vals
    )
    grad_b_query = column_sum(grad_query)
    grad_w_query = weight_grad(rows_one, grad_query)
    grad_w_key = weight_grad(rows_one, grad_keys)
    back_terms = project_back(grad_query, w_query) + project_back(grad_keys, w_key) + back_value
    back_one, reuse_sum = (
        lax.psum_scatter(
            back_terms.astype(jnp.bfloat16), "tp", scatter_dimension=1, tiled=True
        ).astype(jnp.float32),
        lax.psum_scatter(
            reuse_full.astype(jnp.bfloat16), "tp", scatter_dimension=1, tiled=True
        ).astype(jnp.float32),
    )
    grad_first_values = reuse_sum.astype(jnp.bfloat16)
    grad_gain_one = jnp.sum(back_one * unit_one, axis=(0, 1))
    grad_bias_one = jnp.sum(back_one, axis=(0, 1))
    grad_tokens = grad_middle + norm_back(back_one, unit_one, inverse_one, norm1_gain)
    summed = lax.psum(
        (
            grad_w_query,
            grad_w_key,
            grad_w_out,
            grad_w_up,
            grad_w_down,
            grad_b_query,
            grad_b_out,
            grad_b_up,
            grad_b_down,
        ),
        ("seq", "batch"),
    )
    norm_sums = lax.psum(
        (grad_gain_one, grad_bias_one, grad_gain_two, grad_bias_two, grad_w_value, grad_b_value),
        ("seq", "batch", "tp"),
    )
    return (
        output,
        grad_tokens,
        grad_first_values,
        norm_sums[0],
        norm_sums[1],
        summed[0],
        summed[5],
        summed[1],
        norm_sums[4],
        norm_sums[5],
        summed[2],
        summed[6],
        norm_sums[2],
        norm_sums[3],
        summed[3],
        summed[7],
        summed[4],
        summed[8],
    )


BF = jnp.bfloat16
F4 = jnp.float32
MESH = pl.DeviceIdType.MESH
QB = 256


def dot(a, b):
    return lax.dot_general(a, b, (((1,), (0,)), ((), ())), preferred_element_type=F4)


def dot_nt(a, b):
    return lax.dot_general(a, b, (((1,), (1,)), ((), ())), preferred_element_type=F4)


def dot_tn(a, b):
    return lax.dot_general(a, b, (((0,), (0,)), ((), ())), preferred_element_type=F4)


def maybe(cond, act):
    if cond is None:
        act()
    else:
        pl.when(cond)(act)


class Wire:
    def __init__(self, copy, send_if=None, recv_if=None):
        self.copy, self.send_if, self.recv_if = copy, send_if, recv_if

    def start(self):
        maybe(self.send_if, self.copy.start)

    def arrived(self):
        maybe(self.recv_if, self.copy.wait_recv)

    def sent(self):
        maybe(self.send_if, self.copy.wait_send)


class Own:
    def __init__(self, copy, when=None):
        self.copy, self.when = copy, when

    def start(self):
        maybe(self.when, self.copy.start)

    def arrived(self):
        maybe(self.when, self.copy.wait)

    def sent(self):
        pass


class Net:
    def __init__(self, send_sems, recv_sems, own_sems):
        self.send_sems, self.recv_sems, self.own_sems = send_sems, recv_sems, own_sems
        self.n_send = self.n_recv = self.n_own = 0
        self.all = []

    def recv_slots(self, count):
        self.n_recv += count
        return self.n_recv - count

    def wire(self, src, dst, device, send_if=None, recv_if=None, slot=None):
        if slot is None:
            slot = self.recv_slots(1)
        copy = pltpu.make_async_remote_copy(
            src_ref=src,
            dst_ref=dst,
            send_sem=self.send_sems.at[self.n_send],
            recv_sem=self.recv_sems.at[slot],
            device_id=device,
            device_id_type=MESH,
        )
        self.n_send += 1
        made = Wire(copy, send_if, recv_if)
        self.all.append(made)
        return made

    def done(self, wire):
        wire.sent()
        self.all = [item for item in self.all if item is not wire]

    def own(self, src, dst, when=None):
        copy = pltpu.make_async_copy(src, dst, self.own_sems.at[self.n_own])
        self.n_own += 1
        return Own(copy, when)


def norm_stats(values):
    average = jnp.mean(values, axis=-1, keepdims=True)
    centered = values - average
    inverse = lax.rsqrt(jnp.mean(centered * centered, axis=-1, keepdims=True) + eps)
    return centered * inverse, inverse


def layer_kernel(
    tokens, first, cot_in, seg, wq_in, wk_in, wo_in, wup_in, wdown_in, wval_in,
    gain1, bias1, gain2, bias2, b_out, b_down, b_value, b_query, b_up,
    out, gtok, gfirst, f_up, f_down, f_wa, f_wv, f_small,
    x_own, n1, segint, segrow, segcol, vecs, bvec, wa, wval, wup, wdown,
    q, k, v, att, lse, mid, n2, cot,
    mine, xs, xr, out_s, gm, gatt, gv_s,
    gup, gdown, up_r1, up_r2, up_r3, down_r1, down_r2, down_r3,
    gwa, wa_r1, wa_r2, wa_r3, gwv, wv_r1, wv_r3,
    small, small_p, small_z, f_s, f_t, f_w, f_v,
    send_sems, recv_sems, own_sems,
):
    s, b, t = lax.axis_index("seq"), lax.axis_index("batch"), lax.axis_index("tp")
    y, c = lax.div(b, 2), lax.rem(b, 2)
    sn, yn, cn = 1 - s, 1 - y, 1 - c
    rows, blk, width = tokens.shape
    half = rows * blk
    length = 2 * half
    net = Net(send_sems, recv_sems, own_sems)

    def dev(ds, dy, dc, dt):
        return (ds, 2 * dy + dc, dt)

    def ring(step):
        return lax.rem(t + step + rows, rows)

    x_nbr, y_nbr, diag, mate = dev(sn, y, c, t), dev(s, yn, c, t), dev(sn, yn, c, t), dev(s, y, cn, t)
    home = lax.div(t, 2) == c
    away = lax.div(t, 2) != c
    same, other = s == c, s != c

    wa_own = [net.own(src, wa.at[i, lax.rem(t, 2)], home) for i, src in enumerate((wq_in, wk_in, wo_in))]
    for own in wa_own:
        own.start()

    gate = pltpu.get_barrier_semaphore()
    peers = [(ds, 2 * yn + dc, t) for ds in range(2) for dc in range(2)]
    for ds in range(2):
        for dc in range(2):
            for dt in range(rows):
                if ds or dc or dt:
                    peers.append((lax.rem(s + ds, 2), 2 * y + lax.rem(c + dc, 2), lax.rem(t + dt, rows)))
    for peer in peers:
        pl.semaphore_signal(gate, inc=1, device_id=peer, device_id_type=MESH)
    pl.semaphore_wait(gate, len(peers))

    def swap(src, dst):
        wires = []
        for step in range(rows):
            r = ring(step)
            if step == 0:
                wires.append((
                    net.wire(src.at[r], dst.at[t], dev(c, y, s, r), other, other),
                    net.own(src.at[r], dst.at[t], same),
                ))
            else:
                wires.append((net.wire(src.at[r], dst.at[t], dev(c, y, s, r)),))
        return wires

    def start_all(wires):
        for group in wires:
            for wire in group:
                wire.start()

    def sent_all(wires):
        for wire in wires:
            net.done(wire)

    def arrived_all(wires):
        for group in wires:
            for wire in group:
                wire.arrived()

    seg_wire = net.wire(segint.at[0], segint.at[1], mate)
    bvec_wires = []
    for step in range(1, rows):
        bvec_wires.append(net.wire(bvec.at[0], bvec.at[step], dev(s, y, c, ring(-step))))
    token_wires = swap(tokens, x_own)
    wval_own = net.own(wval_in, wval, c == 0)
    lanes_c = pl.ds(pl.multiple_of(c * (wup.shape[-1]), 128), wup.shape[-1])
    up_own = net.own(wup_in.at[:, :, :, lanes_c], wup.at[0])
    down_own = net.own(wdown_in.at[c], wdown.at[0])

    first_slot = net.recv_slots(2 * rows)
    first_wires = []
    for step in range(rows):
        r = ring(step)
        to = net.wire(
            first.at[r], v.at[s * rows + t], dev(c, y, 1, r),
            (c == 0) | (s == 0) if step == 0 else None, None, first_slot + s * rows + step,
        )
        first_wires.append(to)
    first_own = net.own(first.at[t], v.at[s * rows + t], (c == 1) & (s == 1))

    def first_arrived():
        for source in range(2):
            for step in range(rows):
                def take(source=source, step=step):
                    pltpu.make_async_remote_copy(
                        src_ref=first.at[0], dst_ref=v.at[0], send_sem=send_sems.at[0],
                        recv_sem=recv_sems.at[first_slot + source * rows + step],
                        device_id=mate, device_id_type=MESH,
                    ).wait_recv()
                if source == 1 and step == 0:
                    pl.when(s == 0)(take)
                else:
                    take()
        first_own.arrived()

    def along(own_piece, at_slot, only=None):
        rounds = []
        for r in range(1, rows):
            pair = []
            for right in (True, False):
                source = t - (r - 1) if right else t + (r - 1)
                came = t - r if right else t + r
                inside = (source >= 0) & (t < rows - 1) if right else (source < rows) & (t > 0)
                comes = came >= 0 if right else came < rows
                if only is not None:
                    inside, comes = inside & only(source), comes & only(came)
                held = (rows - r + 1 if right else r - 1) % rows
                lands = rows - r if right else r
                src = own_piece if r == 1 else at_slot(source, held)
                to = dev(s, y, c, jnp.minimum(t + 1, rows - 1) if right else jnp.maximum(t - 1, 0))
                pair.append(net.wire(src, at_slot(source, lands), to, inside, comes))
            rounds.append(pair)
        return rounds

    def heads_slot(source, step):
        return wa.at[:, lax.rem(source + rows, 2), s, y]

    wa_z = along(wa.at[:, lax.rem(t, 2), s, y], heads_slot, lambda source: lax.div(source, 2) == c)
    up_z = along(wup_in.at[s, y, :, lanes_c], lambda source, step: wup.at[step, s, y])
    down_z = along(wdown_in.at[c, s, y], lambda source, step: wdown.at[step, s, y])

    class Relay:
        def __init__(self, k_, at_one, at_two, x_first, when=None):
            self.k, self.when = k_, when
            self.one = net.wire(at_one, at_one, x_nbr if x_first else y_nbr, when, when)
            self.two = net.wire(at_two, at_two, y_nbr if x_first else x_nbr, when, when)

        def at_round(self, r, act):
            if r == self.k:
                pl.when(t + self.k < rows)(act)
            if r == rows - self.k:
                pl.when(t + self.k >= rows)(act)

        def first_hop(self, r):
            self.at_round(r, self.one.start)

        def second_hop(self, r):
            def act():
                self.one.arrived()
                self.two.start()

            self.at_round(r, act)

    wa_relay, up_relay, down_relay = [], [], []
    for k_ in range(1, rows):
        source = ring(k_)
        slot_of = lax.rem(source, 2)
        wa_relay.append(Relay(
            k_, wa.at[:, slot_of, s, y], wa.at[:, slot_of, :, y], True, lax.div(source, 2) == c,
        ))
        up_relay.append(Relay(k_, wup.at[k_, s, y], wup.at[k_, :, y], True))
        down_relay.append(Relay(k_, wdown.at[k_, s, y], wdown.at[k_, s], False))
    cot_wires = swap(cot_in, cot.at[s])
    cot_mate = net.wire(cot.at[c], cot.at[c], mate)

    bvec[0] = jnp.zeros(bvec.shape[1:], F4)
    bvec[0, 0:1, :] = b_up[...].reshape(1, width)
    shard = b_query.shape[0]

    @pl.when(lax.rem(t, 2) == 0)
    def _():
        bvec[0, 1:2, :shard] = b_query[...].reshape(1, shard)

    @pl.when(lax.rem(t, 2) == 1)
    def _():
        bvec[0, 1:2, shard:2 * shard] = b_query[...].reshape(1, shard)

    for i, vector in enumerate((gain1, bias1, gain2, bias2, b_out, b_down, b_value)):
        vecs[i:i + 1, :vector.shape[0]] = vector[...].reshape(1, vector.shape[0])
    row_ids = lax.broadcasted_iota(jnp.int32, seg.shape, 0)
    seg_row = jnp.sum(jnp.where(row_ids == t, seg[...], 0), axis=0, keepdims=True)
    segint[0] = jnp.broadcast_to(seg_row, segint.shape[1:])
    for own in wa_own:
        own.arrived()
    for group in (wa_z[0], up_z[0], down_z[0]):
        for wire in group:
            wire.start()
    seg_wire.start()
    for wire in bvec_wires:
        wire.start()
    for own in (wval_own, up_own, down_own):
        own.start()

    paths = ((wa_z, wa_relay), (up_z, up_relay), (down_z, down_relay))

    def hop(r):
        for wires, relays in paths:
            for wire in wires[r - 1]:
                wire.arrived()
            if r < rows - 1:
                for wire in wires[r]:
                    wire.start()
            for relay in relays:
                relay.first_hop(r)

    def second_hop(r):
        for _, relays in paths:
            for relay in relays:
                relay.second_hop(r)

    hop(1)
    hop(2)
    start_all(token_wires)
    second_hop(1)
    seg_wire.arrived()
    chosen = jnp.where(same, segint[0], segint[1]).astype(F4)
    segrow[...] = chosen
    for part in range(length // 128):
        piece = jnp.broadcast_to(chosen[0:1, part * 128:(part + 1) * 128], (128, 128))
        segcol[part * 128:(part + 1) * 128, :] = piece.T
    hop(3)
    second_hop(2)
    sent_all([group[0] for group in token_wires[1:]])
    for wire in first_wires:
        wire.start()
    first_own.start()

    n1_wires = []
    for step in range(rows):
        place = ring(-step)
        for wire in token_wires[step]:
            wire.arrived()
        unit, _ = norm_stats(x_own[place].astype(F4))
        n1[c, place] = (unit * vecs[0:1, :] + vecs[1:2, :]).astype(BF)
        wire = net.wire(n1.at[c, place], n1.at[c, place], mate)
        wire.start()
        n1_wires.append(wire)
    second_hop(3)
    for relay in wa_relay:
        relay.two.arrived()
    wval_own.arrived()
    for wire in bvec_wires:
        wire.arrived()
    for wire in n1_wires:
        wire.arrived()

    heads_width = q.shape[1]
    factor = HEAD_DIM ** (-0.5)
    b_q = (bvec[lax.rem(2 * c + rows - t, rows), 1:2, :heads_width]
           + bvec[lax.rem(2 * c + 1 + rows - t, rows), 1:2, :heads_width])
    wq, wk, wo = (wa.at[i] for i in range(3))

    def flat(ref_value):
        return ref_value.reshape(-1, ref_value.shape[-1])

    per_half = half // QB
    per_blk = QB // blk

    def n1_rows(i):
        return flat(n1[lax.div(i, per_half), pl.ds(lax.rem(i, per_half) * per_blk, per_blk)])

    def project_in(i, carry):
        at = pl.ds(pl.multiple_of(i * QB, QB), QB)
        block = n1_rows(i)
        q[at, :] = ((dot_nt(block, flat(wq[...])) + b_q) * factor).astype(BF)
        k_block = dot_nt(block, flat(wk[...]))
        k[at, :] = k_block.astype(BF)
        return carry

    lax.fori_loop(0, length // QB, project_in, 0)
    sent_all(first_wires)
    start_all(cot_wires)


    @pl.when(c == 0)
    def _():
        def fresh(i, carry):
            got = (dot(n1_rows(i), wval[...]) + vecs[6:7, :heads_width]).astype(BF)
            v[pl.ds(i * per_blk, per_blk)] = got.reshape(per_blk, blk, heads_width)
            return carry

        lax.fori_loop(0, length // QB, fresh, 0)

    @pl.when(c == 1)
    def _():
        first_arrived()

    pairs = heads_width // 128
    n_q = length // QB
    lane = lax.broadcasted_iota(jnp.int32, (1, 128), 1)
    keeps = (lane < HEAD_DIM, lane >= HEAD_DIM)

    def attend(j, bias, lsecol):
        count = (j + 1) * QB
        at = slice(j * QB, count)
        key_pos = lax.broadcasted_iota(jnp.int32, (QB, count), 1)
        query_pos = j * QB + lax.broadcasted_iota(jnp.int32, (QB, count), 0)
        allowed = (segcol[at, 0:1] == segrow[0:1, :count]) & (key_pos <= query_pos)
        bias[:, :count] = jnp.where(allowed, 0.0, far_below)
        lsecol[...] = jnp.zeros_like(lsecol)

        def pair(hp, carry):
            lanes = pl.ds(pl.multiple_of(hp * 128, 128), 128)
            q_pair = q[at, lanes]
            k_pair = k[:count, lanes]
            v_pair = flat(v[:count // blk, :, lanes])
            total = None
            for i in range(2):
                scores = dot_nt(q_pair, jnp.where(keeps[i], k_pair, 0.0)) + bias[:, :count]
                top = jnp.max(scores, axis=1, keepdims=True)
                weights = jnp.exp(scores - top)
                norm = jnp.sum(weights, axis=1, keepdims=True)
                part = dot(weights.astype(BF), jnp.where(keeps[i], v_pair, 0.0)) * (1.0 / norm)
                total = part if total is None else total + part
                lsecol[...] = jnp.where(lane == 2 * hp + i, top + jnp.log(norm), lsecol[...])
            att[at, lanes] = total.astype(BF)
            return carry

        lax.fori_loop(0, pairs, pair, 0)
        lse[:, at] = lsecol[...].T[:lse.shape[0], :]

    def attention(bias, lsecol):
        for j in range(n_q):
            attend(j, bias, lsecol)

    pl.run_scoped(attention, pltpu.VMEM((QB, length), F4), pltpu.VMEM((QB, 128), F4))

    att_wire = net.wire(xs.at[0], xr.at[0], mate)

    def half_rows(h, i):
        return pl.ds(pl.multiple_of(h * half + i * QB, QB), QB)

    def out_proj(i, carry):
        part = dot(att[half_rows(cn, i), :], flat(wo[...]))
        xs[0, pl.ds(i * QB, QB), :] = part.astype(BF)
        return carry

    lax.fori_loop(0, per_half, out_proj, 0)
    att_wire.start()

    def out_proj_mine(i, carry):
        mine[pl.ds(i * QB, QB), :] = dot(att[half_rows(c, i), :], flat(wo[...]))
        return carry

    lax.fori_loop(0, per_half, out_proj_mine, 0)
    att_wire.arrived()

    n2_wires = []
    for i in range(rows):
        at = slice(i * blk, (i + 1) * blk)
        middle = x_own[i].astype(F4) + mine[at, :] + xr[0, at, :].astype(F4) + vecs[4:5, :]
        mid[at, :] = middle
        unit, _ = norm_stats(middle)
        n2[c, i] = (unit * vecs[2:3, :] + vecs[3:4, :]).astype(BF)
        wire = net.wire(n2.at[c, i], n2.at[c, i], mate)
        wire.start()
        n2_wires.append(wire)
    up_own.arrived()
    down_own.arrived()
    for relay in up_relay + down_relay:
        relay.two.arrived()

    hid = wup.shape[-1]
    back_wire = net.wire(xs.at[1], xr.at[1], mate)
    mlp_wire = net.wire(xs.at[2], xr.at[2], mate)
    out_wires = swap(out_s, out)
    gm_wires = [net.wire(gm.at[c, i], gm.at[c, i], mate) for i in range(rows)]
    order = tuple(range(1, rows)) + (0,)

    class Reduce:
        def __init__(self, grad, one, two, z, p, y_first):
            self.grad, self.p, self.y_first = grad, p, y_first
            self.got_one, self.got_two, self.z = one, two, None
            if y_first:
                self.one = net.wire(grad.at[p, :, yn], one.at[p], y_nbr)
                self.two = net.wire(grad.at[p, sn, y], two.at[p], x_nbr)
            else:
                self.one = net.wire(grad.at[p, sn], one.at[p], x_nbr)
                self.two = net.wire(grad.at[p, s, yn], two.at[p], y_nbr)
            if p:
                self.z = net.wire(grad.at[p, s, y], z.at[p], dev(s, y, c, ring(p)))

        def run(self, stage):
            grad, p = self.grad, self.p
            if stage == 1:
                self.one.arrived()
                if self.y_first:
                    grad[p, :, y] = add(grad[p, :, y], self.got_one[p])
                else:
                    grad[p, s] = add(grad[p, s], self.got_one[p])
                self.two.start()
            else:
                self.two.arrived()
                grad[p, s, y] = add(grad[p, s, y], self.got_two[p])
                if p:
                    self.z.start()

    def add(one, two):
        return (one.astype(F4) + two.astype(F4)).astype(BF)

    down_rs = [Reduce(gdown, down_r1, down_r2, down_r3, p, True) for p in range(rows)]
    up_rs = [Reduce(gup, up_r1, up_r2, up_r3, p, p == 0) for p in range(rows)]

    class Small:
        def __init__(self, group):
            self.group = group
            self.here = 4 * s + 2 * y + c
            mine_at = small_p.at[group, self.here]
            self.plane = []
            for ds in range(2):
                for dy in range(2):
                    for dc in range(2):
                        if ds or dy or dc:
                            to = dev(lax.rem(s + ds, 2), lax.rem(y + dy, 2), lax.rem(c + dc, 2), t)
                            self.plane.append(net.wire(mine_at, mine_at, to))
            at_z = small_z.at[group, t]
            self.z = [net.wire(at_z, at_z, dev(s, y, c, ring(step))) for step in range(1, rows)]

        def run(self, stage):
            group = self.group
            if stage == 0:
                small_p[group, self.here] = small[group]
                for wire in self.plane:
                    wire.start()
            elif stage == 1:
                for wire in self.plane:
                    wire.arrived()
                total = small_p[group, 0]
                for i in range(1, 8):
                    total = total + small_p[group, i]
                small_z[group, t] = total
                for wire in self.z:
                    wire.start()
            else:
                for wire in self.z:
                    wire.arrived()
                f_small[8 * group:8 * group + 8, :] = (
                    (small_z[group, 0] + small_z[group, 1]) + (small_z[group, 2] + small_z[group, 3])
                )

    small_sums = [Small(0), Small(1)]
    gelu_scale = math.sqrt(2.0 / math.pi)

    def feed_forward(act, ghid, bup_sum, back_own):
        bup_sum[...] = jnp.zeros_like(bup_sum)

        def forward(h, i, keep):
            at = half_rows(h, i)
            n2_block = flat(n2[h, pl.ds(i * per_blk, per_blk)])
            mlp = None
            for p in range(rows):
                cols = slice(p * hid, (p + 1) * hid)
                z = dot(n2_block, flat(wup[p])) + bvec[p, 0:1, lanes_c]
                z2 = z * z
                th = jnp.tanh(gelu_scale * z * (1.0 + 0.044715 * z2))
                cdf = 0.5 * (1.0 + th)
                a = (z * cdf).astype(BF)
                slope = cdf + 0.5 * z * (1.0 - th * th) * (gelu_scale * (1.0 + 3 * 0.044715 * z2))
                act[at, cols] = a
                ghid[at, cols] = slope.astype(BF)
                part = dot(a, flat(wdown[p]))
                mlp = part if mlp is None else mlp + part
            to = pl.ds(pl.multiple_of(i * QB, QB), QB)
            if keep:
                mine[to, :] = mlp
            else:
                xs[2, to, :] = mlp.astype(BF)

        def backward(h, i, keep):
            at = half_rows(h, i)
            cot_block = flat(cot[h, pl.ds(i * per_blk, per_blk)])
            back = None
            for p in range(rows):
                cols = slice(p * hid, (p + 1) * hid)
                g = (dot_nt(cot_block, flat(wdown[p])) * ghid[at, cols].astype(F4)).astype(BF)
                ghid[at, cols] = g
                bup_sum[0:1, cols] += jnp.sum(g.astype(F4), axis=0, keepdims=True)
                part = dot_nt(g, flat(wup[p]))
                back = part if back is None else back + part
            to = pl.ds(pl.multiple_of(i * QB, QB), QB)
            if keep:
                back_own[to, :] = back
            else:
                xs[1, to, :] = back.astype(BF)

        def each(step, h, keep):
            def body(i, carry):
                step(h, i, keep)
                return carry

            lax.fori_loop(0, per_half, body, 0)

        each(forward, c, True)
        for wire in n2_wires:
            wire.arrived()
        each(forward, cn, False)
        mlp_wire.start()
        arrived_all(cot_wires)
        cot_mate.start()
        each(backward, c, True)
        mlp_wire.arrived()
        for i in range(rows):
            at = slice(i * blk, (i + 1) * blk)
            out_s[i] = (mid[at, :] + mine[at, :] + xr[2, at, :].astype(F4) + vecs[5:6, :]).astype(BF)
        start_all(out_wires)
        cot_mate.arrived()

        for p in order:
            got = dot_tn(act[:, p * hid:(p + 1) * hid], flat(cot[...]))
            gdown[p] = got.astype(BF).reshape(gdown.shape[1:])
            down_rs[p].one.start()
        each(backward, cn, False)
        back_wire.start()
        for p in order:
            for m in range(2):
                n2_part = flat(n2[:, :, :, m * (width // 2):(m + 1) * (width // 2)])
                got = dot_tn(n2_part, ghid[:, p * hid:(p + 1) * hid])
                gup[p, m] = got.astype(BF).reshape(gup.shape[2:])
            up_rs[p].one.start()
        small[...] = jnp.zeros_like(small)
        for p in range(rows):
            small[1, pl.ds(ring(p), 1), lanes_c] = bup_sum[0:1, p * hid:(p + 1) * hid]

        back_wire.arrived()
        sums = [jnp.zeros((1, width), F4) for _ in range(4)]
        for i in range(rows):
            at = slice(i * blk, (i + 1) * blk)
            middle = mid[at, :]
            unit, inverse = norm_stats(middle)
            back = back_own[at, :] + xr[1, at, :].astype(F4)
            cot_block = cot[c, i].astype(F4)
            g_middle = cot_block + norm_back(back, unit, inverse, vecs[2:3, :])
            mid[at, :] = g_middle
            g_low = g_middle.astype(BF)
            gm[c, i] = g_low
            gm_wires[i].start()
            for n, item in enumerate((back * unit, back, g_low.astype(F4), cot_block)):
                sums[n] += jnp.sum(item, axis=0, keepdims=True)
        for n in range(4):
            small[1, 4 + n:5 + n, :] = sums[n]
        small_sums[1].run(0)

    pl.run_scoped(
        feed_forward,
        pltpu.VMEM((length, rows * hid), BF),
        pltpu.VMEM((length, rows * hid), BF),
        pltpu.VMEM((8, rows * hid), F4),
        pltpu.VMEM((half, width), F4),
    )

    plane = ((x_nbr, sn, y), (y_nbr, s, yn), (diag, sn, yn))

    class Gather:
        def __init__(self, parts, grad, got, total, at_own, at_core):
            self.parts, self.grad, self.got, self.total = parts, grad, got, total
            self.keep = net.own(total, at_own)
            self.ag = [net.wire(total, at_own, to) for to, _, _ in plane]
            self.over = net.wire(at_core, at_core, mate)

        def run(self, stage):
            if stage == 0:
                for p in range(1, rows):
                    self.parts[p].z.arrived()
                total = self.grad[0, s, y].astype(F4)
                for p in range(1, rows):
                    total += self.got[p].astype(F4)
                self.total[...] = total.astype(BF)
                self.keep.start()
                for wire in self.ag:
                    wire.start()
            elif stage == 1:
                self.keep.arrived()
                for wire in self.ag:
                    wire.arrived()
                self.over.start()
            else:
                self.over.arrived()

    up_end = Gather(up_rs, gup, up_r3, f_s.at[0], f_up.at[s, y, :, lanes_c], f_up.at[:, :, :, lanes_c])
    down_end = Gather(down_rs, gdown, down_r3, f_t, f_down.at[c, s, y], f_down.at[c])

    back1_wire = net.wire(xs.at[0], xr.at[0], mate)
    gtok_wires = swap(out_s, gtok)
    gfirst_slot = net.recv_slots(rows)
    gfirst_wires = []
    for h in range(2):
        for step in range(rows):
            j = ring(step)
            to_me = (c == 1) & (s == h) & (s == 1) if step == 0 else None
            fine = (c == 1) & jnp.logical_not(to_me) if step == 0 else c == 1
            gfirst_wires.append(net.wire(
                gv_s.at[h * rows + j], gfirst.at[t], dev(h, y, s, j), fine, None, gfirst_slot + step,
            ))
    gfirst_own = net.own(gv_s.at[rows + t], gfirst.at[t], (c == 1) & (s == 1))
    class Heads:
        def __init__(self, first_one, count, x_first):
            self.part = part = pl.ds(first_one, count)
            self.x_first = x_first
            if x_first:
                self.one = net.wire(gwa.at[part, :, sn], wa_r1.at[part], x_nbr)
                self.two = net.wire(gwa.at[part, :, s, yn], wa_r2.at[part], y_nbr)
            else:
                self.one = net.wire(gwa.at[part, :, :, yn], wa_r1.at[part], y_nbr)
                self.two = net.wire(gwa.at[part, :, sn, y], wa_r2.at[part], x_nbr)
            self.rz = []
            for step in range(1, rows):
                to = ring(step)
                self.rz.append(net.wire(
                    gwa.at[part, lax.rem(to, 2), s, y], wa_r3.at[step, part], dev(s, y, c, to),
                    lax.div(to, 2) == c, home,
                ))
            self.keep = net.own(f_w.at[part], f_wa.at[part, s, y], home)
            self.ag = [net.wire(f_w.at[part], f_wa.at[part, s, y], to, home, home) for to, _, _ in plane]
            self.over = net.wire(f_wa.at[part], f_wa.at[part], mate, home, away)

        def run(self, stage):
            part = self.part
            if stage == 0:
                self.one.start()
            elif stage == 0.5:
                self.one.arrived()
                if self.x_first:
                    gwa[part, :, s] = add(gwa[part, :, s], wa_r1[part])
                else:
                    gwa[part, :, :, y] = add(gwa[part, :, :, y], wa_r1[part])
                self.two.start()
            elif stage == 1:
                self.two.arrived()
                gwa[part, :, s, y] = add(gwa[part, :, s, y], wa_r2[part])
                for wire in self.rz:
                    wire.start()
            elif stage == 2:
                @pl.when(home)
                def _():
                    for wire in self.rz:
                        wire.copy.wait_recv()
                    total = gwa[part, lax.rem(t, 2), s, y].astype(F4)
                    for i in range(1, rows):
                        total += wa_r3[i, part].astype(F4)
                    f_w[part] = total.astype(BF)

                self.keep.start()
                for wire in self.ag:
                    wire.start()
            elif stage == 3:
                self.keep.arrived()
                for wire in self.ag:
                    wire.arrived()
                self.over.start()
            else:
                self.over.arrived()

    heads_out, heads_q, heads_k = Heads(2, 1, False), Heads(0, 1, True), Heads(1, 1, False)
    lead, follow = c == 0, c == 1
    wv_rs = [net.wire(gwv.at[ds, dy], wv_r1.at[i], to, lead, lead) for i, (to, ds, dy) in enumerate(plane)]
    wv_rz = [
        net.wire(wv_r3.at[t], wv_r3.at[t], dev(s, y, c, ring(step)), lead, lead) for step in range(1, rows)
    ]
    wv_own_f = net.own(f_v, f_wv.at[s, y], lead)
    wv_ag = [net.wire(f_v, f_wv.at[s, y], to, lead, lead) for to, _, _ in plane]
    wv_over = net.wire(f_wv, f_wv, mate, lead, follow)

    def fresh_reduce(stage):
        if stage == 0:
            for wire in wv_rs:
                wire.start()
        elif stage == 1:
            @pl.when(lead)
            def _():
                for wire in wv_rs:
                    wire.copy.wait_recv()
                total = gwv[s, y].astype(F4)
                for i in range(3):
                    total += wv_r1[i].astype(F4)
                wv_r3[t] = total.astype(BF)

            for wire in wv_rz:
                wire.start()
        elif stage == 2:
            @pl.when(lead)
            def _():
                for wire in wv_rz:
                    wire.copy.wait_recv()
                parts = [wv_r3[i].astype(F4) for i in range(rows)]
                f_v[...] = ((parts[0] + parts[1]) + (parts[2] + parts[3])).astype(BF)

            wv_own_f.start()
            for wire in wv_ag:
                wire.start()
        elif stage == 3:
            wv_own_f.arrived()
            for wire in wv_ag:
                wire.arrived()
            wv_over.start()
        else:
            wv_over.arrived()

    heads_here = heads_width // HEAD_DIM
    pick_head = lax.broadcasted_iota(jnp.int32, (lse.shape[0], heads_width), 1) // HEAD_DIM
    pick = (pick_head == lax.broadcasted_iota(jnp.int32, pick_head.shape, 0)).astype(BF)

    def attention_back(gk, gv, delta, tmp, gq, kt, gqt, bias_t):
        kt[...] = k[...].T
        gk[...] = jnp.zeros_like(gk)
        gv[...] = jnp.zeros_like(gv)

        def grad_att(h, i):
            at = half_rows(h, i)
            block = flat(gm[h, pl.ds(i * per_blk, per_blk)])
            low = dot_nt(block, flat(wo[...])).astype(BF)
            gatt[at, :] = low
            product = low.astype(F4) * att[at, :].astype(F4)
            high = product.astype(BF)
            rest_of = (product - high.astype(F4)).astype(BF)
            delta[:, at] = dot_nt(pick, high) + dot_nt(pick, rest_of)

        def grad_att_mine(i, carry):
            grad_att(c, i)
            return carry

        def grad_att_mate(i, carry):
            grad_att(cn, i)
            return carry

        lax.fori_loop(0, per_half, grad_att_mine, 0)
        for wire in gm_wires:
            wire.arrived()
        lax.fori_loop(0, per_half, grad_att_mate, 0)
        gwa[2] = dot_tn(att[...], flat(gm[...])).astype(BF).reshape(gwa.shape[1:])
        heads_out.run(0)
        down_rs[1].run(1)
        down_rs[2].run(1)

        def back_block(j):
            count = (j + 1) * QB
            at = slice(j * QB, count)
            key_pos = lax.broadcasted_iota(jnp.int32, (count, QB), 0)
            query_pos = j * QB + lax.broadcasted_iota(jnp.int32, (count, QB), 1)
            allowed = (segcol[:count, 0:1] == segrow[0:1, at]) & (key_pos <= query_pos)
            bias_t[:count, :] = jnp.where(allowed, 0.0, far_below)

            def pair(hp, carry):
                lanes = pl.ds(pl.multiple_of(hp * 128, 128), 128)
                q_pair = q[at, lanes]
                k_pair = k[:count, lanes]
                v_pair = flat(v[:count // blk, :, lanes])
                ga_pair = gatt[at, lanes]
                sum_k = sum_v = None
                for i in range(2):
                    head = 2 * hp + i
                    scores = dot_nt(jnp.where(keeps[i], k_pair, 0.0), q_pair) + bias_t[:count, :]
                    probs = jnp.exp(scores - lse[pl.ds(head, 1), at])
                    grad_prob = dot_nt(jnp.where(keeps[i], v_pair, 0.0), ga_pair)
                    grad_score = (probs * (grad_prob - delta[pl.ds(head, 1), at])).astype(BF)
                    part_v = dot(probs.astype(BF), jnp.where(keeps[i], ga_pair, 0.0))
                    part_k = dot(grad_score, jnp.where(keeps[i], q_pair, 0.0))
                    sum_v = part_v if sum_v is None else sum_v + part_v
                    sum_k = part_k if sum_k is None else sum_k + part_k
                    channels = pl.ds(pl.multiple_of(hp * 128 + i * HEAD_DIM, HEAD_DIM), HEAD_DIM)
                    gqt[channels, at] = (dot(kt[channels, :count], grad_score) * factor).astype(BF)
                gk[:count, lanes] += sum_k
                gv[:count, lanes] += sum_v
                return carry

            lax.fori_loop(0, pairs, pair, 0)

        for j in range(n_q):
            back_block(j)
            if j == 1:
                down_rs[3].run(1)
                up_rs[2].run(1)
            if j == 2:
                down_rs[0].run(1)
                up_rs[3].run(1)
                down_rs[1].run(2)
                down_rs[2].run(2)
            if j == 3:
                up_rs[1].run(1)
                down_rs[3].run(2)
                up_rs[2].run(2)
                up_rs[3].run(2)

        gq[...] = gqt[...].T
        gk_low = gk[...].astype(BF)
        k[...] = gk_low
        gv_s[...] = gv[...].astype(BF).reshape(gv_s.shape)

        n1_all = flat(n1[...])
        gwa[0] = dot(gqt[...], n1_all).astype(BF).reshape(gwa.shape[1:])
        heads_q.run(0)
        gwa[1] = dot_tn(k[...], n1_all).astype(BF).reshape(gwa.shape[1:])
        heads_k.run(0)
        for wire in gfirst_wires:
            wire.start()
        gfirst_own.start()
        up_rs[0].run(1)
        down_rs[0].run(2)
        small[0, 7:8, lanes_h] = jnp.sum(gq[...].astype(F4), axis=0, keepdims=True)

        @pl.when(lead)
        def _():
            gv_low = flat(gv_s[...])
            gwv[...] = dot_tn(gv_low, n1_all).astype(BF).reshape(gwv.shape)
            small[0, 6:7, :heads_width] = jnp.sum(gv_low.astype(F4), axis=0, keepdims=True)

        fresh_reduce(0)
        heads_out.run(0.5)
        small_sums[1].run(1)

        def back_rows(h, i):
            at = half_rows(h, i)
            tmp[...] = dot(gq[at, :], flat(wq[...])) + dot(k[at, :], flat(wk[...]))

            @pl.when(lead)
            def _():
                block = flat(gv_s[pl.ds(h * rows + i * per_blk, per_blk)])
                tmp[...] += dot_nt(block, wval[...])

        def back_mate(i, carry):
            back_rows(cn, i)
            xs[0, pl.ds(pl.multiple_of(i * QB, QB), QB), :] = tmp[...].astype(BF)
            return carry

        def back_mine(i, carry):
            back_rows(c, i)
            mine[pl.ds(pl.multiple_of(i * QB, QB), QB), :] = tmp[...]
            return carry

        net.done(att_wire)
        lax.fori_loop(0, per_half, back_mate, 0)
        back1_wire.start()
        lax.fori_loop(0, per_half, back_mine, 0)
        up_rs[1].run(2)

    lanes_h = pl.ds(pl.multiple_of(c * heads_width, 128), heads_width)
    pl.run_scoped(
        attention_back,
        pltpu.VMEM((length, heads_width), F4),
        pltpu.VMEM((length, heads_width), F4),
        pltpu.VMEM((lse.shape[0], length), F4),
        pltpu.VMEM((QB, width), F4),
        pltpu.VMEM((length, heads_width), BF),
        pltpu.VMEM((heads_width, length), BF),
        pltpu.VMEM((heads_width, length), BF),
        pltpu.VMEM((length, QB), F4),
    )

    back1_wire.arrived()
    for group in out_wires:
        net.done(group[0])
    out_wires[0][1].arrived()
    gain_sum = jnp.zeros((1, width), F4)
    bias_sum = jnp.zeros((1, width), F4)
    for i in range(rows):
        at = slice(i * blk, (i + 1) * blk)
        unit, inverse = norm_stats(x_own[i].astype(F4))
        back = mine[at, :] + xr[0, at, :].astype(F4)
        gain_sum += jnp.sum(back * unit, axis=0, keepdims=True)
        bias_sum += jnp.sum(back, axis=0, keepdims=True)
        out_s[i] = (mid[at, :] + norm_back(back, unit, inverse, vecs[0:1, :])).astype(BF)
    small[0, 0:1, :] = gain_sum
    small[0, 1:2, :] = bias_sum
    start_all(gtok_wires)
    small_sums[0].run(0)

    heads_out.run(1)
    up_rs[0].run(2)
    down_end.run(0)
    heads_q.run(0.5)
    heads_k.run(0.5)
    fresh_reduce(1)
    small_sums[0].run(1)
    heads_q.run(1)
    heads_k.run(1)
    heads_out.run(2)
    up_end.run(0)
    down_end.run(1)
    fresh_reduce(2)
    heads_q.run(2)
    heads_k.run(2)
    heads_out.run(3)
    up_end.run(1)
    fresh_reduce(3)
    heads_q.run(3)
    heads_k.run(3)
    small_sums[1].run(2)
    small_sums[0].run(2)
    down_end.run(2)
    up_end.run(2)
    heads_out.run(4)
    heads_q.run(4)
    heads_k.run(4)
    fresh_reduce(4)
    for group in out_wires:
        group[0].arrived()
    arrived_all(gtok_wires)
    for step in range(rows):
        def take(step=step):
            pltpu.make_async_remote_copy(
                src_ref=gv_s.at[0], dst_ref=gfirst.at[0], send_sem=send_sems.at[0],
                recv_sem=recv_sems.at[gfirst_slot + step], device_id=mate, device_id_type=MESH,
            ).wait_recv()
        if step == 0:
            pl.when((c == 0) | (s == 0))(take)
        else:
            take()
    gfirst_own.arrived()
    for wire in net.all:
        wire.sent()


def whole_layer(
    tokens, first_values, segment_ids, cotangent, norm1_gain, norm1_bias, w_query, b_query, w_key,
    w_value, b_value, w_out, b_out, norm2_gain, norm2_bias, w_up, b_up, w_down, b_down,
):
    rows, blk, width = tokens.shape
    half = rows * blk
    length = 2 * half
    valf = w_value.shape[1]
    tp_width = w_query.shape[1]
    hid = w_up.shape[1] // 2
    heads = tuple(w.reshape(2, 2, tp_width // 4, width) for w in (w_query.T, w_key.T, w_out))
    hbm = pl.BlockSpec(memory_space=pl.ANY)
    vmem = pl.BlockSpec(memory_space=pltpu.VMEM)
    piece = tp_width // 4
    up_rows, down_rows = width // 4, hid // 4

    def of(*shape, dtype=BF):
        return jax.ShapeDtypeStruct(shape, dtype)

    def room(*shape, dtype=BF):
        return pltpu.VMEM(shape, dtype)

    outs = (
        of(rows, blk, width), of(rows, blk, width), of(rows, blk, valf),
        of(2, 2, up_rows, 2 * hid), of(2, 2, 2, down_rows, width),
        of(3, 2, 2, piece, width), of(2, 2, valf // 4, width), of(16, width, dtype=F4),
    )
    scratch = [
        room(rows, blk, width), room(2, rows, blk, width), room(2, 8, length, dtype=jnp.int32),
        room(8, length, dtype=F4), room(length, 128, dtype=F4), room(8, width, dtype=F4), room(rows, 8, width, dtype=F4),
        room(3, 2, 2, 2, piece, width), room(width, valf),
        room(rows, 2, 2, up_rows, hid), room(rows, 2, 2, down_rows, width),
        room(length, 2 * tp_width), room(length, 2 * tp_width), room(2 * rows, blk, valf),
        room(length, 2 * tp_width), room(16, length, dtype=F4),
        room(half, width, dtype=F4), room(2, rows, blk, width), room(2, rows, blk, width),
        room(half, width, dtype=F4), room(3, half, width), room(3, half, width),
        room(rows, blk, width), room(2, rows, blk, width),
        room(length, 2 * tp_width), room(2 * rows, blk, valf),
        room(rows, 2, 2, up_rows, hid), room(rows, 2, 2, down_rows, width),
        room(rows, 2, up_rows, hid), room(rows, up_rows, hid), room(rows, up_rows, hid),
        room(rows, 2, down_rows, width), room(rows, down_rows, width), room(rows, down_rows, width),
        room(3, 2, 2, 2, piece, width), room(3, 2, 2, piece, width), room(3, 2, piece, width), room(rows, 3, piece, width),
        room(2, 2, valf // 4, width), room(3, valf // 4, width), room(rows, valf // 4, width),
        room(2, 8, width, dtype=F4), room(2, 8, 8, width, dtype=F4), room(2, rows, 8, width, dtype=F4),
        room(1, up_rows, hid), room(down_rows, width), room(3, piece, width), room(valf // 4, width),
        pltpu.SemaphoreType.DMA((SENDS,)), pltpu.SemaphoreType.DMA((RECVS,)), pltpu.SemaphoreType.DMA((OWNS,)),
    ]
    out, gtok, gfirst, f_up, f_down, f_wa, f_wv, f_small = pl.pallas_call(
        layer_kernel,
        out_shape=outs,
        in_specs=[hbm, hbm, hbm, vmem] + [hbm] * 6 + [vmem] * 9,
        out_specs=(hbm,) * 7 + (vmem,),
        scratch_shapes=scratch,
        compiler_params=pltpu.CompilerParams(
            collective_id=0, has_side_effects=True, vmem_limit_bytes=VMEM_BYTES
        ),
    )(
        tokens, first_values, cotangent, segment_ids, *heads,
        w_up.reshape(2, 2, up_rows, 2 * hid), w_down.reshape(2, 2, 2, down_rows, width), w_value,
        norm1_gain, norm1_bias, norm2_gain, norm2_bias, b_out, b_down, b_value, b_query, b_up,
    )
    vector = of(width, dtype=F4)
    results = pl.pallas_call(
        finish_kernel,
        out_shape=(
            of(rows, blk, width), of(rows, blk, valf), of(rows, blk, width, dtype=F4),
            of(width, 2 * hid, dtype=F4), of(2 * hid, width, dtype=F4),
            of(tp_width, width, dtype=F4), of(tp_width, width, dtype=F4), of(tp_width, width, dtype=F4),
            of(width, valf, dtype=F4),
            vector, vector, vector, vector, vector, vector, of(valf, dtype=F4), of(tp_width, dtype=F4), vector,
        ),
        in_specs=[hbm] * 7 + [vmem],
        out_specs=(hbm,) * 9 + (vmem,) * 9,
        scratch_shapes=[
            room(rows, blk, width), room(rows, blk, valf),
            room(rows, blk, width), room(width, 2 * hid), room(2 * hid, width), room(3 * tp_width, width), room(valf, width),
            room(rows, blk, width, dtype=F4), room(width, 2 * hid, dtype=F4), room(2 * hid, width, dtype=F4),
            room(tp_width, width, dtype=F4), room(tp_width, width, dtype=F4), room(tp_width, width, dtype=F4),
            room(width, valf, dtype=F4),
            pltpu.SemaphoreType.DMA((7,)), pltpu.SemaphoreType.DMA((9,)),
        ],
        compiler_params=pltpu.CompilerParams(vmem_limit_bytes=VMEM_BYTES),
    )(
        out, gfirst, gtok, f_up.reshape(width, 2 * hid), f_down.reshape(2 * hid, width),
        f_wa.reshape(3 * tp_width, width), f_wv.reshape(valf, width), f_small,
    )
    (out, gfirst, gtok, grad_up, grad_down, grad_q, grad_k, grad_o, grad_v,
     gain1, bias1, gain2, bias2, grad_b_out, grad_b_down, grad_b_v, grad_b_q, grad_b_up) = results
    return (
        out, gtok, gfirst, gain1, bias1, grad_q.T, grad_b_q, grad_k.T, grad_v, grad_b_v, grad_o, grad_b_out,
        gain2, bias2, grad_up, grad_b_up, grad_down, grad_b_down,
    )


def finish_kernel(
    out, gfirst, gtok, up, down, heads, value, small,
    out_o, gfirst_o, gtok_o, up_o, down_o, q_o, k_o, o_o, value_o,
    gain1, bias1, gain2, bias2, b_out, b_down, b_value, b_query, b_up,
    out_i, gfirst_i, gtok_i, up_i, down_i, heads_i, value_i, gtok_f, up_f, down_f, q_f, k_f, o_f, value_f, in_sems, out_sems,
):
    t = lax.axis_index("tp")
    loads = [
        pltpu.make_async_copy(src, dst, in_sems.at[i])
        for i, (src, dst) in enumerate((
            (up, up_i), (down, down_i), (gtok, gtok_i), (heads, heads_i), (value, value_i), (out, out_i), (gfirst, gfirst_i),
        ))
    ]
    for copy in loads:
        copy.start()
    stores = [
        pltpu.make_async_copy(src, dst, out_sems.at[i])
        for i, (src, dst) in enumerate((
            (up_f, up_o), (down_f, down_o), (gtok_f, gtok_o), (q_f, q_o), (k_f, k_o), (o_f, o_o), (value_f, value_o),
            (out_i, out_o), (gfirst_i, gfirst_o),
        ))
    ]
    for row, ref in enumerate((gain1, bias1)):
        ref[...] = small[row, :]
    for row, ref in enumerate((gain2, bias2, b_out, b_down)):
        ref[...] = small[12 + row, :]
    b_value[...] = small[6, :b_value.shape[0]]
    b_up[...] = small[8 + t, :]
    shard = b_query.shape[0]
    mine = jnp.zeros((1, shard), F4)
    for i in range(small.shape[1] // shard):
        mine = jnp.where(t == i, small[7:8, i * shard:(i + 1) * shard], mine)
    b_query[...] = mine.reshape(shard)
    for i, (src, dst) in enumerate(((up_i, up_f), (down_i, down_f), (gtok_i, gtok_f))):
        loads[i].wait()
        dst[...] = src[...].astype(F4)
        stores[i].start()
    loads[3].wait()
    for i, ref in enumerate((q_f, k_f)):
        ref[...] = heads_i[i * shard:(i + 1) * shard, :].astype(F4)
        stores[3 + i].start()
    o_f[...] = heads_i[2 * shard:3 * shard, :].astype(F4)
    stores[5].start()
    loads[4].wait()
    value_f[...] = value_i[...].astype(F4).T
    stores[6].start()
    for i in range(2):
        loads[5 + i].wait()
        stores[7 + i].start()
    for copy in stores:
        copy.wait()


SENDS = 176
RECVS = 176
OWNS = 20
VMEM_BYTES = 63 * 1024 * 1024


def fits(mesh):
    return mesh.shape["seq"] == 2 and mesh.shape["batch"] == 4 and mesh.shape["tp"] == 4


def solution(mesh):
    placed = (
        P("batch", ("seq", "tp"), None),
        P("batch", ("seq", "tp"), None),
        P("batch", None),
        P("batch", ("seq", "tp"), None),
        P(),
        P(),
        P(None, "tp"),
        P("tp"),
        P(None, "tp"),
        P(),
        P(),
        P("tp", None),
        P(),
        P(),
        P(),
        P(None, "tp"),
        P("tp"),
        P("tp", None),
        P(),
    )
    return jax.shard_map(
        whole_layer if fits(mesh) else on_device,
        mesh=mesh,
        in_specs=placed,
        out_specs=(
            P("batch", ("seq", "tp"), None),
            P("batch", ("seq", "tp"), None),
            P("batch", ("seq", "tp"), None),
            P(),
            P(),
            P(None, "tp"),
            P("tp"),
            P(None, "tp"),
            P(),
            P(),
            P("tp", None),
            P(),
            P(),
            P(),
            P(None, "tp"),
            P("tp"),
            P("tp", None),
            P(),
        ),
        check_vma=False,
    )
```

```python
import math

import jax
import jax.numpy as jnp
from jax import lax
from jax.experimental import pallas as pl
from jax.experimental.pallas import tpu as pltpu
from jax.sharding import PartitionSpec as P

HEADS = 12
HEAD_DIM = 64


eps = 1e-05
block_cap = 256
far_below = -1e30


def from_behind(block, axis, distance):
    devices = range(lax.axis_size(axis))
    route = [((i - distance) % len(devices), i) for i in devices]
    return lax.ppermute(block, axis, route)


def layer_norm(values, norm_gain, norm_bias):
    average = jnp.mean(values, axis=-1, keepdims=True)
    centered = values - average
    inverse = lax.rsqrt(jnp.mean(centered * centered, axis=-1, keepdims=True) + eps)
    unit = centered * inverse
    return (unit * norm_gain + norm_bias, unit, inverse)


def norm_back(grad_result, unit, inverse, norm_gain):
    scaled = grad_result * norm_gain
    return inverse * (
        scaled
        - jnp.mean(scaled, axis=-1, keepdims=True)
        - unit * jnp.mean(scaled * unit, axis=-1, keepdims=True)
    )


def project(values, weight):
    return jnp.einsum("rtd,de->rte", values, weight, preferred_element_type=jnp.float32)


def project_back(grads, weight):
    return jnp.einsum("rte,de->rtd", grads, weight, preferred_element_type=jnp.float32)


def weight_grad(values, grads):
    return jnp.einsum("rtd,rte->de", values, grads, preferred_element_type=jnp.float32)


def column_sum(values):
    return jnp.sum(values, axis=(0, 1), dtype=jnp.float32)


def gelu_tanh(values):
    return jax.nn.gelu(values, approximate=True)


def over_key_blocks(arrays, key_first, state, step, limit):
    count = arrays[0].shape[1]
    width = math.gcd(count, block_cap)

    def one(index, carry):
        offset = index * width
        parts = tuple((lax.dynamic_slice_in_dim(item, offset, width, 1) for item in arrays))
        first_key = key_first + offset

        def taken(inner):
            return step(inner, parts, first_key, offset)

        def skipped(inner):
            return inner

        return lax.cond(first_key <= limit, taken, skipped, carry)

    return lax.fori_loop(0, count // width, one, state)


def on_device(
    tokens,
    first_values,
    segment_ids,
    cotangent,
    norm1_gain,
    norm1_bias,
    w_query,
    b_query,
    w_key,
    w_value,
    b_value,
    w_out,
    b_out,
    norm2_gain,
    norm2_bias,
    w_up,
    b_up,
    w_down,
    b_down,
):
    rows = tokens.shape[0]
    model_width = tokens.shape[2]
    tp_count = lax.axis_size("tp")
    seq_count = lax.axis_size("seq")
    local_len = tokens.shape[1] * tp_count
    heads = w_query.shape[1] // HEAD_DIM
    width_tp = heads * HEAD_DIM
    valf_all = w_value.shape[1]
    factor = HEAD_DIM ** (-0.5)
    seq_index = lax.axis_index("seq")
    head_first = lax.axis_index("tp") * heads
    is_fresh = head_first < HEADS // 2
    fresh_col = jnp.minimum(head_first * HEAD_DIM, valf_all - width_tp)
    reuse_col = jnp.maximum(head_first * HEAD_DIM - valf_all, 0)
    own_first = seq_index * local_len
    own_last = own_first + local_len - 1
    own_pos = own_first + jnp.arange(local_len, dtype=jnp.int32)
    own_seg = lax.dynamic_slice_in_dim(segment_ids, own_first, local_len, 1)

    def masked_scores(query4, key_part, query_pos, query_seg, key_first):
        width = key_part.shape[1]
        scores = (
            jnp.einsum("rqhc,rkhc->rhqk", query4, key_part, preferred_element_type=jnp.float32)
            * factor
        )
        key_seg = lax.dynamic_slice_in_dim(segment_ids, key_first, width, 1)
        key_pos = key_first + jnp.arange(width, dtype=jnp.int32)
        allowed = (query_seg[:, :, None] == key_seg[:, None, :]) & (
            key_pos[None, None, :] <= query_pos[None, :, None]
        )
        return (scores, allowed[:, None])

    resid = tokens.astype(jnp.float32)
    normed_one, unit_one, inverse_one = layer_norm(resid, norm1_gain, norm1_bias)
    rows_one, grad_rows, first_rows = (
        lax.all_gather(normed_one.astype(jnp.bfloat16), "tp", axis=1, tiled=True),
        lax.all_gather(cotangent, "tp", axis=1, tiled=True),
        lax.all_gather(first_values, "tp", axis=1, tiled=True),
    )
    query4 = (
        (project(rows_one, w_query) + b_query)
        .astype(jnp.bfloat16)
        .reshape(rows, local_len, heads, HEAD_DIM)
    )
    keys4 = project(rows_one, w_key).astype(jnp.bfloat16).reshape(rows, local_len, heads, HEAD_DIM)
    w_part = lax.dynamic_slice_in_dim(w_value, fresh_col, width_tp, 1)
    b_part = lax.dynamic_slice_in_dim(b_value, fresh_col, width_tp, 0)

    def fresh_side(normed_rows):
        return (project(normed_rows, w_part) + b_part).astype(jnp.bfloat16)

    def reuse_side(normed_rows):
        return lax.dynamic_slice_in_dim(first_rows, reuse_col, width_tp, 2)

    vals4 = lax.cond(is_fresh, fresh_side, reuse_side, rows_one).reshape(
        rows, local_len, heads, HEAD_DIM
    )

    def stats_step(carry, parts, key_first, offset):
        top, total = carry
        scores, allowed = masked_scores(query4, parts[0], own_pos, own_seg, key_first)
        masked = jnp.where(allowed, scores, far_below)
        new_top = jnp.maximum(top, jnp.max(masked, axis=3))
        weights = jnp.where(allowed, jnp.exp(masked - new_top[..., None]), 0.0)
        return (new_top, total * jnp.exp(top - new_top) + jnp.sum(weights, axis=3))

    start_top = jnp.full((rows, heads, local_len), far_below, jnp.float32)
    start_total = jnp.zeros((rows, heads, local_len), jnp.float32)
    top, total = over_key_blocks(
        (lax.all_gather(keys4, "seq", axis=1, tiled=True),),
        jnp.int32(0),
        (start_top, start_total),
        stats_step,
        own_last,
    )
    lse = top + jnp.log(total)

    def value_step(acc, parts, key_first, offset):
        scores, allowed = masked_scores(query4, parts[0], own_pos, own_seg, key_first)
        weights = jnp.where(allowed, jnp.exp(scores - lse[..., None]), 0.0).astype(jnp.bfloat16)
        return acc + jnp.einsum(
            "rhqk,rkhc->rqhc", weights, parts[1], preferred_element_type=jnp.float32
        )

    zeros_q = jnp.zeros((rows, local_len, heads, HEAD_DIM), jnp.float32)
    attended = over_key_blocks(
        (
            lax.all_gather(keys4, "seq", axis=1, tiled=True),
            lax.all_gather(vals4, "seq", axis=1, tiled=True),
        ),
        jnp.int32(0),
        zeros_q,
        value_step,
        own_last,
    )
    attended_low = attended.astype(jnp.bfloat16).reshape(rows, local_len, width_tp)
    attn_share = lax.psum_scatter(
        project(attended_low, w_out).astype(jnp.bfloat16), "tp", scatter_dimension=1, tiled=True
    ).astype(jnp.float32)
    middle = resid + attn_share + b_out
    normed_two, unit_two, inverse_two = layer_norm(middle, norm2_gain, norm2_bias)
    rows_two = lax.all_gather(normed_two.astype(jnp.bfloat16), "tp", axis=1, tiled=True)
    hidden_pre = project(rows_two, w_up) + b_up
    activated_full, gelu_pull = jax.vjp(gelu_tanh, hidden_pre)
    activated = activated_full.astype(jnp.bfloat16)
    mlp_share = lax.psum_scatter(
        project(activated, w_down).astype(jnp.bfloat16), "tp", scatter_dimension=1, tiled=True
    ).astype(jnp.float32)
    output = (middle + mlp_share + b_down).astype(jnp.bfloat16)
    grad_b_down = column_sum(grad_rows)
    grad_w_down = weight_grad(activated, grad_rows)
    grad_hidden = gelu_pull(project_back(grad_rows, w_down))[0].astype(jnp.bfloat16)
    grad_b_up = column_sum(grad_hidden)
    grad_w_up = weight_grad(rows_two, grad_hidden)
    back_two = lax.psum_scatter(
        project_back(grad_hidden, w_up).astype(jnp.bfloat16), "tp", scatter_dimension=1, tiled=True
    ).astype(jnp.float32)
    grad_gain_two = jnp.sum(back_two * unit_two, axis=(0, 1))
    grad_bias_two = jnp.sum(back_two, axis=(0, 1))
    grad_middle = cotangent.astype(jnp.float32) + norm_back(
        back_two, unit_two, inverse_two, norm2_gain
    )
    grad_mid_rows = lax.all_gather(grad_middle.astype(jnp.bfloat16), "tp", axis=1, tiled=True)
    grad_b_out = column_sum(grad_mid_rows)
    grad_w_out = weight_grad(attended_low, grad_mid_rows)
    grad_out4 = (
        project_back(grad_mid_rows, w_out)
        .astype(jnp.bfloat16)
        .reshape(rows, local_len, heads, HEAD_DIM)
    )
    delta = jnp.einsum("rqhc,rqhc->rhq", grad_out4.astype(jnp.float32), attended)

    def pair_terms(key_side, val_side, key_first, grad_query, grad_keys, grad_vals):

        def pair_step(carry, parts, first, offset):
            acc_query, acc_keys, acc_vals = carry
            key_part, val_part = parts
            width = key_part.shape[1]
            scores, allowed = masked_scores(query4, key_part, own_pos, own_seg, first)
            probs = jnp.where(allowed, jnp.exp(scores - lse[..., None]), 0.0)
            grad_val = jnp.einsum(
                "rhqk,rqhc->rkhc",
                probs.astype(jnp.bfloat16),
                grad_out4,
                preferred_element_type=jnp.float32,
            )
            grad_prob = jnp.einsum(
                "rqhc,rkhc->rhqk", grad_out4, val_part, preferred_element_type=jnp.float32
            )
            grad_score = (probs * (grad_prob - delta[..., None])).astype(jnp.bfloat16)
            acc_query = (
                acc_query
                + jnp.einsum(
                    "rhqk,rkhc->rqhc", grad_score, key_part, preferred_element_type=jnp.float32
                )
                * factor
            )
            grad_key = (
                jnp.einsum(
                    "rhqk,rqhc->rkhc", grad_score, query4, preferred_element_type=jnp.float32
                )
                * factor
            )
            acc_keys = lax.dynamic_update_slice_in_dim(
                acc_keys, lax.dynamic_slice_in_dim(acc_keys, offset, width, 1) + grad_key, offset, 1
            )
            acc_vals = lax.dynamic_update_slice_in_dim(
                acc_vals, lax.dynamic_slice_in_dim(acc_vals, offset, width, 1) + grad_val, offset, 1
            )
            return (acc_query, acc_keys, acc_vals)

        return over_key_blocks(
            (key_side, val_side), key_first, (grad_query, grad_keys, grad_vals), pair_step, own_last
        )

    def turn_keys(turn, carry):
        moving_keys, moving_vals, moving_gk, moving_gv, grad_query = carry
        anchor = (seq_index - turn) % seq_count
        grad_query, moving_gk, moving_gv = pair_terms(
            moving_keys, moving_vals, anchor * local_len, grad_query, moving_gk, moving_gv
        )
        moving_keys, moving_vals, moving_gk, moving_gv = (
            from_behind(moving_keys, "seq", 1),
            from_behind(moving_vals, "seq", 1),
            from_behind(moving_gk.astype(jnp.bfloat16), "seq", 1).astype(moving_gk.dtype),
            from_behind(moving_gv.astype(jnp.bfloat16), "seq", 1).astype(moving_gv.dtype),
        )
        return (moving_keys, moving_vals, moving_gk, moving_gv, grad_query)

    start_state = (keys4, vals4, zeros_q, zeros_q, zeros_q)
    final_state = lax.fori_loop(0, seq_count, turn_keys, start_state)
    grad_keys4, grad_vals4, grad_query4 = (final_state[2], final_state[3], final_state[4])
    grad_query = grad_query4.astype(jnp.bfloat16).reshape(rows, local_len, width_tp)
    grad_keys = grad_keys4.astype(jnp.bfloat16).reshape(rows, local_len, width_tp)
    grad_vals = grad_vals4.astype(jnp.bfloat16).reshape(rows, local_len, width_tp)

    def fresh_back(grad_flat):
        gw_full = lax.dynamic_update_slice_in_dim(
            jnp.zeros((model_width, valf_all), jnp.float32),
            weight_grad(rows_one, grad_flat),
            fresh_col,
            1,
        )
        gb_full = lax.dynamic_update_slice_in_dim(
            jnp.zeros((valf_all,), jnp.float32), column_sum(grad_flat), fresh_col, 0
        )
        back_value = project_back(grad_flat, w_part)
        reuse_full = jnp.zeros((rows, local_len, valf_all), jnp.float32)
        return (gw_full, gb_full, back_value, reuse_full)

    def reuse_back(grad_flat):
        gw_full = jnp.zeros((model_width, valf_all), jnp.float32)
        gb_full = jnp.zeros((valf_all,), jnp.float32)
        back_value = jnp.zeros((rows, local_len, model_width), jnp.float32)
        reuse_full = lax.dynamic_update_slice_in_dim(
            jnp.zeros((rows, local_len, valf_all), jnp.float32),
            grad_flat.astype(jnp.float32),
            reuse_col,
            2,
        )
        return (gw_full, gb_full, back_value, reuse_full)

    grad_w_value, grad_b_value, back_value, reuse_full = lax.cond(
        is_fresh, fresh_back, reuse_back, grad_vals
    )
    grad_b_query = column_sum(grad_query)
    grad_w_query = weight_grad(rows_one, grad_query)
    grad_w_key = weight_grad(rows_one, grad_keys)
    back_terms = project_back(grad_query, w_query) + project_back(grad_keys, w_key) + back_value
    back_one, reuse_sum = (
        lax.psum_scatter(
            back_terms.astype(jnp.bfloat16), "tp", scatter_dimension=1, tiled=True
        ).astype(jnp.float32),
        lax.psum_scatter(
            reuse_full.astype(jnp.bfloat16), "tp", scatter_dimension=1, tiled=True
        ).astype(jnp.float32),
    )
    grad_first_values = reuse_sum.astype(jnp.bfloat16)
    grad_gain_one = jnp.sum(back_one * unit_one, axis=(0, 1))
    grad_bias_one = jnp.sum(back_one, axis=(0, 1))
    grad_tokens = grad_middle + norm_back(back_one, unit_one, inverse_one, norm1_gain)
    summed = lax.psum(
        (
            grad_w_query,
            grad_w_key,
            grad_w_out,
            grad_w_up,
            grad_w_down,
            grad_b_query,
            grad_b_out,
            grad_b_up,
            grad_b_down,
        ),
        ("seq", "batch"),
    )
    norm_sums = lax.psum(
        (grad_gain_one, grad_bias_one, grad_gain_two, grad_bias_two, grad_w_value, grad_b_value),
        ("seq", "batch", "tp"),
    )
    return (
        output,
        grad_tokens,
        grad_first_values,
        norm_sums[0],
        norm_sums[1],
        summed[0],
        summed[5],
        summed[1],
        norm_sums[4],
        norm_sums[5],
        summed[2],
        summed[6],
        norm_sums[2],
        norm_sums[3],
        summed[3],
        summed[7],
        summed[4],
        summed[8],
    )


BF = jnp.bfloat16
F4 = jnp.float32
MESH = pl.DeviceIdType.MESH
QB = 256


def dot(a, b):
    return lax.dot_general(a, b, (((1,), (0,)), ((), ())), preferred_element_type=F4)


def dot_nt(a, b):
    return lax.dot_general(a, b, (((1,), (1,)), ((), ())), preferred_element_type=F4)


def dot_tn(a, b):
    return lax.dot_general(a, b, (((0,), (0,)), ((), ())), preferred_element_type=F4)


def maybe(cond, act):
    if cond is None:
        act()
    else:
        pl.when(cond)(act)


class Wire:
    def __init__(self, copy, send_if=None, recv_if=None):
        self.copy, self.send_if, self.recv_if = copy, send_if, recv_if

    def start(self):
        maybe(self.send_if, self.copy.start)

    def arrived(self):
        maybe(self.recv_if, self.copy.wait_recv)

    def sent(self):
        maybe(self.send_if, self.copy.wait_send)


class Own:
    def __init__(self, copy, when=None):
        self.copy, self.when = copy, when

    def start(self):
        maybe(self.when, self.copy.start)

    def arrived(self):
        maybe(self.when, self.copy.wait)

    def sent(self):
        pass


class Net:
    def __init__(self, send_sems, recv_sems, own_sems):
        self.send_sems, self.recv_sems, self.own_sems = send_sems, recv_sems, own_sems
        self.n_send = self.n_recv = self.n_own = 0
        self.all = []

    def recv_slots(self, count):
        self.n_recv += count
        return self.n_recv - count

    def wire(self, src, dst, device, send_if=None, recv_if=None, slot=None):
        if slot is None:
            slot = self.recv_slots(1)
        copy = pltpu.make_async_remote_copy(
            src_ref=src,
            dst_ref=dst,
            send_sem=self.send_sems.at[self.n_send],
            recv_sem=self.recv_sems.at[slot],
            device_id=device,
            device_id_type=MESH,
        )
        self.n_send += 1
        made = Wire(copy, send_if, recv_if)
        self.all.append(made)
        return made

    def done(self, wire):
        wire.sent()
        self.all = [item for item in self.all if item is not wire]

    def own(self, src, dst, when=None):
        copy = pltpu.make_async_copy(src, dst, self.own_sems.at[self.n_own])
        self.n_own += 1
        return Own(copy, when)


def norm_stats(values):
    average = jnp.mean(values, axis=-1, keepdims=True)
    centered = values - average
    inverse = lax.rsqrt(jnp.mean(centered * centered, axis=-1, keepdims=True) + eps)
    return centered * inverse, inverse


def layer_kernel(
    tokens, first, cot_in, seg, wq_in, wk_in, wo_in, wup_in, wdown_in, wval_in,
    gain1, bias1, gain2, bias2, b_out, b_down, b_value, b_query, b_up,
    out, gtok, gfirst, f_up, f_down, f_wa, f_wv, f_small,
    x_own, n1, segint, segrow, segcol, vecs, bvec, wa, wval, wup, wdown,
    q, k, v, att, lse, mid, n2, cot,
    mine, xs, xr, out_s, gm, gatt, gv_s,
    gup, gdown, up_r1, up_r2, up_r3, down_r1, down_r2, down_r3,
    gwa, wa_r1, wa_r2, wa_r3, gwv, wv_r1, wv_r3,
    small, small_p, small_z, f_s, f_t, f_w, f_v,
    send_sems, recv_sems, own_sems,
):
    s, b, t = lax.axis_index("seq"), lax.axis_index("batch"), lax.axis_index("tp")
    y, c = lax.div(b, 2), lax.rem(b, 2)
    sn, yn, cn = 1 - s, 1 - y, 1 - c
    rows, blk, width = tokens.shape
    half = rows * blk
    length = 2 * half
    net = Net(send_sems, recv_sems, own_sems)

    def dev(ds, dy, dc, dt):
        return (ds, 2 * dy + dc, dt)

    def ring(step):
        return lax.rem(t + step + rows, rows)

    x_nbr, y_nbr, diag, mate = dev(sn, y, c, t), dev(s, yn, c, t), dev(sn, yn, c, t), dev(s, y, cn, t)
    home = lax.div(t, 2) == c
    away = lax.div(t, 2) != c
    same, other = s == c, s != c

    wa_own = [net.own(src, wa.at[i, lax.rem(t, 2)], home) for i, src in enumerate((wq_in, wk_in, wo_in))]
    for own in wa_own:
        own.start()

    gate = pltpu.get_barrier_semaphore()
    peers = [(ds, 2 * yn + dc, t) for ds in range(2) for dc in range(2)]
    for ds in range(2):
        for dc in range(2):
            for dt in range(rows):
                if ds or dc or dt:
                    peers.append((lax.rem(s + ds, 2), 2 * y + lax.rem(c + dc, 2), lax.rem(t + dt, rows)))
    for peer in peers:
        pl.semaphore_signal(gate, inc=1, device_id=peer, device_id_type=MESH)
    pl.semaphore_wait(gate, len(peers))

    def swap(src, dst):
        wires = []
        for step in range(rows):
            r = ring(step)
            if step == 0:
                wires.append((
                    net.wire(src.at[r], dst.at[t], dev(c, y, s, r), other, other),
                    net.own(src.at[r], dst.at[t], same),
                ))
            else:
                wires.append((net.wire(src.at[r], dst.at[t], dev(c, y, s, r)),))
        return wires

    def start_all(wires):
        for group in wires:
            for wire in group:
                wire.start()

    def sent_all(wires):
        for wire in wires:
            net.done(wire)

    def arrived_all(wires):
        for group in wires:
            for wire in group:
                wire.arrived()

    seg_wire = net.wire(segint.at[0], segint.at[1], mate)
    bvec_wires = []
    for step in range(1, rows):
        bvec_wires.append(net.wire(bvec.at[0], bvec.at[step], dev(s, y, c, ring(-step))))
    token_wires = swap(tokens, x_own)
    wval_own = net.own(wval_in, wval, c == 0)
    lanes_c = pl.ds(pl.multiple_of(c * (wup.shape[-1]), 128), wup.shape[-1])
    up_own = net.own(wup_in.at[:, :, :, lanes_c], wup.at[0])
    down_own = net.own(wdown_in.at[c], wdown.at[0])

    first_slot = net.recv_slots(2 * rows)
    first_wires = []
    for step in range(rows):
        r = ring(step)
        to = net.wire(
            first.at[r], v.at[s * rows + t], dev(c, y, 1, r),
            (c == 0) | (s == 0) if step == 0 else None, None, first_slot + s * rows + step,
        )
        first_wires.append(to)
    first_own = net.own(first.at[t], v.at[s * rows + t], (c == 1) & (s == 1))

    def first_arrived():
        for source in range(2):
            for step in range(rows):
                def take(source=source, step=step):
                    pltpu.make_async_remote_copy(
                        src_ref=first.at[0], dst_ref=v.at[0], send_sem=send_sems.at[0],
                        recv_sem=recv_sems.at[first_slot + source * rows + step],
                        device_id=mate, device_id_type=MESH,
                    ).wait_recv()
                if source == 1 and step == 0:
                    pl.when(s == 0)(take)
                else:
                    take()
        first_own.arrived()

    def along(own_piece, at_slot, only=None):
        rounds = []
        for r in range(1, rows):
            pair = []
            for right in (True, False):
                source = t - (r - 1) if right else t + (r - 1)
                came = t - r if right else t + r
                inside = (source >= 0) & (t < rows - 1) if right else (source < rows) & (t > 0)
                comes = came >= 0 if right else came < rows
                if only is not None:
                    inside, comes = inside & only(source), comes & only(came)
                held = (rows - r + 1 if right else r - 1) % rows
                lands = rows - r if right else r
                src = own_piece if r == 1 else at_slot(source, held)
                to = dev(s, y, c, jnp.minimum(t + 1, rows - 1) if right else jnp.maximum(t - 1, 0))
                pair.append(net.wire(src, at_slot(source, lands), to, inside, comes))
            rounds.append(pair)
        return rounds

    def heads_slot(source, step):
        return wa.at[:, lax.rem(source + rows, 2), s, y]

    wa_z = along(wa.at[:, lax.rem(t, 2), s, y], heads_slot, lambda source: lax.div(source, 2) == c)
    up_z = along(wup_in.at[s, y, :, lanes_c], lambda source, step: wup.at[step, s, y])
    down_z = along(wdown_in.at[c, s, y], lambda source, step: wdown.at[step, s, y])

    class Relay:
        def __init__(self, k_, at_one, at_two, x_first, when=None):
            self.k, self.when = k_, when
            self.one = net.wire(at_one, at_one, x_nbr if x_first else y_nbr, when, when)
            self.two = net.wire(at_two, at_two, y_nbr if x_first else x_nbr, when, when)

        def at_round(self, r, act):
            if r == self.k:
                pl.when(t + self.k < rows)(act)
            if r == rows - self.k:
                pl.when(t + self.k >= rows)(act)

        def first_hop(self, r):
            self.at_round(r, self.one.start)

        def second_hop(self, r):
            def act():
                self.one.arrived()
                self.two.start()

            self.at_round(r, act)

    wa_relay, up_relay, down_relay = [], [], []
    for k_ in range(1, rows):
        source = ring(k_)
        slot_of = lax.rem(source, 2)
        wa_relay.append(Relay(
            k_, wa.at[:, slot_of, s, y], wa.at[:, slot_of, :, y], True, lax.div(source, 2) == c,
        ))
        up_relay.append(Relay(k_, wup.at[k_, s, y], wup.at[k_, :, y], True))
        down_relay.append(Relay(k_, wdown.at[k_, s, y], wdown.at[k_, s], False))
    cot_wires = swap(cot_in, cot.at[s])
    cot_mate = net.wire(cot.at[c], cot.at[c], mate)

    bvec[0] = jnp.zeros(bvec.shape[1:], F4)
    bvec[0, 0:1, :] = b_up[...].reshape(1, width)
    shard = b_query.shape[0]

    @pl.when(lax.rem(t, 2) == 0)
    def _():
        bvec[0, 1:2, :shard] = b_query[...].reshape(1, shard)

    @pl.when(lax.rem(t, 2) == 1)
    def _():
        bvec[0, 1:2, shard:2 * shard] = b_query[...].reshape(1, shard)

    for i, vector in enumerate((gain1, bias1, gain2, bias2, b_out, b_down, b_value)):
        vecs[i:i + 1, :vector.shape[0]] = vector[...].reshape(1, vector.shape[0])
    row_ids = lax.broadcasted_iota(jnp.int32, seg.shape, 0)
    seg_row = jnp.sum(jnp.where(row_ids == t, seg[...], 0), axis=0, keepdims=True)
    segint[0] = jnp.broadcast_to(seg_row, segint.shape[1:])
    for own in wa_own:
        own.arrived()
    for group in (wa_z[0], up_z[0], down_z[0]):
        for wire in group:
            wire.start()
    seg_wire.start()
    for wire in bvec_wires:
        wire.start()
    for own in (wval_own, up_own, down_own):
        own.start()

    paths = ((wa_z, wa_relay), (up_z, up_relay), (down_z, down_relay))

    def hop(r):
        for wires, relays in paths:
            for wire in wires[r - 1]:
                wire.arrived()
            if r < rows - 1:
                for wire in wires[r]:
                    wire.start()
            for relay in relays:
                relay.first_hop(r)

    def second_hop(r):
        for _, relays in paths:
            for relay in relays:
                relay.second_hop(r)

    hop(1)
    hop(2)
    start_all(token_wires)
    second_hop(1)
    seg_wire.arrived()
    chosen = jnp.where(same, segint[0], segint[1]).astype(F4)
    segrow[...] = chosen
    for part in range(length // 128):
        piece = jnp.broadcast_to(chosen[0:1, part * 128:(part + 1) * 128], (128, 128))
        segcol[part * 128:(part + 1) * 128, :] = piece.T
    hop(3)
    second_hop(2)
    sent_all([group[0] for group in token_wires[1:]])
    for wire in first_wires:
        wire.start()
    first_own.start()

    n1_wires = []
    for step in range(rows):
        place = ring(-step)
        for wire in token_wires[step]:
            wire.arrived()
        unit, _ = norm_stats(x_own[place].astype(F4))
        n1[c, place] = (unit * vecs[0:1, :] + vecs[1:2, :]).astype(BF)
        wire = net.wire(n1.at[c, place], n1.at[c, place], mate)
        wire.start()
        n1_wires.append(wire)
    second_hop(3)
    for relay in wa_relay:
        relay.two.arrived()
    wval_own.arrived()
    for wire in bvec_wires:
        wire.arrived()
    for wire in n1_wires:
        wire.arrived()

    heads_width = q.shape[1]
    factor = HEAD_DIM ** (-0.5)
    b_q = (bvec[lax.rem(2 * c + rows - t, rows), 1:2, :heads_width]
           + bvec[lax.rem(2 * c + 1 + rows - t, rows), 1:2, :heads_width])
    wq, wk, wo = (wa.at[i] for i in range(3))

    def flat(ref_value):
        return ref_value.reshape(-1, ref_value.shape[-1])

    per_half = half // QB
    per_blk = QB // blk

    def n1_rows(i):
        return flat(n1[lax.div(i, per_half), pl.ds(lax.rem(i, per_half) * per_blk, per_blk)])

    def project_in(i, carry):
        at = pl.ds(pl.multiple_of(i * QB, QB), QB)
        block = n1_rows(i)
        q[at, :] = ((dot_nt(block, flat(wq[...])) + b_q) * factor).astype(BF)
        k_block = dot_nt(block, flat(wk[...]))
        k[at, :] = k_block.astype(BF)
        return carry

    lax.fori_loop(0, length // QB, project_in, 0)
    sent_all(first_wires)
    start_all(cot_wires)


    @pl.when(c == 0)
    def _():
        def fresh(i, carry):
            got = (dot(n1_rows(i), wval[...]) + vecs[6:7, :heads_width]).astype(BF)
            v[pl.ds(i * per_blk, per_blk)] = got.reshape(per_blk, blk, heads_width)
            return carry

        lax.fori_loop(0, length // QB, fresh, 0)

    @pl.when(c == 1)
    def _():
        first_arrived()

    pairs = heads_width // 128
    n_q = length // QB
    lane = lax.broadcasted_iota(jnp.int32, (1, 128), 1)
    keeps = (lane < HEAD_DIM, lane >= HEAD_DIM)

    def attend(j, bias, lsecol):
        count = (j + 1) * QB
        at = slice(j * QB, count)
        key_pos = lax.broadcasted_iota(jnp.int32, (QB, count), 1)
        query_pos = j * QB + lax.broadcasted_iota(jnp.int32, (QB, count), 0)
        allowed = (segcol[at, 0:1] == segrow[0:1, :count]) & (key_pos <= query_pos)
        bias[:, :count] = jnp.where(allowed, 0.0, far_below)
        lsecol[...] = jnp.zeros_like(lsecol)

        def pair(hp, carry):
            lanes = pl.ds(pl.multiple_of(hp * 128, 128), 128)
            q_pair = q[at, lanes]
            k_pair = k[:count, lanes]
            v_pair = flat(v[:count // blk, :, lanes])
            total = None
            for i in range(2):
                scores = dot_nt(q_pair, jnp.where(keeps[i], k_pair, 0.0)) + bias[:, :count]
                top = jnp.max(scores, axis=1, keepdims=True)
                weights = jnp.exp(scores - top)
                norm = jnp.sum(weights, axis=1, keepdims=True)
                part = dot(weights.astype(BF), jnp.where(keeps[i], v_pair, 0.0)) * (1.0 / norm)
                total = part if total is None else total + part
                lsecol[...] = jnp.where(lane == 2 * hp + i, top + jnp.log(norm), lsecol[...])
            att[at, lanes] = total.astype(BF)
            return carry

        lax.fori_loop(0, pairs, pair, 0)
        lse[:, at] = lsecol[...].T[:lse.shape[0], :]

    def attention(bias, lsecol):
        for j in range(n_q):
            attend(j, bias, lsecol)

    pl.run_scoped(attention, pltpu.VMEM((QB, length), F4), pltpu.VMEM((QB, 128), F4))

    att_wire = net.wire(xs.at[0], xr.at[0], mate)

    def half_rows(h, i):
        return pl.ds(pl.multiple_of(h * half + i * QB, QB), QB)

    def out_proj(i, carry):
        part = dot(att[half_rows(cn, i), :], flat(wo[...]))
        xs[0, pl.ds(i * QB, QB), :] = part.astype(BF)
        return carry

    lax.fori_loop(0, per_half, out_proj, 0)
    att_wire.start()

    def out_proj_mine(i, carry):
        mine[pl.ds(i * QB, QB), :] = dot(att[half_rows(c, i), :], flat(wo[...]))
        return carry

    lax.fori_loop(0, per_half, out_proj_mine, 0)
    att_wire.arrived()

    n2_wires = []
    for i in range(rows):
        at = slice(i * blk, (i + 1) * blk)
        middle = x_own[i].astype(F4) + mine[at, :] + xr[0, at, :].astype(F4) + vecs[4:5, :]
        mid[at, :] = middle
        unit, _ = norm_stats(middle)
        n2[c, i] = (unit * vecs[2:3, :] + vecs[3:4, :]).astype(BF)
        wire = net.wire(n2.at[c, i], n2.at[c, i], mate)
        wire.start()
        n2_wires.append(wire)
    up_own.arrived()
    down_own.arrived()
    for relay in up_relay + down_relay:
        relay.two.arrived()

    hid = wup.shape[-1]
    back_wire = net.wire(xs.at[1], xr.at[1], mate)
    mlp_wire = net.wire(xs.at[2], xr.at[2], mate)
    out_wires = swap(out_s, out)
    gm_wires = [net.wire(gm.at[c, i], gm.at[c, i], mate) for i in range(rows)]
    order = tuple(range(1, rows)) + (0,)

    class Reduce:
        def __init__(self, grad, one, two, z, p, y_first):
            self.grad, self.p, self.y_first = grad, p, y_first
            self.got_one, self.got_two, self.z = one, two, None
            if y_first:
                self.one = net.wire(grad.at[p, :, yn], one.at[p], y_nbr)
                self.two = net.wire(grad.at[p, sn, y], two.at[p], x_nbr)
            else:
                self.one = net.wire(grad.at[p, sn], one.at[p], x_nbr)
                self.two = net.wire(grad.at[p, s, yn], two.at[p], y_nbr)
            if p:
                self.z = net.wire(grad.at[p, s, y], z.at[p], dev(s, y, c, ring(p)))

        def run(self, stage):
            grad, p = self.grad, self.p
            if stage == 1:
                self.one.arrived()
                if self.y_first:
                    grad[p, :, y] = add(grad[p, :, y], self.got_one[p])
                else:
                    grad[p, s] = add(grad[p, s], self.got_one[p])
                self.two.start()
            else:
                self.two.arrived()
                grad[p, s, y] = add(grad[p, s, y], self.got_two[p])
                if p:
                    self.z.start()

    def add(one, two):
        return (one.astype(F4) + two.astype(F4)).astype(BF)

    down_rs = [Reduce(gdown, down_r1, down_r2, down_r3, p, True) for p in range(rows)]
    up_rs = [Reduce(gup, up_r1, up_r2, up_r3, p, p == 0) for p in range(rows)]

    class Small:
        def __init__(self, group):
            self.group = group
            self.here = 4 * s + 2 * y + c
            mine_at = small_p.at[group, self.here]
            self.plane = []
            for ds in range(2):
                for dy in range(2):
                    for dc in range(2):
                        if ds or dy or dc:
                            to = dev(lax.rem(s + ds, 2), lax.rem(y + dy, 2), lax.rem(c + dc, 2), t)
                            self.plane.append(net.wire(mine_at, mine_at, to))
            at_z = small_z.at[group, t]
            self.z = [net.wire(at_z, at_z, dev(s, y, c, ring(step))) for step in range(1, rows)]

        def run(self, stage):
            group = self.group
            if stage == 0:
                small_p[group, self.here] = small[group]
                for wire in self.plane:
                    wire.start()
            elif stage == 1:
                for wire in self.plane:
                    wire.arrived()
                total = small_p[group, 0]
                for i in range(1, 8):
                    total = total + small_p[group, i]
                small_z[group, t] = total
                for wire in self.z:
                    wire.start()
            else:
                for wire in self.z:
                    wire.arrived()
                f_small[8 * group:8 * group + 8, :] = (
                    (small_z[group, 0] + small_z[group, 1]) + (small_z[group, 2] + small_z[group, 3])
                )

    small_sums = [Small(0), Small(1)]
    gelu_scale = math.sqrt(2.0 / math.pi)

    def feed_forward(act, ghid, bup_sum, back_own):
        bup_sum[...] = jnp.zeros_like(bup_sum)

        def forward(h, i, keep):
            at = half_rows(h, i)
            n2_block = flat(n2[h, pl.ds(i * per_blk, per_blk)])
            mlp = None
            for p in range(rows):
                cols = slice(p * hid, (p + 1) * hid)
                z = dot(n2_block, flat(wup[p])) + bvec[p, 0:1, lanes_c]
                z2 = z * z
                th = jnp.tanh(gelu_scale * z * (1.0 + 0.044715 * z2))
                cdf = 0.5 * (1.0 + th)
                a = (z * cdf).astype(BF)
                slope = cdf + 0.5 * z * (1.0 - th * th) * (gelu_scale * (1.0 + 3 * 0.044715 * z2))
                act[at, cols] = a
                ghid[at, cols] = slope.astype(BF)
                part = dot(a, flat(wdown[p]))
                mlp = part if mlp is None else mlp + part
            to = pl.ds(pl.multiple_of(i * QB, QB), QB)
            if keep:
                mine[to, :] = mlp
            else:
                xs[2, to, :] = mlp.astype(BF)

        def backward(h, i, keep):
            at = half_rows(h, i)
            cot_block = flat(cot[h, pl.ds(i * per_blk, per_blk)])
            back = None
            for p in range(rows):
                cols = slice(p * hid, (p + 1) * hid)
                g = (dot_nt(cot_block, flat(wdown[p])) * ghid[at, cols].astype(F4)).astype(BF)
                ghid[at, cols] = g
                bup_sum[0:1, cols] += jnp.sum(g.astype(F4), axis=0, keepdims=True)
                part = dot_nt(g, flat(wup[p]))
                back = part if back is None else back + part
            to = pl.ds(pl.multiple_of(i * QB, QB), QB)
            if keep:
                back_own[to, :] = back
            else:
                xs[1, to, :] = back.astype(BF)

        def each(step, h, keep):
            def body(i, carry):
                step(h, i, keep)
                return carry

            lax.fori_loop(0, per_half, body, 0)

        each(forward, c, True)
        for wire in n2_wires:
            wire.arrived()
        arrived_all(cot_wires)
        cot_mate.start()
        each(forward, cn, False)
        mlp_wire.start()
        cot_mate.arrived()

        for p in order:
            got = dot_tn(act[:, p * hid:(p + 1) * hid], flat(cot[...]))
            gdown[p] = got.astype(BF).reshape(gdown.shape[1:])
            down_rs[p].one.start()
        each(backward, c, True)
        mlp_wire.arrived()
        for i in range(rows):
            at = slice(i * blk, (i + 1) * blk)
            out_s[i] = (mid[at, :] + mine[at, :] + xr[2, at, :].astype(F4) + vecs[5:6, :]).astype(BF)
        start_all(out_wires)
        each(backward, cn, False)
        back_wire.start()
        for p in order:
            for m in range(2):
                n2_part = flat(n2[:, :, :, m * (width // 2):(m + 1) * (width // 2)])
                got = dot_tn(n2_part, ghid[:, p * hid:(p + 1) * hid])
                gup[p, m] = got.astype(BF).reshape(gup.shape[2:])
            up_rs[p].one.start()
        small[...] = jnp.zeros_like(small)
        for p in range(rows):
            small[1, pl.ds(ring(p), 1), lanes_c] = bup_sum[0:1, p * hid:(p + 1) * hid]

        back_wire.arrived()
        sums = [jnp.zeros((1, width), F4) for _ in range(4)]
        for i in range(rows):
            at = slice(i * blk, (i + 1) * blk)
            middle = mid[at, :]
            unit, inverse = norm_stats(middle)
            back = back_own[at, :] + xr[1, at, :].astype(F4)
            cot_block = cot[c, i].astype(F4)
            g_middle = cot_block + norm_back(back, unit, inverse, vecs[2:3, :])
            mid[at, :] = g_middle
            g_low = g_middle.astype(BF)
            gm[c, i] = g_low
            gm_wires[i].start()
            for n, item in enumerate((back * unit, back, g_low.astype(F4), cot_block)):
                sums[n] += jnp.sum(item, axis=0, keepdims=True)
        for n in range(4):
            small[1, 4 + n:5 + n, :] = sums[n]
        small_sums[1].run(0)

    pl.run_scoped(
        feed_forward,
        pltpu.VMEM((length, rows * hid), BF),
        pltpu.VMEM((length, rows * hid), BF),
        pltpu.VMEM((8, rows * hid), F4),
        pltpu.VMEM((half, width), F4),
    )

    plane = ((x_nbr, sn, y), (y_nbr, s, yn), (diag, sn, yn))

    class Gather:
        def __init__(self, parts, grad, got, total, at_own, at_core):
            self.parts, self.grad, self.got, self.total = parts, grad, got, total
            self.keep = net.own(total, at_own)
            self.ag = [net.wire(total, at_own, to) for to, _, _ in plane]
            self.over = net.wire(at_core, at_core, mate)

        def run(self, stage):
            if stage == 0:
                for p in range(1, rows):
                    self.parts[p].z.arrived()
                total = self.grad[0, s, y].astype(F4)
                for p in range(1, rows):
                    total += self.got[p].astype(F4)
                self.total[...] = total.astype(BF)
                self.keep.start()
                for wire in self.ag:
                    wire.start()
            elif stage == 1:
                self.keep.arrived()
                for wire in self.ag:
                    wire.arrived()
                self.over.start()
            else:
                self.over.arrived()

    up_end = Gather(up_rs, gup, up_r3, f_s.at[0], f_up.at[s, y, :, lanes_c], f_up.at[:, :, :, lanes_c])
    down_end = Gather(down_rs, gdown, down_r3, f_t, f_down.at[c, s, y], f_down.at[c])

    back1_wire = net.wire(xs.at[0], xr.at[0], mate)
    gtok_wires = swap(out_s, gtok)
    gfirst_slot = net.recv_slots(rows)
    gfirst_wires = []
    for h in range(2):
        for step in range(rows):
            j = ring(step)
            to_me = (c == 1) & (s == h) & (s == 1) if step == 0 else None
            fine = (c == 1) & jnp.logical_not(to_me) if step == 0 else c == 1
            gfirst_wires.append(net.wire(
                gv_s.at[h * rows + j], gfirst.at[t], dev(h, y, s, j), fine, None, gfirst_slot + step,
            ))
    gfirst_own = net.own(gv_s.at[rows + t], gfirst.at[t], (c == 1) & (s == 1))
    class Heads:
        def __init__(self, first_one, count, x_first):
            self.part = part = pl.ds(first_one, count)
            self.x_first = x_first
            if x_first:
                self.one = net.wire(gwa.at[part, :, sn], wa_r1.at[part], x_nbr)
                self.two = net.wire(gwa.at[part, :, s, yn], wa_r2.at[part], y_nbr)
            else:
                self.one = net.wire(gwa.at[part, :, :, yn], wa_r1.at[part], y_nbr)
                self.two = net.wire(gwa.at[part, :, sn, y], wa_r2.at[part], x_nbr)
            self.rz = []
            for step in range(1, rows):
                to = ring(step)
                self.rz.append(net.wire(
                    gwa.at[part, lax.rem(to, 2), s, y], wa_r3.at[step, part], dev(s, y, c, to),
                    lax.div(to, 2) == c, home,
                ))
            self.keep = net.own(f_w.at[part], f_wa.at[part, s, y], home)
            self.ag = [net.wire(f_w.at[part], f_wa.at[part, s, y], to, home, home) for to, _, _ in plane]
            self.over = net.wire(f_wa.at[part], f_wa.at[part], mate, home, away)

        def run(self, stage):
            part = self.part
            if stage == 0:
                self.one.start()
            elif stage == 0.5:
                self.one.arrived()
                if self.x_first:
                    gwa[part, :, s] = add(gwa[part, :, s], wa_r1[part])
                else:
                    gwa[part, :, :, y] = add(gwa[part, :, :, y], wa_r1[part])
                self.two.start()
            elif stage == 1:
                self.two.arrived()
                gwa[part, :, s, y] = add(gwa[part, :, s, y], wa_r2[part])
                for wire in self.rz:
                    wire.start()
            elif stage == 2:
                @pl.when(home)
                def _():
                    for wire in self.rz:
                        wire.copy.wait_recv()
                    total = gwa[part, lax.rem(t, 2), s, y].astype(F4)
                    for i in range(1, rows):
                        total += wa_r3[i, part].astype(F4)
                    f_w[part] = total.astype(BF)

                self.keep.start()
                for wire in self.ag:
                    wire.start()
            elif stage == 3:
                self.keep.arrived()
                for wire in self.ag:
                    wire.arrived()
                self.over.start()
            else:
                self.over.arrived()

    heads_out, heads_q, heads_k = Heads(2, 1, False), Heads(0, 1, True), Heads(1, 1, False)
    lead, follow = c == 0, c == 1
    wv_rs = [net.wire(gwv.at[ds, dy], wv_r1.at[i], to, lead, lead) for i, (to, ds, dy) in enumerate(plane)]
    wv_rz = [
        net.wire(wv_r3.at[t], wv_r3.at[t], dev(s, y, c, ring(step)), lead, lead) for step in range(1, rows)
    ]
    wv_own_f = net.own(f_v, f_wv.at[s, y], lead)
    wv_ag = [net.wire(f_v, f_wv.at[s, y], to, lead, lead) for to, _, _ in plane]
    wv_over = net.wire(f_wv, f_wv, mate, lead, follow)

    def fresh_reduce(stage):
        if stage == 0:
            for wire in wv_rs:
                wire.start()
        elif stage == 1:
            @pl.when(lead)
            def _():
                for wire in wv_rs:
                    wire.copy.wait_recv()
                total = gwv[s, y].astype(F4)
                for i in range(3):
                    total += wv_r1[i].astype(F4)
                wv_r3[t] = total.astype(BF)

            for wire in wv_rz:
                wire.start()
        elif stage == 2:
            @pl.when(lead)
            def _():
                for wire in wv_rz:
                    wire.copy.wait_recv()
                parts = [wv_r3[i].astype(F4) for i in range(rows)]
                f_v[...] = ((parts[0] + parts[1]) + (parts[2] + parts[3])).astype(BF)

            wv_own_f.start()
            for wire in wv_ag:
                wire.start()
        elif stage == 3:
            wv_own_f.arrived()
            for wire in wv_ag:
                wire.arrived()
            wv_over.start()
        else:
            wv_over.arrived()

    heads_here = heads_width // HEAD_DIM
    pick_head = lax.broadcasted_iota(jnp.int32, (lse.shape[0], heads_width), 1) // HEAD_DIM
    pick = (pick_head == lax.broadcasted_iota(jnp.int32, pick_head.shape, 0)).astype(BF)

    def attention_back(gk, gv, delta, tmp, gq, kt, gqt, bias_t):
        kt[...] = k[...].T
        gk[...] = jnp.zeros_like(gk)
        gv[...] = jnp.zeros_like(gv)

        def grad_att(h, i):
            at = half_rows(h, i)
            block = flat(gm[h, pl.ds(i * per_blk, per_blk)])
            low = dot_nt(block, flat(wo[...])).astype(BF)
            gatt[at, :] = low
            product = low.astype(F4) * att[at, :].astype(F4)
            high = product.astype(BF)
            rest_of = (product - high.astype(F4)).astype(BF)
            delta[:, at] = dot_nt(pick, high) + dot_nt(pick, rest_of)

        def grad_att_mine(i, carry):
            grad_att(c, i)
            return carry

        def grad_att_mate(i, carry):
            grad_att(cn, i)
            return carry

        lax.fori_loop(0, per_half, grad_att_mine, 0)
        for wire in gm_wires:
            wire.arrived()
        lax.fori_loop(0, per_half, grad_att_mate, 0)
        gwa[2] = dot_tn(att[...], flat(gm[...])).astype(BF).reshape(gwa.shape[1:])
        heads_out.run(0)
        down_rs[1].run(1)
        down_rs[2].run(1)

        def back_block(j):
            count = (j + 1) * QB
            at = slice(j * QB, count)
            key_pos = lax.broadcasted_iota(jnp.int32, (count, QB), 0)
            query_pos = j * QB + lax.broadcasted_iota(jnp.int32, (count, QB), 1)
            allowed = (segcol[:count, 0:1] == segrow[0:1, at]) & (key_pos <= query_pos)
            bias_t[:count, :] = jnp.where(allowed, 0.0, far_below)

            def pair(hp, carry):
                lanes = pl.ds(pl.multiple_of(hp * 128, 128), 128)
                q_pair = q[at, lanes]
                k_pair = k[:count, lanes]
                v_pair = flat(v[:count // blk, :, lanes])
                ga_pair = gatt[at, lanes]
                sum_k = sum_v = None
                for i in range(2):
                    head = 2 * hp + i
                    scores = dot_nt(jnp.where(keeps[i], k_pair, 0.0), q_pair) + bias_t[:count, :]
                    probs = jnp.exp(scores - lse[pl.ds(head, 1), at])
                    grad_prob = dot_nt(jnp.where(keeps[i], v_pair, 0.0), ga_pair)
                    grad_score = (probs * (grad_prob - delta[pl.ds(head, 1), at])).astype(BF)
                    part_v = dot(probs.astype(BF), jnp.where(keeps[i], ga_pair, 0.0))
                    part_k = dot(grad_score, jnp.where(keeps[i], q_pair, 0.0))
                    sum_v = part_v if sum_v is None else sum_v + part_v
                    sum_k = part_k if sum_k is None else sum_k + part_k
                    channels = pl.ds(pl.multiple_of(hp * 128 + i * HEAD_DIM, HEAD_DIM), HEAD_DIM)
                    gqt[channels, at] = (dot(kt[channels, :count], grad_score) * factor).astype(BF)
                gk[:count, lanes] += sum_k
                gv[:count, lanes] += sum_v
                return carry

            lax.fori_loop(0, pairs, pair, 0)

        for j in range(n_q):
            back_block(j)
            if j == 1:
                down_rs[3].run(1)
                up_rs[1].run(1)
            if j == 2:
                up_rs[2].run(1)
                down_rs[1].run(2)
                down_rs[2].run(2)
            if j == 3:
                down_rs[0].run(1)
                up_rs[3].run(1)
                down_rs[3].run(2)
                up_rs[1].run(2)

        gq[...] = gqt[...].T
        gk_low = gk[...].astype(BF)
        k[...] = gk_low
        gv_s[...] = gv[...].astype(BF).reshape(gv_s.shape)

        n1_all = flat(n1[...])
        gwa[0] = dot(gqt[...], n1_all).astype(BF).reshape(gwa.shape[1:])
        heads_q.run(0)
        gwa[1] = dot_tn(k[...], n1_all).astype(BF).reshape(gwa.shape[1:])
        heads_k.run(0)
        for wire in gfirst_wires:
            wire.start()
        gfirst_own.start()
        small[0, 7:8, lanes_h] = jnp.sum(gq[...].astype(F4), axis=0, keepdims=True)

        @pl.when(lead)
        def _():
            gv_low = flat(gv_s[...])
            gwv[...] = dot_tn(gv_low, n1_all).astype(BF).reshape(gwv.shape)
            small[0, 6:7, :heads_width] = jnp.sum(gv_low.astype(F4), axis=0, keepdims=True)

        fresh_reduce(0)

        def back_rows(h, i):
            at = half_rows(h, i)
            tmp[...] = dot(gq[at, :], flat(wq[...])) + dot(k[at, :], flat(wk[...]))

            @pl.when(lead)
            def _():
                block = flat(gv_s[pl.ds(h * rows + i * per_blk, per_blk)])
                tmp[...] += dot_nt(block, wval[...])

        def back_mate(i, carry):
            back_rows(cn, i)
            xs[0, pl.ds(pl.multiple_of(i * QB, QB), QB), :] = tmp[...].astype(BF)
            return carry

        def back_mine(i, carry):
            back_rows(c, i)
            mine[pl.ds(pl.multiple_of(i * QB, QB), QB), :] = tmp[...]
            return carry

        net.done(att_wire)
        lax.fori_loop(0, per_half, back_mate, 0)
        back1_wire.start()
        lax.fori_loop(0, per_half, back_mine, 0)
        up_rs[0].run(1)
        up_rs[2].run(2)
        heads_out.run(0.5)
        small_sums[1].run(1)
        up_rs[3].run(2)
        down_rs[0].run(2)

    lanes_h = pl.ds(pl.multiple_of(c * heads_width, 128), heads_width)
    pl.run_scoped(
        attention_back,
        pltpu.VMEM((length, heads_width), F4),
        pltpu.VMEM((length, heads_width), F4),
        pltpu.VMEM((lse.shape[0], length), F4),
        pltpu.VMEM((QB, width), F4),
        pltpu.VMEM((length, heads_width), BF),
        pltpu.VMEM((heads_width, length), BF),
        pltpu.VMEM((heads_width, length), BF),
        pltpu.VMEM((length, QB), F4),
    )

    back1_wire.arrived()
    for group in out_wires:
        net.done(group[0])
    out_wires[0][1].arrived()
    gain_sum = jnp.zeros((1, width), F4)
    bias_sum = jnp.zeros((1, width), F4)
    for i in range(rows):
        at = slice(i * blk, (i + 1) * blk)
        unit, inverse = norm_stats(x_own[i].astype(F4))
        back = mine[at, :] + xr[0, at, :].astype(F4)
        gain_sum += jnp.sum(back * unit, axis=0, keepdims=True)
        bias_sum += jnp.sum(back, axis=0, keepdims=True)
        out_s[i] = (mid[at, :] + norm_back(back, unit, inverse, vecs[0:1, :])).astype(BF)
    small[0, 0:1, :] = gain_sum
    small[0, 1:2, :] = bias_sum
    small_sums[0].run(0)

    heads_out.run(1)
    up_rs[0].run(2)
    down_end.run(0)
    heads_q.run(0.5)
    heads_k.run(0.5)
    fresh_reduce(1)
    small_sums[0].run(1)
    heads_q.run(1)
    heads_k.run(1)
    start_all(gtok_wires)
    heads_out.run(2)
    up_end.run(0)
    down_end.run(1)
    fresh_reduce(2)
    heads_q.run(2)
    heads_k.run(2)
    heads_out.run(3)
    up_end.run(1)
    fresh_reduce(3)
    heads_q.run(3)
    heads_k.run(3)
    small_sums[1].run(2)
    small_sums[0].run(2)
    down_end.run(2)
    up_end.run(2)
    heads_out.run(4)
    heads_q.run(4)
    heads_k.run(4)
    fresh_reduce(4)
    for group in out_wires:
        group[0].arrived()
    arrived_all(gtok_wires)
    for step in range(rows):
        def take(step=step):
            pltpu.make_async_remote_copy(
                src_ref=gv_s.at[0], dst_ref=gfirst.at[0], send_sem=send_sems.at[0],
                recv_sem=recv_sems.at[gfirst_slot + step], device_id=mate, device_id_type=MESH,
            ).wait_recv()
        if step == 0:
            pl.when((c == 0) | (s == 0))(take)
        else:
            take()
    gfirst_own.arrived()
    for wire in net.all:
        wire.sent()


def whole_layer(
    tokens, first_values, segment_ids, cotangent, norm1_gain, norm1_bias, w_query, b_query, w_key,
    w_value, b_value, w_out, b_out, norm2_gain, norm2_bias, w_up, b_up, w_down, b_down,
):
    rows, blk, width = tokens.shape
    half = rows * blk
    length = 2 * half
    valf = w_value.shape[1]
    tp_width = w_query.shape[1]
    hid = w_up.shape[1] // 2
    heads = tuple(w.reshape(2, 2, tp_width // 4, width) for w in (w_query.T, w_key.T, w_out))
    hbm = pl.BlockSpec(memory_space=pl.ANY)
    vmem = pl.BlockSpec(memory_space=pltpu.VMEM)
    piece = tp_width // 4
    up_rows, down_rows = width // 4, hid // 4

    def of(*shape, dtype=BF):
        return jax.ShapeDtypeStruct(shape, dtype)

    def room(*shape, dtype=BF):
        return pltpu.VMEM(shape, dtype)

    outs = (
        of(rows, blk, width), of(rows, blk, width), of(rows, blk, valf),
        of(2, 2, up_rows, 2 * hid), of(2, 2, 2, down_rows, width),
        of(3, 2, 2, piece, width), of(2, 2, valf // 4, width), of(16, width, dtype=F4),
    )
    scratch = [
        room(rows, blk, width), room(2, rows, blk, width), room(2, 8, length, dtype=jnp.int32),
        room(8, length, dtype=F4), room(length, 128, dtype=F4), room(8, width, dtype=F4), room(rows, 8, width, dtype=F4),
        room(3, 2, 2, 2, piece, width), room(width, valf),
        room(rows, 2, 2, up_rows, hid), room(rows, 2, 2, down_rows, width),
        room(length, 2 * tp_width), room(length, 2 * tp_width), room(2 * rows, blk, valf),
        room(length, 2 * tp_width), room(16, length, dtype=F4),
        room(half, width, dtype=F4), room(2, rows, blk, width), room(2, rows, blk, width),
        room(half, width, dtype=F4), room(3, half, width), room(3, half, width),
        room(rows, blk, width), room(2, rows, blk, width),
        room(length, 2 * tp_width), room(2 * rows, blk, valf),
        room(rows, 2, 2, up_rows, hid), room(rows, 2, 2, down_rows, width),
        room(rows, 2, up_rows, hid), room(rows, up_rows, hid), room(rows, up_rows, hid),
        room(rows, 2, down_rows, width), room(rows, down_rows, width), room(rows, down_rows, width),
        room(3, 2, 2, 2, piece, width), room(3, 2, 2, piece, width), room(3, 2, piece, width), room(rows, 3, piece, width),
        room(2, 2, valf // 4, width), room(3, valf // 4, width), room(rows, valf // 4, width),
        room(2, 8, width, dtype=F4), room(2, 8, 8, width, dtype=F4), room(2, rows, 8, width, dtype=F4),
        room(1, up_rows, hid), room(down_rows, width), room(3, piece, width), room(valf // 4, width),
        pltpu.SemaphoreType.DMA((SENDS,)), pltpu.SemaphoreType.DMA((RECVS,)), pltpu.SemaphoreType.DMA((OWNS,)),
    ]
    out, gtok, gfirst, f_up, f_down, f_wa, f_wv, f_small = pl.pallas_call(
        layer_kernel,
        out_shape=outs,
        in_specs=[hbm, hbm, hbm, vmem] + [hbm] * 6 + [vmem] * 9,
        out_specs=(hbm,) * 7 + (vmem,),
        scratch_shapes=scratch,
        compiler_params=pltpu.CompilerParams(
            collective_id=0, has_side_effects=True, vmem_limit_bytes=VMEM_BYTES
        ),
    )(
        tokens, first_values, cotangent, segment_ids, *heads,
        w_up.reshape(2, 2, up_rows, 2 * hid), w_down.reshape(2, 2, 2, down_rows, width), w_value,
        norm1_gain, norm1_bias, norm2_gain, norm2_bias, b_out, b_down, b_value, b_query, b_up,
    )
    vector = of(width, dtype=F4)
    results = pl.pallas_call(
        finish_kernel,
        out_shape=(
            of(rows, blk, width), of(rows, blk, valf), of(rows, blk, width, dtype=F4),
            of(width, 2 * hid, dtype=F4), of(2 * hid, width, dtype=F4),
            of(tp_width, width, dtype=F4), of(tp_width, width, dtype=F4), of(tp_width, width, dtype=F4),
            of(width, valf, dtype=F4),
            vector, vector, vector, vector, vector, vector, of(valf, dtype=F4), of(tp_width, dtype=F4), vector,
        ),
        in_specs=[hbm] * 7 + [vmem],
        out_specs=(hbm,) * 9 + (vmem,) * 9,
        scratch_shapes=[
            room(rows, blk, width), room(rows, blk, valf),
            room(rows, blk, width), room(width, 2 * hid), room(2 * hid, width), room(3 * tp_width, width), room(valf, width),
            room(rows, blk, width, dtype=F4), room(width, 2 * hid, dtype=F4), room(2 * hid, width, dtype=F4),
            room(tp_width, width, dtype=F4), room(tp_width, width, dtype=F4), room(tp_width, width, dtype=F4),
            room(width, valf, dtype=F4),
            pltpu.SemaphoreType.DMA((7,)), pltpu.SemaphoreType.DMA((9,)),
        ],
        compiler_params=pltpu.CompilerParams(vmem_limit_bytes=VMEM_BYTES),
    )(
        out, gfirst, gtok, f_up.reshape(width, 2 * hid), f_down.reshape(2 * hid, width),
        f_wa.reshape(3 * tp_width, width), f_wv.reshape(valf, width), f_small,
    )
    (out, gfirst, gtok, grad_up, grad_down, grad_q, grad_k, grad_o, grad_v,
     gain1, bias1, gain2, bias2, grad_b_out, grad_b_down, grad_b_v, grad_b_q, grad_b_up) = results
    return (
        out, gtok, gfirst, gain1, bias1, grad_q.T, grad_b_q, grad_k.T, grad_v, grad_b_v, grad_o, grad_b_out,
        gain2, bias2, grad_up, grad_b_up, grad_down, grad_b_down,
    )


def finish_kernel(
    out, gfirst, gtok, up, down, heads, value, small,
    out_o, gfirst_o, gtok_o, up_o, down_o, q_o, k_o, o_o, value_o,
    gain1, bias1, gain2, bias2, b_out, b_down, b_value, b_query, b_up,
    out_i, gfirst_i, gtok_i, up_i, down_i, heads_i, value_i, gtok_f, up_f, down_f, q_f, k_f, o_f, value_f, in_sems, out_sems,
):
    t = lax.axis_index("tp")
    loads = [
        pltpu.make_async_copy(src, dst, in_sems.at[i])
        for i, (src, dst) in enumerate((
            (up, up_i), (down, down_i), (gtok, gtok_i), (heads, heads_i), (value, value_i), (out, out_i), (gfirst, gfirst_i),
        ))
    ]
    for copy in loads:
        copy.start()
    stores = [
        pltpu.make_async_copy(src, dst, out_sems.at[i])
        for i, (src, dst) in enumerate((
            (up_f, up_o), (down_f, down_o), (gtok_f, gtok_o), (q_f, q_o), (k_f, k_o), (o_f, o_o), (value_f, value_o),
            (out_i, out_o), (gfirst_i, gfirst_o),
        ))
    ]
    for row, ref in enumerate((gain1, bias1)):
        ref[...] = small[row, :]
    for row, ref in enumerate((gain2, bias2, b_out, b_down)):
        ref[...] = small[12 + row, :]
    b_value[...] = small[6, :b_value.shape[0]]
    b_up[...] = small[8 + t, :]
    shard = b_query.shape[0]
    mine = jnp.zeros((1, shard), F4)
    for i in range(small.shape[1] // shard):
        mine = jnp.where(t == i, small[7:8, i * shard:(i + 1) * shard], mine)
    b_query[...] = mine.reshape(shard)
    for i, (src, dst) in enumerate(((up_i, up_f), (down_i, down_f), (gtok_i, gtok_f))):
        loads[i].wait()
        dst[...] = src[...].astype(F4)
        stores[i].start()
    loads[3].wait()
    for i, ref in enumerate((q_f, k_f)):
        ref[...] = heads_i[i * shard:(i + 1) * shard, :].astype(F4)
        stores[3 + i].start()
    o_f[...] = heads_i[2 * shard:3 * shard, :].astype(F4)
    stores[5].start()
    loads[4].wait()
    value_f[...] = value_i[...].astype(F4).T
    stores[6].start()
    for i in range(2):
        loads[5 + i].wait()
        stores[7 + i].start()
    for copy in stores:
        copy.wait()


SENDS = 176
RECVS = 176
OWNS = 20
VMEM_BYTES = 63 * 1024 * 1024


def fits(mesh):
    return mesh.shape["seq"] == 2 and mesh.shape["batch"] == 4 and mesh.shape["tp"] == 4


def solution(mesh):
    placed = (
        P("batch", ("seq", "tp"), None),
        P("batch", ("seq", "tp"), None),
        P("batch", None),
        P("batch", ("seq", "tp"), None),
        P(),
        P(),
        P(None, "tp"),
        P("tp"),
        P(None, "tp"),
        P(),
        P(),
        P("tp", None),
        P(),
        P(),
        P(),
        P(None, "tp"),
        P("tp"),
        P("tp", None),
        P(),
    )
    return jax.shard_map(
        whole_layer if fits(mesh) else on_device,
        mesh=mesh,
        in_specs=placed,
        out_specs=(
            P("batch", ("seq", "tp"), None),
            P("batch", ("seq", "tp"), None),
            P("batch", ("seq", "tp"), None),
            P(),
            P(),
            P(None, "tp"),
            P("tp"),
            P(None, "tp"),
            P(),
            P(),
            P("tp", None),
            P(),
            P(),
            P(),
            P(None, "tp"),
            P("tp"),
            P("tp", None),
            P(),
        ),
        check_vma=False,
    )
```

```python
import math

import jax
import jax.numpy as jnp
from jax import lax
from jax.experimental import pallas as pl
from jax.experimental.pallas import tpu as pltpu
from jax.sharding import PartitionSpec as P

HEADS = 12
HEAD_DIM = 64


eps = 1e-05
block_cap = 256
far_below = -1e30


def from_behind(block, axis, distance):
    devices = range(lax.axis_size(axis))
    route = [((i - distance) % len(devices), i) for i in devices]
    return lax.ppermute(block, axis, route)


def layer_norm(values, norm_gain, norm_bias):
    average = jnp.mean(values, axis=-1, keepdims=True)
    centered = values - average
    inverse = lax.rsqrt(jnp.mean(centered * centered, axis=-1, keepdims=True) + eps)
    unit = centered * inverse
    return (unit * norm_gain + norm_bias, unit, inverse)


def norm_back(grad_result, unit, inverse, norm_gain):
    scaled = grad_result * norm_gain
    return inverse * (
        scaled
        - jnp.mean(scaled, axis=-1, keepdims=True)
        - unit * jnp.mean(scaled * unit, axis=-1, keepdims=True)
    )


def project(values, weight):
    return jnp.einsum("rtd,de->rte", values, weight, preferred_element_type=jnp.float32)


def project_back(grads, weight):
    return jnp.einsum("rte,de->rtd", grads, weight, preferred_element_type=jnp.float32)


def weight_grad(values, grads):
    return jnp.einsum("rtd,rte->de", values, grads, preferred_element_type=jnp.float32)


def column_sum(values):
    return jnp.sum(values, axis=(0, 1), dtype=jnp.float32)


def gelu_tanh(values):
    return jax.nn.gelu(values, approximate=True)


def over_key_blocks(arrays, key_first, state, step, limit):
    count = arrays[0].shape[1]
    width = math.gcd(count, block_cap)

    def one(index, carry):
        offset = index * width
        parts = tuple((lax.dynamic_slice_in_dim(item, offset, width, 1) for item in arrays))
        first_key = key_first + offset

        def taken(inner):
            return step(inner, parts, first_key, offset)

        def skipped(inner):
            return inner

        return lax.cond(first_key <= limit, taken, skipped, carry)

    return lax.fori_loop(0, count // width, one, state)


def on_device(
    tokens,
    first_values,
    segment_ids,
    cotangent,
    norm1_gain,
    norm1_bias,
    w_query,
    b_query,
    w_key,
    w_value,
    b_value,
    w_out,
    b_out,
    norm2_gain,
    norm2_bias,
    w_up,
    b_up,
    w_down,
    b_down,
):
    rows = tokens.shape[0]
    model_width = tokens.shape[2]
    tp_count = lax.axis_size("tp")
    seq_count = lax.axis_size("seq")
    local_len = tokens.shape[1] * tp_count
    heads = w_query.shape[1] // HEAD_DIM
    width_tp = heads * HEAD_DIM
    valf_all = w_value.shape[1]
    factor = HEAD_DIM ** (-0.5)
    seq_index = lax.axis_index("seq")
    head_first = lax.axis_index("tp") * heads
    is_fresh = head_first < HEADS // 2
    fresh_col = jnp.minimum(head_first * HEAD_DIM, valf_all - width_tp)
    reuse_col = jnp.maximum(head_first * HEAD_DIM - valf_all, 0)
    own_first = seq_index * local_len
    own_last = own_first + local_len - 1
    own_pos = own_first + jnp.arange(local_len, dtype=jnp.int32)
    own_seg = lax.dynamic_slice_in_dim(segment_ids, own_first, local_len, 1)

    def masked_scores(query4, key_part, query_pos, query_seg, key_first):
        width = key_part.shape[1]
        scores = (
            jnp.einsum("rqhc,rkhc->rhqk", query4, key_part, preferred_element_type=jnp.float32)
            * factor
        )
        key_seg = lax.dynamic_slice_in_dim(segment_ids, key_first, width, 1)
        key_pos = key_first + jnp.arange(width, dtype=jnp.int32)
        allowed = (query_seg[:, :, None] == key_seg[:, None, :]) & (
            key_pos[None, None, :] <= query_pos[None, :, None]
        )
        return (scores, allowed[:, None])

    resid = tokens.astype(jnp.float32)
    normed_one, unit_one, inverse_one = layer_norm(resid, norm1_gain, norm1_bias)
    rows_one, grad_rows, first_rows = (
        lax.all_gather(normed_one.astype(jnp.bfloat16), "tp", axis=1, tiled=True),
        lax.all_gather(cotangent, "tp", axis=1, tiled=True),
        lax.all_gather(first_values, "tp", axis=1, tiled=True),
    )
    query4 = (
        (project(rows_one, w_query) + b_query)
        .astype(jnp.bfloat16)
        .reshape(rows, local_len, heads, HEAD_DIM)
    )
    keys4 = project(rows_one, w_key).astype(jnp.bfloat16).reshape(rows, local_len, heads, HEAD_DIM)
    w_part = lax.dynamic_slice_in_dim(w_value, fresh_col, width_tp, 1)
    b_part = lax.dynamic_slice_in_dim(b_value, fresh_col, width_tp, 0)

    def fresh_side(normed_rows):
        return (project(normed_rows, w_part) + b_part).astype(jnp.bfloat16)

    def reuse_side(normed_rows):
        return lax.dynamic_slice_in_dim(first_rows, reuse_col, width_tp, 2)

    vals4 = lax.cond(is_fresh, fresh_side, reuse_side, rows_one).reshape(
        rows, local_len, heads, HEAD_DIM
    )

    def stats_step(carry, parts, key_first, offset):
        top, total = carry
        scores, allowed = masked_scores(query4, parts[0], own_pos, own_seg, key_first)
        masked = jnp.where(allowed, scores, far_below)
        new_top = jnp.maximum(top, jnp.max(masked, axis=3))
        weights = jnp.where(allowed, jnp.exp(masked - new_top[..., None]), 0.0)
        return (new_top, total * jnp.exp(top - new_top) + jnp.sum(weights, axis=3))

    start_top = jnp.full((rows, heads, local_len), far_below, jnp.float32)
    start_total = jnp.zeros((rows, heads, local_len), jnp.float32)
    top, total = over_key_blocks(
        (lax.all_gather(keys4, "seq", axis=1, tiled=True),),
        jnp.int32(0),
        (start_top, start_total),
        stats_step,
        own_last,
    )
    lse = top + jnp.log(total)

    def value_step(acc, parts, key_first, offset):
        scores, allowed = masked_scores(query4, parts[0], own_pos, own_seg, key_first)
        weights = jnp.where(allowed, jnp.exp(scores - lse[..., None]), 0.0).astype(jnp.bfloat16)
        return acc + jnp.einsum(
            "rhqk,rkhc->rqhc", weights, parts[1], preferred_element_type=jnp.float32
        )

    zeros_q = jnp.zeros((rows, local_len, heads, HEAD_DIM), jnp.float32)
    attended = over_key_blocks(
        (
            lax.all_gather(keys4, "seq", axis=1, tiled=True),
            lax.all_gather(vals4, "seq", axis=1, tiled=True),
        ),
        jnp.int32(0),
        zeros_q,
        value_step,
        own_last,
    )
    attended_low = attended.astype(jnp.bfloat16).reshape(rows, local_len, width_tp)
    attn_share = lax.psum_scatter(
        project(attended_low, w_out).astype(jnp.bfloat16), "tp", scatter_dimension=1, tiled=True
    ).astype(jnp.float32)
    middle = resid + attn_share + b_out
    normed_two, unit_two, inverse_two = layer_norm(middle, norm2_gain, norm2_bias)
    rows_two = lax.all_gather(normed_two.astype(jnp.bfloat16), "tp", axis=1, tiled=True)
    hidden_pre = project(rows_two, w_up) + b_up
    activated_full, gelu_pull = jax.vjp(gelu_tanh, hidden_pre)
    activated = activated_full.astype(jnp.bfloat16)
    mlp_share = lax.psum_scatter(
        project(activated, w_down).astype(jnp.bfloat16), "tp", scatter_dimension=1, tiled=True
    ).astype(jnp.float32)
    output = (middle + mlp_share + b_down).astype(jnp.bfloat16)
    grad_b_down = column_sum(grad_rows)
    grad_w_down = weight_grad(activated, grad_rows)
    grad_hidden = gelu_pull(project_back(grad_rows, w_down))[0].astype(jnp.bfloat16)
    grad_b_up = column_sum(grad_hidden)
    grad_w_up = weight_grad(rows_two, grad_hidden)
    back_two = lax.psum_scatter(
        project_back(grad_hidden, w_up).astype(jnp.bfloat16), "tp", scatter_dimension=1, tiled=True
    ).astype(jnp.float32)
    grad_gain_two = jnp.sum(back_two * unit_two, axis=(0, 1))
    grad_bias_two = jnp.sum(back_two, axis=(0, 1))
    grad_middle = cotangent.astype(jnp.float32) + norm_back(
        back_two, unit_two, inverse_two, norm2_gain
    )
    grad_mid_rows = lax.all_gather(grad_middle.astype(jnp.bfloat16), "tp", axis=1, tiled=True)
    grad_b_out = column_sum(grad_mid_rows)
    grad_w_out = weight_grad(attended_low, grad_mid_rows)
    grad_out4 = (
        project_back(grad_mid_rows, w_out)
        .astype(jnp.bfloat16)
        .reshape(rows, local_len, heads, HEAD_DIM)
    )
    delta = jnp.einsum("rqhc,rqhc->rhq", grad_out4.astype(jnp.float32), attended)

    def pair_terms(key_side, val_side, key_first, grad_query, grad_keys, grad_vals):

        def pair_step(carry, parts, first, offset):
            acc_query, acc_keys, acc_vals = carry
            key_part, val_part = parts
            width = key_part.shape[1]
            scores, allowed = masked_scores(query4, key_part, own_pos, own_seg, first)
            probs = jnp.where(allowed, jnp.exp(scores - lse[..., None]), 0.0)
            grad_val = jnp.einsum(
                "rhqk,rqhc->rkhc",
                probs.astype(jnp.bfloat16),
                grad_out4,
                preferred_element_type=jnp.float32,
            )
            grad_prob = jnp.einsum(
                "rqhc,rkhc->rhqk", grad_out4, val_part, preferred_element_type=jnp.float32
            )
            grad_score = (probs * (grad_prob - delta[..., None])).astype(jnp.bfloat16)
            acc_query = (
                acc_query
                + jnp.einsum(
                    "rhqk,rkhc->rqhc", grad_score, key_part, preferred_element_type=jnp.float32
                )
                * factor
            )
            grad_key = (
                jnp.einsum(
                    "rhqk,rqhc->rkhc", grad_score, query4, preferred_element_type=jnp.float32
                )
                * factor
            )
            acc_keys = lax.dynamic_update_slice_in_dim(
                acc_keys, lax.dynamic_slice_in_dim(acc_keys, offset, width, 1) + grad_key, offset, 1
            )
            acc_vals = lax.dynamic_update_slice_in_dim(
                acc_vals, lax.dynamic_slice_in_dim(acc_vals, offset, width, 1) + grad_val, offset, 1
            )
            return (acc_query, acc_keys, acc_vals)

        return over_key_blocks(
            (key_side, val_side), key_first, (grad_query, grad_keys, grad_vals), pair_step, own_last
        )

    def turn_keys(turn, carry):
        moving_keys, moving_vals, moving_gk, moving_gv, grad_query = carry
        anchor = (seq_index - turn) % seq_count
        grad_query, moving_gk, moving_gv = pair_terms(
            moving_keys, moving_vals, anchor * local_len, grad_query, moving_gk, moving_gv
        )
        moving_keys, moving_vals, moving_gk, moving_gv = (
            from_behind(moving_keys, "seq", 1),
            from_behind(moving_vals, "seq", 1),
            from_behind(moving_gk.astype(jnp.bfloat16), "seq", 1).astype(moving_gk.dtype),
            from_behind(moving_gv.astype(jnp.bfloat16), "seq", 1).astype(moving_gv.dtype),
        )
        return (moving_keys, moving_vals, moving_gk, moving_gv, grad_query)

    start_state = (keys4, vals4, zeros_q, zeros_q, zeros_q)
    final_state = lax.fori_loop(0, seq_count, turn_keys, start_state)
    grad_keys4, grad_vals4, grad_query4 = (final_state[2], final_state[3], final_state[4])
    grad_query = grad_query4.astype(jnp.bfloat16).reshape(rows, local_len, width_tp)
    grad_keys = grad_keys4.astype(jnp.bfloat16).reshape(rows, local_len, width_tp)
    grad_vals = grad_vals4.astype(jnp.bfloat16).reshape(rows, local_len, width_tp)

    def fresh_back(grad_flat):
        gw_full = lax.dynamic_update_slice_in_dim(
            jnp.zeros((model_width, valf_all), jnp.float32),
            weight_grad(rows_one, grad_flat),
            fresh_col,
            1,
        )
        gb_full = lax.dynamic_update_slice_in_dim(
            jnp.zeros((valf_all,), jnp.float32), column_sum(grad_flat), fresh_col, 0
        )
        back_value = project_back(grad_flat, w_part)
        reuse_full = jnp.zeros((rows, local_len, valf_all), jnp.float32)
        return (gw_full, gb_full, back_value, reuse_full)

    def reuse_back(grad_flat):
        gw_full = jnp.zeros((model_width, valf_all), jnp.float32)
        gb_full = jnp.zeros((valf_all,), jnp.float32)
        back_value = jnp.zeros((rows, local_len, model_width), jnp.float32)
        reuse_full = lax.dynamic_update_slice_in_dim(
            jnp.zeros((rows, local_len, valf_all), jnp.float32),
            grad_flat.astype(jnp.float32),
            reuse_col,
            2,
        )
        return (gw_full, gb_full, back_value, reuse_full)

    grad_w_value, grad_b_value, back_value, reuse_full = lax.cond(
        is_fresh, fresh_back, reuse_back, grad_vals
    )
    grad_b_query = column_sum(grad_query)
    grad_w_query = weight_grad(rows_one, grad_query)
    grad_w_key = weight_grad(rows_one, grad_keys)
    back_terms = project_back(grad_query, w_query) + project_back(grad_keys, w_key) + back_value
    back_one, reuse_sum = (
        lax.psum_scatter(
            back_terms.astype(jnp.bfloat16), "tp", scatter_dimension=1, tiled=True
        ).astype(jnp.float32),
        lax.psum_scatter(
            reuse_full.astype(jnp.bfloat16), "tp", scatter_dimension=1, tiled=True
        ).astype(jnp.float32),
    )
    grad_first_values = reuse_sum.astype(jnp.bfloat16)
    grad_gain_one = jnp.sum(back_one * unit_one, axis=(0, 1))
    grad_bias_one = jnp.sum(back_one, axis=(0, 1))
    grad_tokens = grad_middle + norm_back(back_one, unit_one, inverse_one, norm1_gain)
    summed = lax.psum(
        (
            grad_w_query,
            grad_w_key,
            grad_w_out,
            grad_w_up,
            grad_w_down,
            grad_b_query,
            grad_b_out,
            grad_b_up,
            grad_b_down,
        ),
        ("seq", "batch"),
    )
    norm_sums = lax.psum(
        (grad_gain_one, grad_bias_one, grad_gain_two, grad_bias_two, grad_w_value, grad_b_value),
        ("seq", "batch", "tp"),
    )
    return (
        output,
        grad_tokens,
        grad_first_values,
        norm_sums[0],
        norm_sums[1],
        summed[0],
        summed[5],
        summed[1],
        norm_sums[4],
        norm_sums[5],
        summed[2],
        summed[6],
        norm_sums[2],
        norm_sums[3],
        summed[3],
        summed[7],
        summed[4],
        summed[8],
    )


BF = jnp.bfloat16
F4 = jnp.float32
MESH = pl.DeviceIdType.MESH
QB = 256


def dot(a, b):
    return lax.dot_general(a, b, (((1,), (0,)), ((), ())), preferred_element_type=F4)


def dot_nt(a, b):
    return lax.dot_general(a, b, (((1,), (1,)), ((), ())), preferred_element_type=F4)


def dot_tn(a, b):
    return lax.dot_general(a, b, (((0,), (0,)), ((), ())), preferred_element_type=F4)


def maybe(cond, act):
    if cond is None:
        act()
    else:
        pl.when(cond)(act)


class Wire:
    def __init__(self, copy, send_if=None, recv_if=None):
        self.copy, self.send_if, self.recv_if = copy, send_if, recv_if

    def start(self):
        maybe(self.send_if, self.copy.start)

    def arrived(self):
        maybe(self.recv_if, self.copy.wait_recv)

    def sent(self):
        maybe(self.send_if, self.copy.wait_send)


class Own:
    def __init__(self, copy, when=None):
        self.copy, self.when = copy, when

    def start(self):
        maybe(self.when, self.copy.start)

    def arrived(self):
        maybe(self.when, self.copy.wait)

    def sent(self):
        pass


class Net:
    def __init__(self, send_sems, recv_sems, own_sems):
        self.send_sems, self.recv_sems, self.own_sems = send_sems, recv_sems, own_sems
        self.n_send = self.n_recv = self.n_own = 0
        self.all = []

    def recv_slots(self, count):
        self.n_recv += count
        return self.n_recv - count

    def wire(self, src, dst, device, send_if=None, recv_if=None, slot=None):
        if slot is None:
            slot = self.recv_slots(1)
        copy = pltpu.make_async_remote_copy(
            src_ref=src,
            dst_ref=dst,
            send_sem=self.send_sems.at[self.n_send],
            recv_sem=self.recv_sems.at[slot],
            device_id=device,
            device_id_type=MESH,
        )
        self.n_send += 1
        made = Wire(copy, send_if, recv_if)
        self.all.append(made)
        return made

    def done(self, wire):
        wire.sent()
        self.all = [item for item in self.all if item is not wire]

    def own(self, src, dst, when=None):
        copy = pltpu.make_async_copy(src, dst, self.own_sems.at[self.n_own])
        self.n_own += 1
        return Own(copy, when)


def norm_stats(values):
    average = jnp.mean(values, axis=-1, keepdims=True)
    centered = values - average
    inverse = lax.rsqrt(jnp.mean(centered * centered, axis=-1, keepdims=True) + eps)
    return centered * inverse, inverse


def layer_kernel(
    tokens, first, cot_in, seg, wq_in, wk_in, wo_in, wup_in, wdown_in, wval_in,
    gain1, bias1, gain2, bias2, b_out, b_down, b_value, b_query, b_up,
    out, gtok, gfirst, f_up, f_down, f_wa, f_wv, f_small,
    x_own, n1, segint, segrow, segcol, vecs, bvec, wa, wval, wup, wdown,
    q, k, v, att, lse, mid, n2, cot,
    mine, xs, xr, out_s, gm, gatt, gv_s,
    gup, gdown, up_r1, up_r2, up_r3, down_r1, down_r2, down_r3,
    gwa, wa_r1, wa_r2, wa_r3, gwv, wv_r1, wv_r3,
    small, small_p, small_z, f_s, f_t, f_w, f_v,
    send_sems, recv_sems, own_sems,
):
    s, b, t = lax.axis_index("seq"), lax.axis_index("batch"), lax.axis_index("tp")
    y, c = lax.div(b, 2), lax.rem(b, 2)
    sn, yn, cn = 1 - s, 1 - y, 1 - c
    rows, blk, width = tokens.shape
    half = rows * blk
    length = 2 * half
    net = Net(send_sems, recv_sems, own_sems)

    def dev(ds, dy, dc, dt):
        return (ds, 2 * dy + dc, dt)

    def ring(step):
        return lax.rem(t + step + rows, rows)

    x_nbr, y_nbr, diag, mate = dev(sn, y, c, t), dev(s, yn, c, t), dev(sn, yn, c, t), dev(s, y, cn, t)
    home = lax.div(t, 2) == c
    away = lax.div(t, 2) != c
    same, other = s == c, s != c

    wa_own = [net.own(src, wa.at[i, lax.rem(t, 2)], home) for i, src in enumerate((wq_in, wk_in, wo_in))]
    for own in wa_own:
        own.start()

    gate = pltpu.get_barrier_semaphore()
    peers = [(ds, 2 * yn + dc, t) for ds in range(2) for dc in range(2)]
    for ds in range(2):
        for dc in range(2):
            for dt in range(rows):
                if ds or dc or dt:
                    peers.append((lax.rem(s + ds, 2), 2 * y + lax.rem(c + dc, 2), lax.rem(t + dt, rows)))
    for peer in peers:
        pl.semaphore_signal(gate, inc=1, device_id=peer, device_id_type=MESH)
    pl.semaphore_wait(gate, len(peers))

    def swap(src, dst):
        wires = []
        for step in range(rows):
            r = ring(step)
            if step == 0:
                wires.append((
                    net.wire(src.at[r], dst.at[t], dev(c, y, s, r), other, other),
                    net.own(src.at[r], dst.at[t], same),
                ))
            else:
                wires.append((net.wire(src.at[r], dst.at[t], dev(c, y, s, r)),))
        return wires

    def start_all(wires):
        for group in wires:
            for wire in group:
                wire.start()

    def sent_all(wires):
        for wire in wires:
            net.done(wire)

    def arrived_all(wires):
        for group in wires:
            for wire in group:
                wire.arrived()

    seg_wire = net.wire(segint.at[0], segint.at[1], mate)
    bvec_wires = []
    for step in range(1, rows):
        bvec_wires.append(net.wire(bvec.at[0], bvec.at[step], dev(s, y, c, ring(-step))))
    token_wires = swap(tokens, x_own)
    wval_own = net.own(wval_in, wval, c == 0)
    lanes_c = pl.ds(pl.multiple_of(c * (wup.shape[-1]), 128), wup.shape[-1])
    up_own = net.own(wup_in.at[:, :, :, lanes_c], wup.at[0])
    down_own = net.own(wdown_in.at[c], wdown.at[0])

    first_slot = net.recv_slots(2 * rows)
    first_wires = []
    for step in range(rows):
        r = ring(step)
        to = net.wire(
            first.at[r], v.at[s * rows + t], dev(c, y, 1, r),
            (c == 0) | (s == 0) if step == 0 else None, None, first_slot + s * rows + step,
        )
        first_wires.append(to)
    first_own = net.own(first.at[t], v.at[s * rows + t], (c == 1) & (s == 1))

    def first_arrived():
        for source in range(2):
            for step in range(rows):
                def take(source=source, step=step):
                    pltpu.make_async_remote_copy(
                        src_ref=first.at[0], dst_ref=v.at[0], send_sem=send_sems.at[0],
                        recv_sem=recv_sems.at[first_slot + source * rows + step],
                        device_id=mate, device_id_type=MESH,
                    ).wait_recv()
                if source == 1 and step == 0:
                    pl.when(s == 0)(take)
                else:
                    take()
        first_own.arrived()

    def along(own_piece, at_slot, only=None):
        rounds = []
        for r in range(1, rows):
            pair = []
            for right in (True, False):
                source = t - (r - 1) if right else t + (r - 1)
                came = t - r if right else t + r
                inside = (source >= 0) & (t < rows - 1) if right else (source < rows) & (t > 0)
                comes = came >= 0 if right else came < rows
                if only is not None:
                    inside, comes = inside & only(source), comes & only(came)
                held = (rows - r + 1 if right else r - 1) % rows
                lands = rows - r if right else r
                src = own_piece if r == 1 else at_slot(source, held)
                to = dev(s, y, c, jnp.minimum(t + 1, rows - 1) if right else jnp.maximum(t - 1, 0))
                pair.append(net.wire(src, at_slot(source, lands), to, inside, comes))
            rounds.append(pair)
        return rounds

    def heads_slot(source, step):
        return wa.at[:, lax.rem(source + rows, 2), s, y]

    wa_z = along(wa.at[:, lax.rem(t, 2), s, y], heads_slot, lambda source: lax.div(source, 2) == c)
    up_z = along(wup_in.at[s, y, :, lanes_c], lambda source, step: wup.at[step, s, y])
    down_z = along(wdown_in.at[c, s, y], lambda source, step: wdown.at[step, s, y])

    class Relay:
        def __init__(self, k_, at_one, at_two, x_first, when=None):
            self.k, self.when = k_, when
            self.one = net.wire(at_one, at_one, x_nbr if x_first else y_nbr, when, when)
            self.two = net.wire(at_two, at_two, y_nbr if x_first else x_nbr, when, when)

        def at_round(self, r, act):
            if r == self.k:
                pl.when(t + self.k < rows)(act)
            if r == rows - self.k:
                pl.when(t + self.k >= rows)(act)

        def first_hop(self, r):
            self.at_round(r, self.one.start)

        def second_hop(self, r):
            def act():
                self.one.arrived()
                self.two.start()

            self.at_round(r, act)

    wa_relay, up_relay, down_relay = [], [], []
    for k_ in range(1, rows):
        source = ring(k_)
        slot_of = lax.rem(source, 2)
        wa_relay.append(Relay(
            k_, wa.at[:, slot_of, s, y], wa.at[:, slot_of, :, y], True, lax.div(source, 2) == c,
        ))
        up_relay.append(Relay(k_, wup.at[k_, s, y], wup.at[k_, :, y], True))
        down_relay.append(Relay(k_, wdown.at[k_, s, y], wdown.at[k_, s], False))
    cot_wires = swap(cot_in, cot.at[s])
    cot_mate = net.wire(cot.at[c], cot.at[c], mate)

    bvec[0] = jnp.zeros(bvec.shape[1:], F4)
    bvec[0, 0:1, :] = b_up[...].reshape(1, width)
    shard = b_query.shape[0]

    @pl.when(lax.rem(t, 2) == 0)
    def _():
        bvec[0, 1:2, :shard] = b_query[...].reshape(1, shard)

    @pl.when(lax.rem(t, 2) == 1)
    def _():
        bvec[0, 1:2, shard:2 * shard] = b_query[...].reshape(1, shard)

    for i, vector in enumerate((gain1, bias1, gain2, bias2, b_out, b_down, b_value)):
        vecs[i:i + 1, :vector.shape[0]] = vector[...].reshape(1, vector.shape[0])
    row_ids = lax.broadcasted_iota(jnp.int32, seg.shape, 0)
    seg_row = jnp.sum(jnp.where(row_ids == t, seg[...], 0), axis=0, keepdims=True)
    segint[0] = jnp.broadcast_to(seg_row, segint.shape[1:])
    for own in wa_own:
        own.arrived()
    for group in (wa_z[0], up_z[0], down_z[0]):
        for wire in group:
            wire.start()
    seg_wire.start()
    for wire in bvec_wires:
        wire.start()
    for own in (wval_own, up_own, down_own):
        own.start()

    paths = ((wa_z, wa_relay), (up_z, up_relay), (down_z, down_relay))

    def hop(r):
        for wires, relays in paths:
            for wire in wires[r - 1]:
                wire.arrived()
            if r < rows - 1:
                for wire in wires[r]:
                    wire.start()
            for relay in relays:
                relay.first_hop(r)

    def second_hop(r):
        for _, relays in paths:
            for relay in relays:
                relay.second_hop(r)

    hop(1)
    hop(2)
    start_all(token_wires)
    second_hop(1)
    seg_wire.arrived()
    chosen = jnp.where(same, segint[0], segint[1]).astype(F4)
    segrow[...] = chosen
    for part in range(length // 128):
        piece = jnp.broadcast_to(chosen[0:1, part * 128:(part + 1) * 128], (128, 128))
        segcol[part * 128:(part + 1) * 128, :] = piece.T
    hop(3)
    second_hop(2)
    sent_all([group[0] for group in token_wires[1:]])
    for wire in first_wires:
        wire.start()
    first_own.start()

    n1_wires = []
    for step in range(rows):
        place = ring(-step)
        for wire in token_wires[step]:
            wire.arrived()
        unit, _ = norm_stats(x_own[place].astype(F4))
        n1[c, place] = (unit * vecs[0:1, :] + vecs[1:2, :]).astype(BF)
        wire = net.wire(n1.at[c, place], n1.at[c, place], mate)
        wire.start()
        n1_wires.append(wire)
    second_hop(3)
    for relay in wa_relay:
        relay.two.arrived()
    wval_own.arrived()
    for wire in bvec_wires:
        wire.arrived()
    for wire in n1_wires:
        wire.arrived()

    heads_width = q.shape[1]
    factor = HEAD_DIM ** (-0.5)
    b_q = (bvec[lax.rem(2 * c + rows - t, rows), 1:2, :heads_width]
           + bvec[lax.rem(2 * c + 1 + rows - t, rows), 1:2, :heads_width])
    wq, wk, wo = (wa.at[i] for i in range(3))

    def flat(ref_value):
        return ref_value.reshape(-1, ref_value.shape[-1])

    per_half = half // QB
    per_blk = QB // blk

    def n1_rows(i):
        return flat(n1[lax.div(i, per_half), pl.ds(lax.rem(i, per_half) * per_blk, per_blk)])

    def project_in(i, carry):
        at = pl.ds(pl.multiple_of(i * QB, QB), QB)
        block = n1_rows(i)
        q[at, :] = ((dot_nt(block, flat(wq[...])) + b_q) * factor).astype(BF)
        k_block = dot_nt(block, flat(wk[...]))
        k[at, :] = k_block.astype(BF)
        return carry

    lax.fori_loop(0, length // QB, project_in, 0)
    sent_all(first_wires)
    start_all(cot_wires)


    @pl.when(c == 0)
    def _():
        def fresh(i, carry):
            got = (dot(n1_rows(i), wval[...]) + vecs[6:7, :heads_width]).astype(BF)
            v[pl.ds(i * per_blk, per_blk)] = got.reshape(per_blk, blk, heads_width)
            return carry

        lax.fori_loop(0, length // QB, fresh, 0)

    @pl.when(c == 1)
    def _():
        first_arrived()

    pairs = heads_width // 128
    n_q = length // QB
    lane = lax.broadcasted_iota(jnp.int32, (1, 128), 1)
    keeps = (lane < HEAD_DIM, lane >= HEAD_DIM)

    def attend(j, bias, lsecol):
        count = (j + 1) * QB
        at = slice(j * QB, count)
        key_pos = lax.broadcasted_iota(jnp.int32, (QB, count), 1)
        query_pos = j * QB + lax.broadcasted_iota(jnp.int32, (QB, count), 0)
        allowed = (segcol[at, 0:1] == segrow[0:1, :count]) & (key_pos <= query_pos)
        bias[:, :count] = jnp.where(allowed, 0.0, far_below)
        lsecol[...] = jnp.zeros_like(lsecol)

        def pair(hp, carry):
            lanes = pl.ds(pl.multiple_of(hp * 128, 128), 128)
            q_pair = q[at, lanes]
            k_pair = k[:count, lanes]
            v_pair = flat(v[:count // blk, :, lanes])
            total = None
            for i in range(2):
                scores = dot_nt(q_pair, jnp.where(keeps[i], k_pair, 0.0)) + bias[:, :count]
                top = jnp.max(scores, axis=1, keepdims=True)
                weights = jnp.exp(scores - top)
                norm = jnp.sum(weights, axis=1, keepdims=True)
                part = dot(weights.astype(BF), jnp.where(keeps[i], v_pair, 0.0)) * (1.0 / norm)
                total = part if total is None else total + part
                lsecol[...] = jnp.where(lane == 2 * hp + i, top + jnp.log(norm), lsecol[...])
            att[at, lanes] = total.astype(BF)
            return carry

        lax.fori_loop(0, pairs, pair, 0)
        lse[:, at] = lsecol[...].T[:lse.shape[0], :]

    def attention(bias, lsecol):
        for j in range(n_q):
            attend(j, bias, lsecol)

    pl.run_scoped(attention, pltpu.VMEM((QB, length), F4), pltpu.VMEM((QB, 128), F4))

    att_wire = net.wire(xs.at[0], xr.at[0], mate)

    def half_rows(h, i):
        return pl.ds(pl.multiple_of(h * half + i * QB, QB), QB)

    def out_proj(i, carry):
        part = dot(att[half_rows(cn, i), :], flat(wo[...]))
        xs[0, pl.ds(i * QB, QB), :] = part.astype(BF)
        return carry

    lax.fori_loop(0, per_half, out_proj, 0)
    att_wire.start()

    def out_proj_mine(i, carry):
        mine[pl.ds(i * QB, QB), :] = dot(att[half_rows(c, i), :], flat(wo[...]))
        return carry

    lax.fori_loop(0, per_half, out_proj_mine, 0)
    att_wire.arrived()

    n2_wires = []
    for i in range(rows):
        at = slice(i * blk, (i + 1) * blk)
        middle = x_own[i].astype(F4) + mine[at, :] + xr[0, at, :].astype(F4) + vecs[4:5, :]
        mid[at, :] = middle
        unit, _ = norm_stats(middle)
        n2[c, i] = (unit * vecs[2:3, :] + vecs[3:4, :]).astype(BF)
        wire = net.wire(n2.at[c, i], n2.at[c, i], mate)
        wire.start()
        n2_wires.append(wire)
    up_own.arrived()
    down_own.arrived()
    for relay in up_relay + down_relay:
        relay.two.arrived()

    hid = wup.shape[-1]
    back_wire = net.wire(xs.at[1], xr.at[1], mate)
    mlp_wire = net.wire(xs.at[2], xr.at[2], mate)
    out_wires = swap(out_s, out)
    gm_wires = [net.wire(gm.at[c, i], gm.at[c, i], mate) for i in range(rows)]
    order = tuple(range(1, rows)) + (0,)

    class Reduce:
        def __init__(self, grad, one, two, z, p, y_first):
            self.grad, self.p, self.y_first = grad, p, y_first
            self.got_one, self.got_two, self.z = one, two, None
            if y_first:
                self.one = net.wire(grad.at[p, :, yn], one.at[p], y_nbr)
                self.two = net.wire(grad.at[p, sn, y], two.at[p], x_nbr)
            else:
                self.one = net.wire(grad.at[p, sn], one.at[p], x_nbr)
                self.two = net.wire(grad.at[p, s, yn], two.at[p], y_nbr)
            if p:
                self.z = net.wire(grad.at[p, s, y], z.at[p], dev(s, y, c, ring(p)))

        def run(self, stage):
            grad, p = self.grad, self.p
            if stage == 1:
                self.one.arrived()
                if self.y_first:
                    grad[p, :, y] = add(grad[p, :, y], self.got_one[p])
                else:
                    grad[p, s] = add(grad[p, s], self.got_one[p])
                self.two.start()
            else:
                self.two.arrived()
                grad[p, s, y] = add(grad[p, s, y], self.got_two[p])
                if p:
                    self.z.start()

    def add(one, two):
        return (one.astype(F4) + two.astype(F4)).astype(BF)

    down_rs = [Reduce(gdown, down_r1, down_r2, down_r3, p, True) for p in range(rows)]
    up_rs = [Reduce(gup, up_r1, up_r2, up_r3, p, p == 0) for p in range(rows)]

    class Small:
        def __init__(self, group):
            self.group = group
            self.here = 4 * s + 2 * y + c
            mine_at = small_p.at[group, self.here]
            self.plane = []
            for ds in range(2):
                for dy in range(2):
                    for dc in range(2):
                        if ds or dy or dc:
                            to = dev(lax.rem(s + ds, 2), lax.rem(y + dy, 2), lax.rem(c + dc, 2), t)
                            self.plane.append(net.wire(mine_at, mine_at, to))
            at_z = small_z.at[group, t]
            self.z = [net.wire(at_z, at_z, dev(s, y, c, ring(step))) for step in range(1, rows)]

        def run(self, stage):
            group = self.group
            if stage == 0:
                small_p[group, self.here] = small[group]
                for wire in self.plane:
                    wire.start()
            elif stage == 1:
                for wire in self.plane:
                    wire.arrived()
                total = small_p[group, 0]
                for i in range(1, 8):
                    total = total + small_p[group, i]
                small_z[group, t] = total
                for wire in self.z:
                    wire.start()
            else:
                for wire in self.z:
                    wire.arrived()
                f_small[8 * group:8 * group + 8, :] = (
                    (small_z[group, 0] + small_z[group, 1]) + (small_z[group, 2] + small_z[group, 3])
                )

    small_sums = [Small(0), Small(1)]
    gelu_scale = math.sqrt(2.0 / math.pi)

    def feed_forward(act, ghid, bup_sum, back_own):
        bup_sum[...] = jnp.zeros_like(bup_sum)

        def forward(h, i, keep):
            at = half_rows(h, i)
            n2_block = flat(n2[h, pl.ds(i * per_blk, per_blk)])
            mlp = None
            for p in range(rows):
                cols = slice(p * hid, (p + 1) * hid)
                z = dot(n2_block, flat(wup[p])) + bvec[p, 0:1, lanes_c]
                z2 = z * z
                th = jnp.tanh(gelu_scale * z * (1.0 + 0.044715 * z2))
                cdf = 0.5 * (1.0 + th)
                a = (z * cdf).astype(BF)
                slope = cdf + 0.5 * z * (1.0 - th * th) * (gelu_scale * (1.0 + 3 * 0.044715 * z2))
                act[at, cols] = a
                ghid[at, cols] = slope.astype(BF)
                part = dot(a, flat(wdown[p]))
                mlp = part if mlp is None else mlp + part
            to = pl.ds(pl.multiple_of(i * QB, QB), QB)
            if keep:
                mine[to, :] = mlp
            else:
                xs[2, to, :] = mlp.astype(BF)

        def backward(h, i, keep):
            at = half_rows(h, i)
            cot_block = flat(cot[h, pl.ds(i * per_blk, per_blk)])
            back = None
            for p in range(rows):
                cols = slice(p * hid, (p + 1) * hid)
                g = (dot_nt(cot_block, flat(wdown[p])) * ghid[at, cols].astype(F4)).astype(BF)
                ghid[at, cols] = g
                bup_sum[0:1, cols] += jnp.sum(g.astype(F4), axis=0, keepdims=True)
                part = dot_nt(g, flat(wup[p]))
                back = part if back is None else back + part
            to = pl.ds(pl.multiple_of(i * QB, QB), QB)
            if keep:
                back_own[to, :] = back
            else:
                xs[1, to, :] = back.astype(BF)

        def each(step, h, keep):
            def body(i, carry):
                step(h, i, keep)
                return carry

            lax.fori_loop(0, per_half, body, 0)

        each(forward, c, True)
        for wire in n2_wires:
            wire.arrived()
        arrived_all(cot_wires)
        cot_mate.start()
        each(forward, cn, False)
        mlp_wire.start()
        cot_mate.arrived()

        for p in order:
            got = dot_tn(act[:, p * hid:(p + 1) * hid], flat(cot[...]))
            gdown[p] = got.astype(BF).reshape(gdown.shape[1:])
            down_rs[p].one.start()
        each(backward, c, True)
        mlp_wire.arrived()
        for i in range(rows):
            at = slice(i * blk, (i + 1) * blk)
            out_s[i] = (mid[at, :] + mine[at, :] + xr[2, at, :].astype(F4) + vecs[5:6, :]).astype(BF)
        start_all(out_wires)
        each(backward, cn, False)
        back_wire.start()
        for p in order:
            for m in range(2):
                n2_part = flat(n2[:, :, :, m * (width // 2):(m + 1) * (width // 2)])
                got = dot_tn(n2_part, ghid[:, p * hid:(p + 1) * hid])
                gup[p, m] = got.astype(BF).reshape(gup.shape[2:])
            up_rs[p].one.start()
        small[...] = jnp.zeros_like(small)
        for p in range(rows):
            small[1, pl.ds(ring(p), 1), lanes_c] = bup_sum[0:1, p * hid:(p + 1) * hid]

        back_wire.arrived()
        sums = [jnp.zeros((1, width), F4) for _ in range(4)]
        for i in range(rows):
            at = slice(i * blk, (i + 1) * blk)
            middle = mid[at, :]
            unit, inverse = norm_stats(middle)
            back = back_own[at, :] + xr[1, at, :].astype(F4)
            cot_block = cot[c, i].astype(F4)
            g_middle = cot_block + norm_back(back, unit, inverse, vecs[2:3, :])
            mid[at, :] = g_middle
            g_low = g_middle.astype(BF)
            gm[c, i] = g_low
            gm_wires[i].start()
            for n, item in enumerate((back * unit, back, g_low.astype(F4), cot_block)):
                sums[n] += jnp.sum(item, axis=0, keepdims=True)
        for n in range(4):
            small[1, 4 + n:5 + n, :] = sums[n]
        small_sums[1].run(0)

    pl.run_scoped(
        feed_forward,
        pltpu.VMEM((length, rows * hid), BF),
        pltpu.VMEM((length, rows * hid), BF),
        pltpu.VMEM((8, rows * hid), F4),
        pltpu.VMEM((half, width), F4),
    )

    plane = ((x_nbr, sn, y), (y_nbr, s, yn), (diag, sn, yn))

    class Gather:
        def __init__(self, parts, grad, got, total, at_own, at_core):
            self.parts, self.grad, self.got, self.total = parts, grad, got, total
            self.keep = net.own(total, at_own)
            self.ag = [net.wire(total, at_own, to) for to, _, _ in plane]
            self.over = net.wire(at_core, at_core, mate)

        def run(self, stage):
            if stage == 0:
                for p in range(1, rows):
                    self.parts[p].z.arrived()
                total = self.grad[0, s, y].astype(F4)
                for p in range(1, rows):
                    total += self.got[p].astype(F4)
                self.total[...] = total.astype(BF)
                self.keep.start()
                for wire in self.ag:
                    wire.start()
            elif stage == 1:
                self.keep.arrived()
                for wire in self.ag:
                    wire.arrived()
                self.over.start()
            else:
                self.over.arrived()

    up_end = Gather(up_rs, gup, up_r3, f_s.at[0], f_up.at[s, y, :, lanes_c], f_up.at[:, :, :, lanes_c])
    down_end = Gather(down_rs, gdown, down_r3, f_t, f_down.at[c, s, y], f_down.at[c])

    back1_wire = net.wire(xs.at[0], xr.at[0], mate)
    gtok_wires = swap(out_s, gtok)
    gfirst_slot = net.recv_slots(rows)
    gfirst_wires = []
    for h in range(2):
        for step in range(rows):
            j = ring(step)
            to_me = (c == 1) & (s == h) & (s == 1) if step == 0 else None
            fine = (c == 1) & jnp.logical_not(to_me) if step == 0 else c == 1
            gfirst_wires.append(net.wire(
                gv_s.at[h * rows + j], gfirst.at[t], dev(h, y, s, j), fine, None, gfirst_slot + step,
            ))
    gfirst_own = net.own(gv_s.at[rows + t], gfirst.at[t], (c == 1) & (s == 1))
    class Heads:
        def __init__(self, first_one, count, x_first):
            self.part = part = pl.ds(first_one, count)
            self.x_first = x_first
            if x_first:
                self.one = net.wire(gwa.at[part, :, sn], wa_r1.at[part], x_nbr)
                self.two = net.wire(gwa.at[part, :, s, yn], wa_r2.at[part], y_nbr)
            else:
                self.one = net.wire(gwa.at[part, :, :, yn], wa_r1.at[part], y_nbr)
                self.two = net.wire(gwa.at[part, :, sn, y], wa_r2.at[part], x_nbr)
            self.rz = []
            for step in range(1, rows):
                to = ring(step)
                self.rz.append(net.wire(
                    gwa.at[part, lax.rem(to, 2), s, y], wa_r3.at[step, part], dev(s, y, c, to),
                    lax.div(to, 2) == c, home,
                ))
            self.keep = net.own(f_w.at[part], f_wa.at[part, s, y], home)
            self.ag = [net.wire(f_w.at[part], f_wa.at[part, s, y], to, home, home) for to, _, _ in plane]
            self.over = net.wire(f_wa.at[part], f_wa.at[part], mate, home, away)

        def run(self, stage):
            part = self.part
            if stage == 0:
                self.one.start()
            elif stage == 0.5:
                self.one.arrived()
                if self.x_first:
                    gwa[part, :, s] = add(gwa[part, :, s], wa_r1[part])
                else:
                    gwa[part, :, :, y] = add(gwa[part, :, :, y], wa_r1[part])
                self.two.start()
            elif stage == 1:
                self.two.arrived()
                gwa[part, :, s, y] = add(gwa[part, :, s, y], wa_r2[part])
                for wire in self.rz:
                    wire.start()
            elif stage == 2:
                @pl.when(home)
                def _():
                    for wire in self.rz:
                        wire.copy.wait_recv()
                    total = gwa[part, lax.rem(t, 2), s, y].astype(F4)
                    for i in range(1, rows):
                        total += wa_r3[i, part].astype(F4)
                    f_w[part] = total.astype(BF)

                self.keep.start()
                for wire in self.ag:
                    wire.start()
            elif stage == 3:
                self.keep.arrived()
                for wire in self.ag:
                    wire.arrived()
                self.over.start()
            else:
                self.over.arrived()

    heads_out, heads_q, heads_k = Heads(2, 1, False), Heads(0, 1, True), Heads(1, 1, False)
    lead, follow = c == 0, c == 1
    wv_rs = [net.wire(gwv.at[ds, dy], wv_r1.at[i], to, lead, lead) for i, (to, ds, dy) in enumerate(plane)]
    wv_rz = [
        net.wire(wv_r3.at[t], wv_r3.at[t], dev(s, y, c, ring(step)), lead, lead) for step in range(1, rows)
    ]
    wv_own_f = net.own(f_v, f_wv.at[s, y], lead)
    wv_ag = [net.wire(f_v, f_wv.at[s, y], to, lead, lead) for to, _, _ in plane]
    wv_over = net.wire(f_wv, f_wv, mate, lead, follow)

    def fresh_reduce(stage):
        if stage == 0:
            for wire in wv_rs:
                wire.start()
        elif stage == 1:
            @pl.when(lead)
            def _():
                for wire in wv_rs:
                    wire.copy.wait_recv()
                total = gwv[s, y].astype(F4)
                for i in range(3):
                    total += wv_r1[i].astype(F4)
                wv_r3[t] = total.astype(BF)

            for wire in wv_rz:
                wire.start()
        elif stage == 2:
            @pl.when(lead)
            def _():
                for wire in wv_rz:
                    wire.copy.wait_recv()
                parts = [wv_r3[i].astype(F4) for i in range(rows)]
                f_v[...] = ((parts[0] + parts[1]) + (parts[2] + parts[3])).astype(BF)

            wv_own_f.start()
            for wire in wv_ag:
                wire.start()
        elif stage == 3:
            wv_own_f.arrived()
            for wire in wv_ag:
                wire.arrived()
            wv_over.start()
        else:
            wv_over.arrived()

    heads_here = heads_width // HEAD_DIM
    pick_head = lax.broadcasted_iota(jnp.int32, (lse.shape[0], heads_width), 1) // HEAD_DIM
    pick = (pick_head == lax.broadcasted_iota(jnp.int32, pick_head.shape, 0)).astype(BF)

    def attention_back(gk, gv, delta, tmp, gq, kt, gqt, bias_t):
        kt[...] = k[...].T
        gk[...] = jnp.zeros_like(gk)
        gv[...] = jnp.zeros_like(gv)

        def grad_att(h, i):
            at = half_rows(h, i)
            block = flat(gm[h, pl.ds(i * per_blk, per_blk)])
            low = dot_nt(block, flat(wo[...])).astype(BF)
            gatt[at, :] = low
            product = low.astype(F4) * att[at, :].astype(F4)
            high = product.astype(BF)
            rest_of = (product - high.astype(F4)).astype(BF)
            delta[:, at] = dot_nt(pick, high) + dot_nt(pick, rest_of)

        def grad_att_mine(i, carry):
            grad_att(c, i)
            return carry

        def grad_att_mate(i, carry):
            grad_att(cn, i)
            return carry

        lax.fori_loop(0, per_half, grad_att_mine, 0)
        for wire in gm_wires:
            wire.arrived()
        lax.fori_loop(0, per_half, grad_att_mate, 0)
        gwa[2] = dot_tn(att[...], flat(gm[...])).astype(BF).reshape(gwa.shape[1:])
        heads_out.run(0)
        down_rs[1].run(1)
        down_rs[2].run(1)

        def back_block(j):
            count = (j + 1) * QB
            at = slice(j * QB, count)
            key_pos = lax.broadcasted_iota(jnp.int32, (count, QB), 0)
            query_pos = j * QB + lax.broadcasted_iota(jnp.int32, (count, QB), 1)
            allowed = (segcol[:count, 0:1] == segrow[0:1, at]) & (key_pos <= query_pos)
            bias_t[:count, :] = jnp.where(allowed, 0.0, far_below)

            def pair(hp, carry):
                lanes = pl.ds(pl.multiple_of(hp * 128, 128), 128)
                q_pair = q[at, lanes]
                k_pair = k[:count, lanes]
                v_pair = flat(v[:count // blk, :, lanes])
                ga_pair = gatt[at, lanes]
                sum_k = sum_v = None
                for i in range(2):
                    head = 2 * hp + i
                    scores = dot_nt(jnp.where(keeps[i], k_pair, 0.0), q_pair) + bias_t[:count, :]
                    probs = jnp.exp(scores - lse[pl.ds(head, 1), at])
                    grad_prob = dot_nt(jnp.where(keeps[i], v_pair, 0.0), ga_pair)
                    grad_score = (probs * (grad_prob - delta[pl.ds(head, 1), at])).astype(BF)
                    part_v = dot(probs.astype(BF), jnp.where(keeps[i], ga_pair, 0.0))
                    part_k = dot(grad_score, jnp.where(keeps[i], q_pair, 0.0))
                    sum_v = part_v if sum_v is None else sum_v + part_v
                    sum_k = part_k if sum_k is None else sum_k + part_k
                    channels = pl.ds(pl.multiple_of(hp * 128 + i * HEAD_DIM, HEAD_DIM), HEAD_DIM)
                    gqt[channels, at] = (dot(kt[channels, :count], grad_score) * factor).astype(BF)
                gk[:count, lanes] += sum_k
                gv[:count, lanes] += sum_v
                return carry

            lax.fori_loop(0, pairs, pair, 0)

        for j in range(n_q):
            back_block(j)
            if j == 1:
                down_rs[3].run(1)
                up_rs[1].run(1)
            if j == 2:
                up_rs[2].run(1)
                down_rs[1].run(2)
                down_rs[2].run(2)
            if j == 3:
                down_rs[0].run(1)
                up_rs[3].run(1)
                down_rs[3].run(2)
                up_rs[1].run(2)

        gq[...] = gqt[...].T
        gk_low = gk[...].astype(BF)
        k[...] = gk_low
        gv_s[...] = gv[...].astype(BF).reshape(gv_s.shape)

        n1_all = flat(n1[...])
        gwa[0] = dot(gqt[...], n1_all).astype(BF).reshape(gwa.shape[1:])
        heads_q.run(0)
        gwa[1] = dot_tn(k[...], n1_all).astype(BF).reshape(gwa.shape[1:])
        heads_k.run(0)
        for wire in gfirst_wires:
            wire.start()
        gfirst_own.start()
        small[0, 7:8, lanes_h] = jnp.sum(gq[...].astype(F4), axis=0, keepdims=True)

        @pl.when(lead)
        def _():
            gv_low = flat(gv_s[...])
            gwv[...] = dot_tn(gv_low, n1_all).astype(BF).reshape(gwv.shape)
            small[0, 6:7, :heads_width] = jnp.sum(gv_low.astype(F4), axis=0, keepdims=True)

        fresh_reduce(0)

        def back_rows(h, i):
            at = half_rows(h, i)
            tmp[...] = dot(gq[at, :], flat(wq[...])) + dot(k[at, :], flat(wk[...]))

            @pl.when(lead)
            def _():
                block = flat(gv_s[pl.ds(h * rows + i * per_blk, per_blk)])
                tmp[...] += dot_nt(block, wval[...])

        def back_mate(i, carry):
            back_rows(cn, i)
            xs[0, pl.ds(pl.multiple_of(i * QB, QB), QB), :] = tmp[...].astype(BF)
            return carry

        def back_mine(i, carry):
            back_rows(c, i)
            mine[pl.ds(pl.multiple_of(i * QB, QB), QB), :] = tmp[...]
            return carry

        net.done(att_wire)
        lax.fori_loop(0, per_half, back_mate, 0)
        back1_wire.start()
        lax.fori_loop(0, per_half, back_mine, 0)
        up_rs[0].run(1)
        up_rs[2].run(2)
        heads_out.run(0.5)
        small_sums[1].run(1)
        up_rs[3].run(2)
        down_rs[0].run(2)

    lanes_h = pl.ds(pl.multiple_of(c * heads_width, 128), heads_width)
    pl.run_scoped(
        attention_back,
        pltpu.VMEM((length, heads_width), F4),
        pltpu.VMEM((length, heads_width), F4),
        pltpu.VMEM((lse.shape[0], length), F4),
        pltpu.VMEM((QB, width), F4),
        pltpu.VMEM((length, heads_width), BF),
        pltpu.VMEM((heads_width, length), BF),
        pltpu.VMEM((heads_width, length), BF),
        pltpu.VMEM((length, QB), F4),
    )

    back1_wire.arrived()
    for group in out_wires:
        net.done(group[0])
    out_wires[0][1].arrived()
    gain_sum = jnp.zeros((1, width), F4)
    bias_sum = jnp.zeros((1, width), F4)
    for i in range(rows):
        at = slice(i * blk, (i + 1) * blk)
        unit, inverse = norm_stats(x_own[i].astype(F4))
        back = mine[at, :] + xr[0, at, :].astype(F4)
        gain_sum += jnp.sum(back * unit, axis=0, keepdims=True)
        bias_sum += jnp.sum(back, axis=0, keepdims=True)
        out_s[i] = (mid[at, :] + norm_back(back, unit, inverse, vecs[0:1, :])).astype(BF)
    small[0, 0:1, :] = gain_sum
    small[0, 1:2, :] = bias_sum
    start_all(gtok_wires[:2])
    small_sums[0].run(0)

    heads_out.run(1)
    up_rs[0].run(2)
    down_end.run(0)
    heads_q.run(0.5)
    heads_k.run(0.5)
    fresh_reduce(1)
    small_sums[0].run(1)
    heads_q.run(1)
    heads_k.run(1)
    start_all(gtok_wires[2:])
    heads_out.run(2)
    up_end.run(0)
    down_end.run(1)
    fresh_reduce(2)
    heads_q.run(2)
    heads_k.run(2)
    heads_out.run(3)
    up_end.run(1)
    fresh_reduce(3)
    heads_q.run(3)
    heads_k.run(3)
    small_sums[1].run(2)
    small_sums[0].run(2)
    down_end.run(2)
    up_end.run(2)
    heads_out.run(4)
    heads_q.run(4)
    heads_k.run(4)
    fresh_reduce(4)
    for group in out_wires:
        group[0].arrived()
    arrived_all(gtok_wires)
    for step in range(rows):
        def take(step=step):
            pltpu.make_async_remote_copy(
                src_ref=gv_s.at[0], dst_ref=gfirst.at[0], send_sem=send_sems.at[0],
                recv_sem=recv_sems.at[gfirst_slot + step], device_id=mate, device_id_type=MESH,
            ).wait_recv()
        if step == 0:
            pl.when((c == 0) | (s == 0))(take)
        else:
            take()
    gfirst_own.arrived()
    for wire in net.all:
        wire.sent()


def whole_layer(
    tokens, first_values, segment_ids, cotangent, norm1_gain, norm1_bias, w_query, b_query, w_key,
    w_value, b_value, w_out, b_out, norm2_gain, norm2_bias, w_up, b_up, w_down, b_down,
):
    rows, blk, width = tokens.shape
    half = rows * blk
    length = 2 * half
    valf = w_value.shape[1]
    tp_width = w_query.shape[1]
    hid = w_up.shape[1] // 2
    heads = tuple(w.reshape(2, 2, tp_width // 4, width) for w in (w_query.T, w_key.T, w_out))
    hbm = pl.BlockSpec(memory_space=pl.ANY)
    vmem = pl.BlockSpec(memory_space=pltpu.VMEM)
    piece = tp_width // 4
    up_rows, down_rows = width // 4, hid // 4

    def of(*shape, dtype=BF):
        return jax.ShapeDtypeStruct(shape, dtype)

    def room(*shape, dtype=BF):
        return pltpu.VMEM(shape, dtype)

    outs = (
        of(rows, blk, width), of(rows, blk, width), of(rows, blk, valf),
        of(2, 2, up_rows, 2 * hid), of(2, 2, 2, down_rows, width),
        of(3, 2, 2, piece, width), of(2, 2, valf // 4, width), of(16, width, dtype=F4),
    )
    scratch = [
        room(rows, blk, width), room(2, rows, blk, width), room(2, 8, length, dtype=jnp.int32),
        room(8, length, dtype=F4), room(length, 128, dtype=F4), room(8, width, dtype=F4), room(rows, 8, width, dtype=F4),
        room(3, 2, 2, 2, piece, width), room(width, valf),
        room(rows, 2, 2, up_rows, hid), room(rows, 2, 2, down_rows, width),
        room(length, 2 * tp_width), room(length, 2 * tp_width), room(2 * rows, blk, valf),
        room(length, 2 * tp_width), room(16, length, dtype=F4),
        room(half, width, dtype=F4), room(2, rows, blk, width), room(2, rows, blk, width),
        room(half, width, dtype=F4), room(3, half, width), room(3, half, width),
        room(rows, blk, width), room(2, rows, blk, width),
        room(length, 2 * tp_width), room(2 * rows, blk, valf),
        room(rows, 2, 2, up_rows, hid), room(rows, 2, 2, down_rows, width),
        room(rows, 2, up_rows, hid), room(rows, up_rows, hid), room(rows, up_rows, hid),
        room(rows, 2, down_rows, width), room(rows, down_rows, width), room(rows, down_rows, width),
        room(3, 2, 2, 2, piece, width), room(3, 2, 2, piece, width), room(3, 2, piece, width), room(rows, 3, piece, width),
        room(2, 2, valf // 4, width), room(3, valf // 4, width), room(rows, valf // 4, width),
        room(2, 8, width, dtype=F4), room(2, 8, 8, width, dtype=F4), room(2, rows, 8, width, dtype=F4),
        room(1, up_rows, hid), room(down_rows, width), room(3, piece, width), room(valf // 4, width),
        pltpu.SemaphoreType.DMA((SENDS,)), pltpu.SemaphoreType.DMA((RECVS,)), pltpu.SemaphoreType.DMA((OWNS,)),
    ]
    out, gtok, gfirst, f_up, f_down, f_wa, f_wv, f_small = pl.pallas_call(
        layer_kernel,
        out_shape=outs,
        in_specs=[hbm, hbm, hbm, vmem] + [hbm] * 6 + [vmem] * 9,
        out_specs=(hbm,) * 7 + (vmem,),
        scratch_shapes=scratch,
        compiler_params=pltpu.CompilerParams(
            collective_id=0, has_side_effects=True, vmem_limit_bytes=VMEM_BYTES
        ),
    )(
        tokens, first_values, cotangent, segment_ids, *heads,
        w_up.reshape(2, 2, up_rows, 2 * hid), w_down.reshape(2, 2, 2, down_rows, width), w_value,
        norm1_gain, norm1_bias, norm2_gain, norm2_bias, b_out, b_down, b_value, b_query, b_up,
    )
    vector = of(width, dtype=F4)
    results = pl.pallas_call(
        finish_kernel,
        out_shape=(
            of(rows, blk, width), of(rows, blk, valf), of(rows, blk, width, dtype=F4),
            of(width, 2 * hid, dtype=F4), of(2 * hid, width, dtype=F4),
            of(tp_width, width, dtype=F4), of(tp_width, width, dtype=F4), of(tp_width, width, dtype=F4),
            of(width, valf, dtype=F4),
            vector, vector, vector, vector, vector, vector, of(valf, dtype=F4), of(tp_width, dtype=F4), vector,
        ),
        in_specs=[hbm] * 7 + [vmem],
        out_specs=(hbm,) * 9 + (vmem,) * 9,
        scratch_shapes=[
            room(rows, blk, width), room(rows, blk, valf),
            room(rows, blk, width), room(width, 2 * hid), room(2 * hid, width), room(3 * tp_width, width), room(valf, width),
            room(rows, blk, width, dtype=F4), room(width, 2 * hid, dtype=F4), room(2 * hid, width, dtype=F4),
            room(tp_width, width, dtype=F4), room(tp_width, width, dtype=F4), room(tp_width, width, dtype=F4),
            room(width, valf, dtype=F4),
            pltpu.SemaphoreType.DMA((7,)), pltpu.SemaphoreType.DMA((9,)),
        ],
        compiler_params=pltpu.CompilerParams(vmem_limit_bytes=VMEM_BYTES),
    )(
        out, gfirst, gtok, f_up.reshape(width, 2 * hid), f_down.reshape(2 * hid, width),
        f_wa.reshape(3 * tp_width, width), f_wv.reshape(valf, width), f_small,
    )
    (out, gfirst, gtok, grad_up, grad_down, grad_q, grad_k, grad_o, grad_v,
     gain1, bias1, gain2, bias2, grad_b_out, grad_b_down, grad_b_v, grad_b_q, grad_b_up) = results
    return (
        out, gtok, gfirst, gain1, bias1, grad_q.T, grad_b_q, grad_k.T, grad_v, grad_b_v, grad_o, grad_b_out,
        gain2, bias2, grad_up, grad_b_up, grad_down, grad_b_down,
    )


def finish_kernel(
    out, gfirst, gtok, up, down, heads, value, small,
    out_o, gfirst_o, gtok_o, up_o, down_o, q_o, k_o, o_o, value_o,
    gain1, bias1, gain2, bias2, b_out, b_down, b_value, b_query, b_up,
    out_i, gfirst_i, gtok_i, up_i, down_i, heads_i, value_i, gtok_f, up_f, down_f, q_f, k_f, o_f, value_f, in_sems, out_sems,
):
    t = lax.axis_index("tp")
    loads = [
        pltpu.make_async_copy(src, dst, in_sems.at[i])
        for i, (src, dst) in enumerate((
            (up, up_i), (down, down_i), (gtok, gtok_i), (heads, heads_i), (value, value_i), (out, out_i), (gfirst, gfirst_i),
        ))
    ]
    for copy in loads:
        copy.start()
    stores = [
        pltpu.make_async_copy(src, dst, out_sems.at[i])
        for i, (src, dst) in enumerate((
            (up_f, up_o), (down_f, down_o), (gtok_f, gtok_o), (q_f, q_o), (k_f, k_o), (o_f, o_o), (value_f, value_o),
            (out_i, out_o), (gfirst_i, gfirst_o),
        ))
    ]
    for row, ref in enumerate((gain1, bias1)):
        ref[...] = small[row, :]
    for row, ref in enumerate((gain2, bias2, b_out, b_down)):
        ref[...] = small[12 + row, :]
    b_value[...] = small[6, :b_value.shape[0]]
    b_up[...] = small[8 + t, :]
    shard = b_query.shape[0]
    mine = jnp.zeros((1, shard), F4)
    for i in range(small.shape[1] // shard):
        mine = jnp.where(t == i, small[7:8, i * shard:(i + 1) * shard], mine)
    b_query[...] = mine.reshape(shard)
    for i, (src, dst) in enumerate(((up_i, up_f), (down_i, down_f), (gtok_i, gtok_f))):
        loads[i].wait()
        dst[...] = src[...].astype(F4)
        stores[i].start()
    loads[3].wait()
    for i, ref in enumerate((q_f, k_f)):
        ref[...] = heads_i[i * shard:(i + 1) * shard, :].astype(F4)
        stores[3 + i].start()
    o_f[...] = heads_i[2 * shard:3 * shard, :].astype(F4)
    stores[5].start()
    loads[4].wait()
    value_f[...] = value_i[...].astype(F4).T
    stores[6].start()
    for i in range(2):
        loads[5 + i].wait()
        stores[7 + i].start()
    for copy in stores:
        copy.wait()


SENDS = 176
RECVS = 176
OWNS = 20
VMEM_BYTES = 63 * 1024 * 1024


def fits(mesh):
    return mesh.shape["seq"] == 2 and mesh.shape["batch"] == 4 and mesh.shape["tp"] == 4


def solution(mesh):
    placed = (
        P("batch", ("seq", "tp"), None),
        P("batch", ("seq", "tp"), None),
        P("batch", None),
        P("batch", ("seq", "tp"), None),
        P(),
        P(),
        P(None, "tp"),
        P("tp"),
        P(None, "tp"),
        P(),
        P(),
        P("tp", None),
        P(),
        P(),
        P(),
        P(None, "tp"),
        P("tp"),
        P("tp", None),
        P(),
    )
    return jax.shard_map(
        whole_layer if fits(mesh) else on_device,
        mesh=mesh,
        in_specs=placed,
        out_specs=(
            P("batch", ("seq", "tp"), None),
            P("batch", ("seq", "tp"), None),
            P("batch", ("seq", "tp"), None),
            P(),
            P(),
            P(None, "tp"),
            P("tp"),
            P(None, "tp"),
            P(),
            P(),
            P("tp", None),
            P(),
            P(),
            P(),
            P(None, "tp"),
            P("tp"),
            P("tp", None),
            P(),
        ),
        check_vma=False,
    )
```
